32 devices in a mesh: inline: 16 (over z, y, x), xline: 2 (over core).
Axes of the slice: x: 2, y: 2, z: 4, core: 2. Of those that a mesh axis runs over, the one named last changes fastest.
Arguments:
- source_field: bfloat16 [4, 2, 2048, 128], P(None, 'xline', 'inline'), may hold values from -6 to 6
- receiver_field: bfloat16 [4, 2, 2048, 128], P(None, 'xline', 'inline'), may hold values from -6 to 6
- sat_mask: int32 [2, 2048, 128], P('xline', 'inline'), may hold values 0 or 1
- offset_range: int32 [16], P('inline'), may hold values from 8 to 32, as said below
Outputs:
- source_adjoint: bfloat16 [4, 2, 2048, 128], P(None, 'xline', 'inline')
- receiver_adjoint: bfloat16 [4, 2, 2048, 128], P(None, 'xline', 'inline')
- semblance: float32 [], replicated
The draws below stay inside these ranges and needn't reach their ends.
Inputs may be any that keep to these rules, and one draw needn't show every extreme that they name: `offset_range`: some slab has exactly 32.
All inputs are finite; a program needn't handle non-finite values. No bound on the sum of `sat_mask` on one device may be relied on, other than what follows from the above.
Results may differ from the reference program's by a relative error of at most 0.00075.
Values may be sent and summed in bfloat16 or wider, within the bound.
No kernel may reach another device: no remote copies, remote signals or barrier semaphores. Data moves between devices by JAX's collectives and lax.ppermute only.
A program may use at most 64 MiB of HBM per device.

```python
import jax
import jax.numpy as jnp
from jax import lax

NT = 4
H = 32
MINOFF = 8
CX = 128
NZ = 128
NX = 2048
NY = 2
N_INLINE = 16


def draw_offset_range(key, part):
    values = jax.random.randint(key, (N_INLINE,), MINOFF, H + 1, dtype=jnp.int32)
    chosen = jax.random.randint(jax.random.fold_in(key, 7), (), 0, N_INLINE, dtype=jnp.int32)
    positions = jnp.arange(N_INLINE, dtype=jnp.int32)
    return jnp.where(positions == chosen, H, values).astype(jnp.int32)


def with_ends(drawn, stream_key, smallest, largest):
    longest = drawn.shape.index(max(drawn.shape))
    spots = []
    for shift in (0, 1):
        where = [jax.random.randint(jax.random.fold_in(stream_key, axis), (), 0, length) for axis, length in enumerate(drawn.shape)]
        where[longest] = (where[longest] + shift) % drawn.shape[longest]
        spots.append(tuple(where))
    return drawn.at[spots[0]].set(smallest).at[spots[1]].set(largest)


def block_scale(key, dims, cuts, low, largest):
    def one(position, blocks):
        heights = jax.random.uniform(jax.random.fold_in(jax.random.fold_in(key, 6), position), (blocks,), jnp.float32, low / len(cuts), largest / len(cuts))
        return jnp.repeat(jnp.exp(heights), dims[position] // blocks).reshape((-1,) + (1,) * (len(dims) - position - 1))

    level = one(*cuts[0])
    for cut in cuts[1:]:
        level = level * one(*cut)
    return level


def gaussian(stream_key, shape, deviation, most, split=(), kind=jnp.bfloat16):
    factor_of = block_scale(stream_key, shape, split, -0.22, 0.18) if split else 1.0
    drawn = jax.random.normal(stream_key, shape, jnp.float32) * deviation * factor_of
    return jnp.minimum(jnp.maximum(drawn, -most), most).astype(kind)


def setup_inputs(seed: int = 0) -> dict:
    keys = jax.random.split(jax.random.key(seed), 5)
    source_field = gaussian(keys[0], (NT, NY, NX, NZ), 1.0, 6.0, ((1, 2), (2, 16)))
    receiver_field = gaussian(keys[1], (NT, NY, NX, NZ), 1.0, 6.0, ((1, 2), (2, 16)))
    sat_mask = with_ends((jax.random.randint(keys[2], (NY, NX, NZ), 0, 3) < 1).astype(jnp.int32), jax.random.fold_in(keys[2], 1), 0, 1)
    offset_range = draw_offset_range(jax.random.fold_in(keys[4], 71), 0)
    return {"source_field": source_field, "receiver_field": receiver_field, "sat_mask": sat_mask, "offset_range": offset_range}


EPSILON = 1e-06
SATURATION = 0.25

def reference(source_field, receiver_field, sat_mask, offset_range):
    inline_cells = source_field.shape[2]
    padding = ((0, 0), (0, 0), (H, H), (0, 0))
    src_ext = jnp.pad(source_field.astype(jnp.float32), padding)
    rcv_ext = jnp.pad(receiver_field.astype(jnp.float32), padding)
    reach_limit = jnp.repeat(offset_range, CX)
    saturated = sat_mask != 0

    def image_at(offset):
        src_window = lax.dynamic_slice_in_dim(src_ext, (H - offset).astype(jnp.int32), inline_cells, 2)
        rcv_window = lax.dynamic_slice_in_dim(rcv_ext, (H + offset).astype(jnp.int32), inline_cells, 2)
        inside = (jnp.abs(offset) <= reach_limit).astype(jnp.float32)
        image = lax.optimization_barrier(jnp.sum(src_window * rcv_window, axis=0)) * inside[None, :, None]
        return (image, src_window, rcv_window)

    def weight_square(offset):
        relative = offset.astype(jnp.float32) / H
        squared = relative * relative
        weight = jnp.where(saturated, jnp.minimum(squared, SATURATION), squared)
        return weight * weight
    offsets = jnp.arange(-H, H + 1, dtype=jnp.int32)

    def stats_step(running, offset):
        image = image_at(offset)[0]
        power = image * image
        return ((running[0] + jnp.sum(power), running[1] + jnp.sum(weight_square(offset) * power)), None)
    zero = jnp.zeros((), jnp.float32)
    (energy, weighted), _ = lax.scan(stats_step, (zero, zero), offsets)
    semblance = weighted / energy
    cell_count = float(NX * NY * NZ * (2 * H + 1))
    inverse_rms = 1.0 / jnp.sqrt(energy / cell_count + EPSILON)

    def add_into(buffer, addend, anchor):
        section = lax.dynamic_slice_in_dim(buffer, anchor, inline_cells, 2)
        return lax.dynamic_update_slice_in_dim(buffer, section + addend, anchor, 2)

    def adjoint_step(running, offset):
        src_buf, rcv_buf = running
        image, src_window, rcv_window = image_at(offset)
        adjoint_image = inverse_rms * (weight_square(offset) - semblance) * image
        src_buf = add_into(src_buf, adjoint_image[None] * rcv_window, (H - offset).astype(jnp.int32))
        rcv_buf = add_into(rcv_buf, adjoint_image[None] * src_window, (H + offset).astype(jnp.int32))
        return ((src_buf, rcv_buf), None)
    empty = jnp.zeros(src_ext.shape, jnp.float32)
    (src_buf, rcv_buf), _ = lax.scan(adjoint_step, (empty, empty), offsets)
    source_adjoint = src_buf[:, :, H:H + inline_cells].astype(jnp.bfloat16)
    receiver_adjoint = rcv_buf[:, :, H:H + inline_cells].astype(jnp.bfloat16)
    return (source_adjoint, receiver_adjoint, semblance)
```

```python
import functools

import jax
import jax.numpy as jnp
from jax import lax
from jax.experimental import pallas as pl
from jax.experimental.pallas import tpu as pltpu
from jax.sharding import PartitionSpec as P

H = 32
EPSILON = 1e-06
SATURATION = 0.25
REACH = 2 * H
ALWAYS = 8
ROWS = 8
LIMIT_ROWS = 16
VMEM = pl.BlockSpec(memory_space=pltpu.VMEM)
SMEM = pl.BlockSpec(memory_space=pltpu.SMEM)


def square_weight(offset):
    relative = (offset / H) ** 2
    return relative * relative


def payload_layout(times, lines):
    fields = 2 * times * lines * REACH
    return fields, fields + lines * H, fields + lines * H + LIMIT_ROWS


def pack_kernel(scalars, src, rcv, sat, even_out, odd_out):
    times, lines, cells, depth = src.shape
    mask_at, limit_at, _ = payload_layout(times, lines)
    parity = scalars[0]
    limit = jnp.full((LIMIT_ROWS, depth), scalars[1], jnp.int32).astype(jnp.float32).astype(jnp.bfloat16)

    def fill(out, first):
        start = 0 if first else cells - REACH
        mask_start = 0 if first else cells - H
        for position, field in enumerate((src, rcv)):
            for t in range(times):
                for y in range(lines):
                    at = ((position * times + t) * lines + y) * REACH
                    out[pl.ds(at, REACH), :] = field[t, y, pl.ds(start, REACH), :]
        for y in range(lines):
            out[pl.ds(mask_at + y * H, H), :] = (
                (sat[y, pl.ds(mask_start, H), :] != 0).astype(jnp.float32).astype(jnp.bfloat16)
            )
        out[pl.ds(limit_at, LIMIT_ROWS), :] = limit

    @pl.when(parity == 0)
    def _():
        fill(even_out, False)
        fill(odd_out, True)

    @pl.when(parity != 0)
    def _():
        fill(even_out, True)
        fill(odd_out, False)


def unpack(scalars, src, rcv, sat, even_in, odd_in, fields, masks, limits):
    times, lines, cells, depth = src.shape
    mask_at, limit_at, _ = payload_layout(times, lines)
    parity = scalars[0]

    def halo(arrived, low):
        field_at = 0 if low else REACH + cells
        row_at = 0 if low else H + cells
        for position in range(2):
            for t in range(times):
                for y in range(lines):
                    at = ((position * times + t) * lines + y) * REACH
                    fields[position, t, y, pl.ds(field_at, REACH), :] = arrived[pl.ds(at, REACH), :].astype(jnp.float32)
        limit = arrived[pl.ds(limit_at, LIMIT_ROWS), :].astype(jnp.float32)
        for y in range(lines):
            masks[y, pl.ds(row_at, H), :] = arrived[pl.ds(mask_at + y * H, H), :].astype(jnp.float32)
        for part in range(H // LIMIT_ROWS):
            limits[pl.ds(row_at + part * LIMIT_ROWS, LIMIT_ROWS), :] = limit

    @pl.when(parity == 0)
    def _():
        halo(even_in, False)
        halo(odd_in, True)

    @pl.when(parity != 0)
    def _():
        halo(even_in, True)
        halo(odd_in, False)

    for position, field in enumerate((src, rcv)):
        for t in range(times):
            for y in range(lines):
                fields[position, t, y, pl.ds(REACH, cells), :] = field[t, y].astype(jnp.float32)
    for y in range(lines):
        masks[y, pl.ds(H, cells), :] = (sat[y] != 0).astype(jnp.float32)
    limits[pl.ds(H, cells), :] = jnp.full((cells, depth), scalars[1], jnp.int32).astype(jnp.float32)


def cell(center, fields, other, limits, y, base, offset):
    times = len(center)
    far = [fields[other, t, y, pl.ds(base + REACH + 2 * offset, ROWS), :] for t in range(times)]
    image = center[0] * far[0]
    for t in range(1, times):
        image = image + center[t] * far[t]
    if abs(offset) > ALWAYS:
        limit = limits[pl.ds(base + H + offset, ROWS), :]
        image = jnp.where(limit >= float(abs(offset)), image, 0.0)
    return image, far


def weigh(image, masks, y, base, offset):
    square = square_weight(offset)
    if square <= SATURATION * SATURATION:
        return image * square
    mask = masks[y, pl.ds(base + H + offset, ROWS), :]
    return image * jnp.where(mask != 0.0, SATURATION * SATURATION, square)


def energy_kernel(scalars, src, rcv, sat, even_in, odd_in, out, fields, masks, limits):
    unpack(scalars, src, rcv, sat, even_in, odd_in, fields, masks, limits)
    times, lines, cells, depth = src.shape
    zero = jnp.zeros((ROWS, depth), jnp.float32)

    def tile(index, sums):
        energy, weighted = sums
        base = pl.multiple_of(index * ROWS, ROWS)
        for y in range(lines):
            center = [fields[0, t, y, pl.ds(base + REACH, ROWS), :] for t in range(times)]
            for offset in range(-H, H + 1):
                image, _ = cell(center, fields, 1, limits, y, base, offset)
                power = image * image
                energy = energy + power
                weighted = weighted + weigh(power, masks, y, base, offset)
        return energy, weighted

    energy, weighted = lax.fori_loop(0, cells // ROWS, tile, (zero, zero))
    out[0:1, :] = jnp.full((1, depth), jnp.sum(energy), jnp.float32)
    out[1:2, :] = jnp.full((1, depth), jnp.sum(weighted), jnp.float32)


def adjoint_kernel(scalars, src, rcv, sat, even_in, odd_in, out, fields, masks, limits):
    unpack(scalars, src, rcv, sat, even_in, odd_in, fields, masks, limits)
    times, lines, cells, depth = src.shape
    zero = jnp.zeros((ROWS, depth), jnp.float32)

    for position in range(2):
        for y in range(lines):

            def tile(index, carry):
                base = pl.multiple_of(index * ROWS, ROWS)
                center = [fields[position, t, y, pl.ds(base + REACH, ROWS), :] for t in range(times)]
                heavy, plain = [zero] * times, [zero] * times
                for offset in range(-H, H + 1):
                    image, far = cell(center, fields, 1 - position, limits, y, base, offset)
                    weighed = weigh(image, masks, y, base, offset)
                    for t in range(times):
                        plain[t] = plain[t] + image * far[t]
                        heavy[t] = heavy[t] + weighed * far[t]
                for t in range(times):
                    out[position, 0, t, y, pl.ds(base, ROWS), :] = heavy[t]
                    out[position, 1, t, y, pl.ds(base, ROWS), :] = plain[t]
                return carry

            lax.fori_loop(0, cells // ROWS, tile, 0)


def combine_kernel(cell_count, sums, parts, src_out, rcv_out, semblance_out):
    total = jnp.sum(sums[...], axis=0)
    energy, weighted = total[0:1], total[1:2]
    semblance = weighted / energy
    inverse_rms = 1.0 / jnp.sqrt(energy / cell_count + EPSILON)
    semblance_out[...] = semblance
    _, _, times, lines, _, _ = parts.shape
    for position, out in enumerate((src_out, rcv_out)):
        for t in range(times):
            for y in range(lines):
                value = inverse_rms * (parts[position, 0, t, y] - semblance * parts[position, 1, t, y])
                out[t, y] = value.astype(jnp.bfloat16)


def exchanges(size):
    even = [(i, i + 1) for i in range(0, size - 1, 2)]
    odd = [(i, i + 1) for i in range(1, size - 1, 2)]
    return [pairs + [(j, i) for i, j in pairs] for pairs in (even, odd)]


def local(source_field, receiver_field, sat_mask, offset_range):
    times, lines, cells, depth = source_field.shape
    size = lax.axis_size("inline")
    scalars = jnp.stack([lax.axis_index("inline").astype(jnp.int32) % 2, offset_range[0]])
    rows = payload_layout(times, lines)[2]
    payload = jax.ShapeDtypeStruct((rows, depth), jnp.bfloat16)
    even, odd = pl.pallas_call(
        pack_kernel,
        out_shape=(payload, payload),
        in_specs=[SMEM, VMEM, VMEM, VMEM],
        out_specs=(VMEM, VMEM),
        name="pack",
    )(scalars, source_field, receiver_field, sat_mask)
    even_route, odd_route = exchanges(size)
    even_in = lax.ppermute(even, "inline", even_route)
    odd_in = lax.ppermute(odd, "inline", odd_route)

    operands = (scalars, source_field, receiver_field, sat_mask, even_in, odd_in)
    scratch = [
        pltpu.VMEM((2, times, lines, cells + 2 * REACH, depth), jnp.float32),
        pltpu.VMEM((lines, cells + 2 * H, depth), jnp.float32),
        pltpu.VMEM((cells + 2 * H, depth), jnp.float32),
    ]
    image_cells = lines * cells * depth * (2 * H + 1)
    sums = pl.pallas_call(
        energy_kernel,
        out_shape=jax.ShapeDtypeStruct((2, depth), jnp.float32),
        in_specs=[SMEM] + [VMEM] * 5,
        out_specs=VMEM,
        scratch_shapes=scratch,
        cost_estimate=pl.CostEstimate(flops=14 * image_cells, bytes_accessed=1 << 20, transcendentals=0),
        name="energy",
    )(*operands)
    gathered = lax.all_gather(sums, ("inline", "xline"))
    parts = pl.pallas_call(
        adjoint_kernel,
        out_shape=jax.ShapeDtypeStruct((2, 2, times, lines, cells, depth), jnp.float32),
        in_specs=[SMEM] + [VMEM] * 5,
        out_specs=VMEM,
        scratch_shapes=scratch,
        cost_estimate=pl.CostEstimate(flops=54 * image_cells, bytes_accessed=1 << 22, transcendentals=0),
        name="adjoint",
    )(*operands)
    cell_count = float(lines * lax.axis_size("xline") * cells * size * depth * (2 * H + 1))
    field_out = jax.ShapeDtypeStruct(source_field.shape, jnp.bfloat16)
    src_adj, rcv_adj, semblance = pl.pallas_call(
        functools.partial(combine_kernel, cell_count),
        out_shape=(field_out, field_out, jax.ShapeDtypeStruct((1, depth), jnp.float32)),
        in_specs=[VMEM, VMEM],
        out_specs=(VMEM, VMEM, VMEM),
        name="combine",
    )(gathered, parts)
    return src_adj, rcv_adj, semblance[0, 0]


def solution(mesh):
    return jax.shard_map(
        local,
        mesh=mesh,
        in_specs=(
            P(None, "xline", "inline", None),
            P(None, "xline", "inline", None),
            P("xline", "inline", None),
            P("inline"),
        ),
        out_specs=(P(None, "xline", "inline", None), P(None, "xline", "inline", None), P()),
        check_vma=False,
    )
```

```python
import functools

import jax
import jax.numpy as jnp
from jax import lax
from jax.experimental import pallas as pl
from jax.experimental.pallas import tpu as pltpu
from jax.sharding import PartitionSpec as P

H = 32
EPSILON = 1e-06
SATURATION = 0.25
REACH = 2 * H
ALWAYS = 8
ROWS = 8
LIMIT_ROWS = 16
PARTS = 2
GRANT = 12 << 20
VMEM = pl.BlockSpec(memory_space=pltpu.VMEM)
SMEM = pl.BlockSpec(memory_space=pltpu.SMEM)


def square_weight(offset):
    relative = (offset / H) ** 2
    return relative * relative


def field_rows(times, lines):
    return times * lines * REACH


def critical_rows(times, lines):
    return field_rows(times, lines) + lines * H + LIMIT_ROWS


def parity_of():
    return lax.rem(lax.axis_index("inline"), 2)


def pack_kernel(limit, src, rcv, sat, even_rcv, odd_rcv, even_src, odd_src):
    times, lines, cells, depth = src.shape
    mask_at = field_rows(times, lines)
    limit_at = mask_at + lines * H
    parity = parity_of()
    limits = jnp.full((LIMIT_ROWS, depth), limit[0], jnp.int32).astype(jnp.float32).astype(jnp.bfloat16)

    def fill(rcv_out, src_out, first):
        start = 0 if first else cells - REACH
        mask_start = 0 if first else cells - H
        for field, out in ((rcv, rcv_out), (src, src_out)):
            for t in range(times):
                for y in range(lines):
                    out[pl.ds((t * lines + y) * REACH, REACH), :] = field[t, y, pl.ds(start, REACH), :]
        for y in range(lines):
            rcv_out[pl.ds(mask_at + y * H, H), :] = (
                (sat[y, pl.ds(mask_start, H), :] != 0).astype(jnp.float32).astype(jnp.bfloat16)
            )
        rcv_out[pl.ds(limit_at, LIMIT_ROWS), :] = limits

    @pl.when(parity == 0)
    def _():
        fill(even_rcv, even_src, False)
        fill(odd_rcv, odd_src, True)

    @pl.when(parity != 0)
    def _():
        fill(even_rcv, even_src, True)
        fill(odd_rcv, odd_src, False)


def by_parity(even_in, odd_in, halo):
    parity = parity_of()

    @pl.when(parity == 0)
    def _():
        halo(even_in, False)
        halo(odd_in, True)

    @pl.when(parity != 0)
    def _():
        halo(even_in, True)
        halo(odd_in, False)


def unpack_field(field, even_in, odd_in, out):
    times, lines, cells, depth = field.shape

    def halo(arrived, low):
        for t in range(times):
            for y in range(lines):
                out[t, y, pl.ds(0 if low else REACH + cells, REACH), :] = arrived[
                    pl.ds((t * lines + y) * REACH, REACH), :
                ].astype(jnp.float32)

    by_parity(even_in, odd_in, halo)
    for t in range(times):
        for y in range(lines):
            out[t, y, pl.ds(REACH, cells), :] = field[t, y].astype(jnp.float32)


def unpack_marks(times, limit, sat, even_in, odd_in, masks, limits):
    lines, cells, depth = sat.shape
    mask_at = field_rows(times, lines)
    limit_at = mask_at + lines * H

    def halo(arrived, low):
        row_at = 0 if low else H + cells
        for y in range(lines):
            masks[y, pl.ds(row_at, H), :] = arrived[pl.ds(mask_at + y * H, H), :].astype(jnp.float32)
        value = arrived[pl.ds(limit_at, LIMIT_ROWS), :].astype(jnp.float32)
        for part in range(H // LIMIT_ROWS):
            limits[pl.ds(row_at + part * LIMIT_ROWS, LIMIT_ROWS), :] = value

    by_parity(even_in, odd_in, halo)
    for y in range(lines):
        masks[y, pl.ds(H, cells), :] = (sat[y] != 0).astype(jnp.float32)
    limits[pl.ds(H, cells), :] = jnp.full((cells, depth), limit[0], jnp.int32).astype(jnp.float32)


def cell(center, shifted, limits, y, base, offset):
    times = len(center)
    far = [shifted[t, y, pl.ds(base + REACH + 2 * offset, ROWS), :] for t in range(times)]
    image = center[0] * far[0]
    for t in range(1, times):
        image = image + center[t] * far[t]
    if abs(offset) > ALWAYS:
        limit = limits[pl.ds(base + H + offset, ROWS), :]
        image = jnp.where(limit >= float(abs(offset)), image, 0.0)
    return image, far


def weigh(image, masks, y, base, offset):
    square = square_weight(offset)
    if square <= SATURATION * SATURATION:
        return image * square
    mask = masks[y, pl.ds(base + H + offset, ROWS), :]
    return image * jnp.where(mask != 0.0, SATURATION * SATURATION, square)


def energy_kernel(limit, src, rcv, sat, even_rcv, odd_rcv, out, shifted, masks, limits):
    times, lines, cells, depth = src.shape
    unpack_field(rcv, even_rcv, odd_rcv, shifted)
    unpack_marks(times, limit, sat, even_rcv, odd_rcv, masks, limits)
    zero = jnp.zeros((ROWS, depth), jnp.float32)

    def tile(index, sums):
        energy, weighted = sums
        base = pl.multiple_of(index * 2 * ROWS, 2 * ROWS)
        for y in range(lines):
            pair = [src[t, y, pl.ds(base, 2 * ROWS), :].astype(jnp.float32) for t in range(times)]
            for half in range(2):
                center = [rows[half * ROWS : (half + 1) * ROWS] for rows in pair]
                at = base + half * ROWS
                for offset in range(-H, H + 1):
                    image, _ = cell(center, shifted, limits, y, at, offset)
                    power = image * image
                    energy = energy + power
                    weighted = weighted + weigh(power, masks, y, at, offset)
        return energy, weighted

    energy, weighted = lax.fori_loop(0, cells // (2 * ROWS), tile, (zero, zero))
    out[0:1, :] = jnp.full((1, depth), jnp.sum(energy), jnp.float32)
    out[1:2, :] = jnp.full((1, depth), jnp.sum(weighted), jnp.float32)


def adjoint_kernel(
    first, count, limit, middle, field, even_in, odd_in, sat, even_rcv, odd_rcv, heavy_out, plain_out, shifted, masks, limits
):
    times, lines, cells, depth = field.shape
    unpack_field(field, even_in, odd_in, shifted)
    unpack_marks(times, limit, sat, even_rcv, odd_rcv, masks, limits)
    zero = jnp.zeros((ROWS, depth), jnp.float32)

    def tile(index, carry):
        base = pl.multiple_of(index * 2 * ROWS, 2 * ROWS)
        for y in range(lines):
            pair = [middle[t, y, pl.ds(first + base, 2 * ROWS), :].astype(jnp.float32) for t in range(times)]
            for half in range(2):
                center = [rows[half * ROWS : (half + 1) * ROWS] for rows in pair]
                at = base + half * ROWS
                heavy, plain = [zero] * times, [zero] * times
                for offset in range(-H, H + 1):
                    image, far = cell(center, shifted, limits, y, first + at, offset)
                    weighed = weigh(image, masks, y, first + at, offset)
                    for t in range(times):
                        plain[t] = plain[t] + image * far[t]
                        heavy[t] = heavy[t] + weighed * far[t]
                for t in range(times):
                    heavy_out[t, y, pl.ds(at, ROWS), :] = heavy[t]
                    plain_out[t, y, pl.ds(at, ROWS), :] = plain[t]
        return carry

    lax.fori_loop(0, count // (2 * ROWS), tile, 0)


def combine_kernel(cell_count, parts, sums, *refs):
    pieces, (src_out, rcv_out, semblance_out) = refs[: 4 * parts], refs[4 * parts :]
    energy, weighted = sums[0:1, :], sums[1:2, :]
    semblance = weighted / energy
    inverse_rms = 1.0 / jnp.sqrt(energy / cell_count + EPSILON)
    semblance_out[...] = semblance
    for position, out in enumerate((src_out, rcv_out)):
        for part in range(parts):
            heavy, plain = pieces[2 * (position * parts + part) :][:2]
            times, lines, count, _ = heavy.shape
            for t in range(times):
                for y in range(lines):
                    value = inverse_rms * (heavy[t, y] - semblance * plain[t, y])
                    out[t, y, pl.ds(part * count, count), :] = value.astype(jnp.bfloat16)


def exchanges(size):
    even = [(i, i + 1) for i in range(0, size - 1, 2)]
    odd = [(i, i + 1) for i in range(1, size - 1, 2)]
    return [pairs + [(j, i) for i, j in pairs] for pairs in (even, odd)]


def total_over(value, axis):
    size = lax.axis_size(axis)
    if size & (size - 1):
        return lax.psum(value, axis)
    distance = 1
    while distance < size:
        value = value + lax.ppermute(value, axis, [(i, i ^ distance) for i in range(size)])
        distance *= 2
    return value


def local(source_field, receiver_field, sat_mask, offset_range):
    times, lines, cells, depth = source_field.shape
    size = lax.axis_size("inline")
    grant = pltpu.CompilerParams(vmem_limit_bytes=GRANT)
    critical = jax.ShapeDtypeStruct((critical_rows(times, lines), depth), jnp.bfloat16)
    later = jax.ShapeDtypeStruct((field_rows(times, lines), depth), jnp.bfloat16)
    even_rcv, odd_rcv, even_src, odd_src = pl.pallas_call(
        pack_kernel,
        out_shape=(critical, critical, later, later),
        in_specs=[SMEM, VMEM, VMEM, VMEM],
        out_specs=(VMEM,) * 4,
        compiler_params=grant,
        name="pack",
    )(offset_range, source_field, receiver_field, sat_mask)
    even_route, odd_route = exchanges(size)
    even_rcv = lax.ppermute(even_rcv, "inline", even_route)
    odd_rcv = lax.ppermute(odd_rcv, "inline", odd_route)

    scratch = [
        pltpu.VMEM((times, lines, cells + 2 * REACH, depth), jnp.float32),
        pltpu.VMEM((lines, cells + 2 * H, depth), jnp.float32),
        pltpu.VMEM((cells + 2 * H, depth), jnp.float32),
    ]
    image_cells = lines * cells * depth * (2 * H + 1)
    sums = pl.pallas_call(
        energy_kernel,
        out_shape=jax.ShapeDtypeStruct((2, depth), jnp.float32),
        in_specs=[SMEM] + [VMEM] * 5,
        out_specs=VMEM,
        scratch_shapes=scratch,
        cost_estimate=pl.CostEstimate(flops=14 * image_cells, bytes_accessed=1 << 20, transcendentals=0),
        compiler_params=grant,
        name="energy",
    )(offset_range, source_field, receiver_field, sat_mask, even_rcv, odd_rcv)
    sums, even_src, odd_src = lax.optimization_barrier((sums, even_src, odd_src))
    even_src = lax.ppermute(even_src, "inline", even_route)
    odd_src = lax.ppermute(odd_src, "inline", odd_route)
    for axis in ("xline", "inline"):
        sums = total_over(sums, axis)

    count = cells // PARTS
    piece = jax.ShapeDtypeStruct((times, lines, count, depth), jnp.float32)
    pieces = []
    for middle, field, even_in, odd_in in (
        (source_field, receiver_field, even_rcv, odd_rcv),
        (receiver_field, source_field, even_src, odd_src),
    ):
        for part in range(PARTS):
            pieces += pl.pallas_call(
                functools.partial(adjoint_kernel, part * count, count),
                out_shape=(piece, piece),
                in_specs=[SMEM] + [VMEM] * 7,
                out_specs=(VMEM, VMEM),
                scratch_shapes=scratch,
                cost_estimate=pl.CostEstimate(
                    flops=27 * image_cells // PARTS, bytes_accessed=1 << 20, transcendentals=0
                ),
                compiler_params=grant,
                name="adjoint",
            )(offset_range, middle, field, even_in, odd_in, sat_mask, even_rcv, odd_rcv)
    cell_count = float(lines * lax.axis_size("xline") * cells * size * depth * (2 * H + 1))
    field_out = jax.ShapeDtypeStruct(source_field.shape, jnp.bfloat16)
    src_adj, rcv_adj, semblance = pl.pallas_call(
        functools.partial(combine_kernel, cell_count, PARTS),
        out_shape=(field_out, field_out, jax.ShapeDtypeStruct((1, depth), jnp.float32)),
        in_specs=[VMEM] * (1 + len(pieces)),
        out_specs=(VMEM, VMEM, VMEM),
        compiler_params=grant,
        name="combine",
    )(sums, *pieces)
    return src_adj, rcv_adj, semblance[0, 0]


def solution(mesh):
    return jax.shard_map(
        local,
        mesh=mesh,
        in_specs=(
            P(None, "xline", "inline", None),
            P(None, "xline", "inline", None),
            P("xline", "inline", None),
            P("inline"),
        ),
        out_specs=(P(None, "xline", "inline", None), P(None, "xline", "inline", None), P()),
        check_vma=False,
    )
```

```python
import functools

import jax
import jax.numpy as jnp
from jax import lax
from jax.experimental import pallas as pl
from jax.experimental.pallas import tpu as pltpu
from jax.sharding import PartitionSpec as P

H = 32
EPSILON = 1e-06
SATURATION = 0.25
REACH = 2 * H
ALWAYS = 8
SHARED = H // 2
ROWS = 8
PAIR = 2 * ROWS
LIMIT_ROWS = 16
PIECES = 4
GRANT = 12 << 20
VMEM = pl.BlockSpec(memory_space=pltpu.VMEM)
SMEM = pl.BlockSpec(memory_space=pltpu.SMEM)


def square_weight(offset):
    relative = (offset / H) ** 2
    return relative * relative


def payload_layout(times, lines):
    mask_at = 2 * times * lines * REACH
    limit_at = mask_at + lines * H
    return mask_at, limit_at, limit_at + LIMIT_ROWS


def by_parity(even, odd, work):
    parity = lax.rem(lax.axis_index("inline"), 2)

    @pl.when(parity == 0)
    def _():
        work(even, False)
        work(odd, True)

    @pl.when(parity != 0)
    def _():
        work(even, True)
        work(odd, False)


def payloads(src, rcv, sat, limit):
    cells, depth = src.shape[2:]

    def rows(low):
        start, mask_start = (0, 0) if low else (cells - REACH, cells - H)
        fields = [lax.slice_in_dim(field, start, start + REACH, axis=2).reshape(-1, depth) for field in (src, rcv)]
        mask = lax.slice_in_dim(sat, mask_start, mask_start + H, axis=1).reshape(-1, depth)
        marks = [(mask != 0).astype(jnp.bfloat16), jnp.full((LIMIT_ROWS, depth), limit[0]).astype(jnp.bfloat16)]
        return jnp.concatenate(fields + marks, axis=0)

    low, high = rows(True), rows(False)
    first = lax.axis_index("inline") % 2 == 0
    return jnp.where(first, high, low), jnp.where(first, low, high)


def unpack_marks(times, limit, sat, even_in, odd_in, masks, limits):
    lines, cells, depth = sat.shape
    mask_at, limit_at, _ = payload_layout(times, lines)

    def halo(arrived, low):
        row_at = 0 if low else H + cells
        for y in range(lines):
            masks[y, pl.ds(row_at, H), :] = arrived[pl.ds(mask_at + y * H, H), :].astype(jnp.float32)
        value = arrived[pl.ds(limit_at, LIMIT_ROWS), :].astype(jnp.float32)
        for part in range(H // LIMIT_ROWS):
            limits[pl.ds(row_at + part * LIMIT_ROWS, LIMIT_ROWS), :] = value

    by_parity(even_in, odd_in, halo)
    for y in range(lines):
        masks[y, pl.ds(H, cells), :] = (sat[y] != 0).astype(jnp.float32)
    limits[pl.ds(H, cells), :] = jnp.full((cells, depth), limit[0], jnp.int32).astype(jnp.float32)


def unpack_halo(position, shape, even_in, odd_in, low_out, low_at, high_out, high_at):
    times, lines, _, _ = shape

    def halo(arrived, low):
        out, field_at = (low_out, low_at) if low else (high_out, high_at)
        for t in range(times):
            for y in range(lines):
                at = ((position * times + t) * lines + y) * REACH
                out[t, y, pl.ds(field_at, REACH), :] = arrived[pl.ds(at, REACH), :].astype(jnp.float32)

    by_parity(even_in, odd_in, halo)


def image_of(center, far):
    image = center[0] * far[0]
    for c, f in zip(center[1:], far[1:]):
        image = image + c * f
    return image


def accumulate(center, sums, offsets, far_at, masked, mask_at):
    heavy, plain = sums
    times = range(len(center))
    near = {}
    for offset in offsets:
        far = far_at(offset)
        image = masked(image_of(center, far), offset)
        if abs(offset) <= SHARED:
            terms = [image * f for f in far]
            if abs(offset) in near:
                terms = [a + b for a, b in zip(near.pop(abs(offset)), terms)]
            near[abs(offset)] = terms
            if offset == 0 or -offset not in offsets or offset > 0:
                near.pop(abs(offset))
                plain = [plain[t] + terms[t] for t in times]
                if offset:
                    square = square_weight(offset)
                    heavy = [heavy[t] + terms[t] * square for t in times]
        else:
            square = square_weight(offset)
            weighed = image * jnp.where(mask_at(offset) != 0.0, SATURATION * SATURATION, square)
            plain = [plain[t] + image * far[t] for t in times]
            heavy = [heavy[t] + weighed * far[t] for t in times]
    return heavy, plain


def paired(largest, smallest=0):
    return [sign * size for size in range(smallest, largest + 1) for sign in ((-1, 1) if size else (1,))]


def tiles_of(field, y, base):
    times = field.shape[0]
    both = [field[t, y, pl.ds(base, PAIR), :].astype(jnp.float32) for t in range(times)]
    return [[rows[half * ROWS : (half + 1) * ROWS] for rows in both] for half in range(2)]


def inner_kernel(limit, src, rcv, sat, heavy_out, plain_out, shifted, masks):
    times, lines, cells, depth = src.shape
    zero = jnp.zeros((ROWS, depth), jnp.float32)
    blank = jnp.zeros((REACH, depth), jnp.float32)
    for t in range(times):
        for y in range(lines):
            shifted[t, y, pl.ds(0, REACH), :] = blank
            shifted[t, y, pl.ds(REACH, cells), :] = rcv[t, y].astype(jnp.float32)
            shifted[t, y, pl.ds(REACH + cells, REACH), :] = blank
    for y in range(lines):
        masks[y, pl.ds(0, H), :] = blank[:H]
        masks[y, pl.ds(H, cells), :] = (sat[y] != 0).astype(jnp.float32)
        masks[y, pl.ds(H + cells, H), :] = blank[:H]
    inside = [(size <= limit[0]).astype(jnp.float32) for size in range(H + 1)]

    def tile(index, carry):
        base = pl.multiple_of(index * PAIR, PAIR)
        for y in range(lines):
            for half, center in enumerate(tiles_of(src, y, base)):
                at = base + half * ROWS
                heavy, plain = accumulate(
                    center,
                    ([zero] * times, [zero] * times),
                    paired(H),
                    lambda h: [shifted[t, y, pl.ds(at + REACH + 2 * h, ROWS), :] for t in range(times)],
                    lambda image, h: image * inside[abs(h)] if abs(h) > ALWAYS else image,
                    lambda h: masks[y, pl.ds(at + H + h, ROWS), :],
                )
                for t in range(times):
                    heavy_out[t, y, pl.ds(at, ROWS), :] = heavy[t]
                    plain_out[t, y, pl.ds(at, ROWS), :] = plain[t]
        return carry

    lax.fori_loop(0, cells // PAIR, tile, 0)


def within(limits, at):
    def masked(image, offset):
        if abs(offset) <= ALWAYS:
            return image
        return jnp.where(limits[pl.ds(at + H + offset, ROWS), :] >= float(abs(offset)), image, 0.0)

    return masked


def outer_kernel(limit, src, sat, even_in, odd_in, heavy_in, plain_in, heavy, plain, sums, low, high, masks, limits):
    times, lines, cells, depth = src.shape
    unpack_marks(times, limit, sat, even_in, odd_in, masks, limits)
    unpack_halo(1, src.shape, even_in, odd_in, low, 0, high, ROWS)
    blank = jnp.zeros((ROWS, depth), jnp.float32)
    for t in range(times):
        for y in range(lines):
            low[t, y, pl.ds(REACH, ROWS), :] = blank
            high[t, y, pl.ds(0, ROWS), :] = blank

    for group in range(REACH // PAIR):

        def tile(index, carry, group=group):
            for side, shifted in ((0, low), (1, high)):

                @pl.when(index == side)
                def _():
                    first = group * PAIR if side == 0 else cells - (group + 1) * PAIR
                    base = pl.multiple_of(first + (index - side) * PAIR, PAIR)
                    shift = REACH * 0 if side else REACH
                    origin = ROWS - cells if side else 0
                    for y in range(lines):
                        for half, center in enumerate(tiles_of(src, y, base)):
                            at = base + half * ROWS
                            rank = 2 * group + (1 - half if side else half)
                            sizes = range(ROWS // 2 * rank + 1, H + 1)
                            new_heavy, new_plain = accumulate(
                                center,
                                (
                                    [heavy[t, y, pl.ds(at, ROWS), :] for t in range(times)],
                                    [plain[t, y, pl.ds(at, ROWS), :] for t in range(times)],
                                ),
                                [size if side else -size for size in sizes],
                                lambda h: [
                                    shifted[t, y, pl.ds(at + shift + origin + 2 * h, ROWS), :] for t in range(times)
                                ],
                                within(limits, at),
                                lambda h: masks[y, pl.ds(at + H + h, ROWS), :],
                            )
                            for t in range(times):
                                heavy[t, y, pl.ds(at, ROWS), :] = new_heavy[t]
                                plain[t, y, pl.ds(at, ROWS), :] = new_plain[t]

            return carry

        lax.fori_loop(0, 2, tile, 0)

    zero = jnp.zeros((ROWS, depth), jnp.float32)

    def add(index, totals):
        energy, weighted = totals
        base = pl.multiple_of(index * PAIR, PAIR)
        for y in range(lines):
            for half, center in enumerate(tiles_of(src, y, base)):
                rows = pl.ds(base + half * ROWS, ROWS)
                energy = energy + image_of(center, [plain[t, y, rows, :] for t in range(times)])
                weighted = weighted + image_of(center, [heavy[t, y, rows, :] for t in range(times)])
        return energy, weighted

    energy, weighted = lax.fori_loop(0, cells // PAIR, add, (zero, zero))
    sums[0:1, :] = jnp.full((1, depth), jnp.sum(energy), jnp.float32)
    sums[1:2, :] = jnp.full((1, depth), jnp.sum(weighted), jnp.float32)


def piece_kernel(first, limit, src, rcv, sat, even_in, odd_in, heavy_out, plain_out, shifted, masks, limits):
    times, lines, cells, depth = src.shape
    unpack_marks(times, limit, sat, even_in, odd_in, masks, limits)
    unpack_halo(0, src.shape, even_in, odd_in, shifted, 0, shifted, REACH + cells)
    zero = jnp.zeros((ROWS, depth), jnp.float32)
    for t in range(times):
        for y in range(lines):
            shifted[t, y, pl.ds(REACH, cells), :] = src[t, y].astype(jnp.float32)

    def tile(index, carry):
        base = pl.multiple_of(index * PAIR, PAIR)
        for y in range(lines):
            for half, center in enumerate(tiles_of(rcv, y, first + base)):
                at = first + base + half * ROWS
                heavy, plain = accumulate(
                    center,
                    ([zero] * times, [zero] * times),
                    paired(H),
                    lambda h: [shifted[t, y, pl.ds(at + REACH + 2 * h, ROWS), :] for t in range(times)],
                    within(limits, at),
                    lambda h: masks[y, pl.ds(at + H + h, ROWS), :],
                )
                rows = pl.ds(base + half * ROWS, ROWS)
                for t in range(times):
                    heavy_out[t, y, rows, :] = heavy[t]
                    plain_out[t, y, rows, :] = plain[t]
        return carry

    lax.fori_loop(0, heavy_out.shape[2] // PAIR, tile, 0)


def combine_kernel(cell_count, sums, src_heavy, src_plain, *refs):
    pieces, (src_out, rcv_out, semblance_out) = refs[:-3], refs[-3:]
    energy, weighted = sums[0:1, :], sums[1:2, :]
    semblance = weighted / energy
    inverse_rms = 1.0 / jnp.sqrt(energy / cell_count + EPSILON)
    semblance_out[...] = semblance

    def put(out, start, heavy, plain):
        times, lines, count, _ = heavy.shape
        for t in range(times):
            for y in range(lines):
                value = inverse_rms * (heavy[t, y] - semblance * plain[t, y])
                out[t, y, pl.ds(start, count), :] = value.astype(jnp.bfloat16)

    put(src_out, 0, src_heavy, src_plain)
    start = 0
    for heavy, plain in zip(pieces[::2], pieces[1::2]):
        put(rcv_out, start, heavy, plain)
        start += heavy.shape[2]


def exchanges(size):
    even = [(i, i + 1) for i in range(0, size - 1, 2)]
    odd = [(i, i + 1) for i in range(1, size - 1, 2)]
    return [pairs + [(j, i) for i, j in pairs] for pairs in (even, odd)]


def reduction_steps():
    steps = []
    for axis in ("xline", "inline"):
        size = lax.axis_size(axis)
        assert size & (size - 1) == 0
        for bit in range(size.bit_length() - 1):
            steps.append((axis, [(i, i ^ (1 << bit)) for i in range(size)]))
    return steps


def local(source_field, receiver_field, sat_mask, offset_range):
    times, lines, cells, depth = source_field.shape
    size = lax.axis_size("inline")
    grant = pltpu.CompilerParams(vmem_limit_bytes=GRANT)
    image_cells = lines * cells * depth * (2 * H + 1)
    shape = jax.ShapeDtypeStruct
    sums_shape = shape((2, depth), jnp.float32)
    total = shape((times, lines, cells, depth), jnp.float32)
    field_out = shape(source_field.shape, jnp.bfloat16)
    extended = pltpu.VMEM((times, lines, cells + 2 * REACH, depth), jnp.float32)
    edge = pltpu.VMEM((times, lines, ROWS + REACH, depth), jnp.float32)
    masks = pltpu.VMEM((lines, cells + 2 * H, depth), jnp.float32)
    limits = pltpu.VMEM((cells + 2 * H, depth), jnp.float32)

    def cost(share):
        return pl.CostEstimate(flops=int(24 * image_cells * share), bytes_accessed=1 << 20, transcendentals=0)

    src, rcv, sat = source_field, receiver_field, sat_mask
    even, odd = payloads(src, rcv, sat, offset_range)
    even_route, odd_route = exchanges(size)
    odd = lax.ppermute(odd, "inline", odd_route)
    even = lax.ppermute(even, "inline", even_route)

    heavy, plain = pl.pallas_call(
        inner_kernel,
        out_shape=(total, total),
        in_specs=[SMEM] + [VMEM] * 3,
        out_specs=(VMEM, VMEM),
        scratch_shapes=[extended, masks],
        cost_estimate=cost(1),
        compiler_params=grant,
        name="inner",
    )(offset_range, src, rcv, sat)
    heavy, plain, sums = pl.pallas_call(
        outer_kernel,
        out_shape=(total, total, sums_shape),
        in_specs=[SMEM] + [VMEM] * 6,
        out_specs=(VMEM, VMEM, VMEM),
        scratch_shapes=[edge, edge, masks, limits],
        input_output_aliases={5: 0, 6: 1},
        cost_estimate=cost(0.25),
        compiler_params=grant,
        name="outer",
    )(offset_range, src, sat, even, odd, heavy, plain)

    steps = reduction_steps()
    count = cells // PIECES
    piece = shape((times, lines, count, depth), jnp.float32)
    pieces = []
    for number in range(max(len(steps), PIECES)):
        if number < PIECES:
            sums, src, rcv = lax.optimization_barrier((sums, src, rcv))
            latest = pl.pallas_call(
                functools.partial(piece_kernel, number * count),
                out_shape=(piece, piece),
                in_specs=[SMEM] + [VMEM] * 5,
                out_specs=(VMEM, VMEM),
                scratch_shapes=[extended, masks, limits],
                cost_estimate=cost(1 / PIECES),
                compiler_params=grant,
                name="piece",
            )(offset_range, src, rcv, sat, even, odd)
        if number < len(steps):
            sums = sums + lax.ppermute(sums, *steps[number])
        if number < PIECES:
            sums, latest = lax.optimization_barrier((sums, latest))
            pieces += latest

    cell_count = float(lines * lax.axis_size("xline") * cells * size * depth * (2 * H + 1))
    src_adj, rcv_adj, semblance = pl.pallas_call(
        functools.partial(combine_kernel, cell_count),
        out_shape=(field_out, field_out, shape((1, depth), jnp.float32)),
        in_specs=[VMEM] * (3 + len(pieces)),
        out_specs=(VMEM, VMEM, VMEM),
        compiler_params=grant,
        name="combine",
    )(sums, heavy, plain, *pieces)
    return src_adj, rcv_adj, semblance[0, 0]


def solution(mesh):
    return jax.shard_map(
        local,
        mesh=mesh,
        in_specs=(
            P(None, "xline", "inline", None),
            P(None, "xline", "inline", None),
            P("xline", "inline", None),
            P("inline"),
        ),
        out_specs=(P(None, "xline", "inline", None), P(None, "xline", "inline", None), P()),
        check_vma=False,
    )
```

```python
import functools

import jax
import jax.numpy as jnp
from jax import lax
from jax.experimental import pallas as pl
from jax.experimental.pallas import tpu as pltpu
from jax.sharding import PartitionSpec as P

H = 32
EPSILON = 1e-06
SATURATION = 0.25
REACH = 2 * H
ALWAYS = 8
SHARED = H // 2
ROWS = 8
PAIR = 2 * ROWS
LIMIT_ROWS = 16
PIECES = 4
GROUP = 8
GRANT = 12 << 20
VMEM = pl.BlockSpec(memory_space=pltpu.VMEM)
SMEM = pl.BlockSpec(memory_space=pltpu.SMEM)


def square_weight(offset):
    relative = (offset / H) ** 2
    return relative * relative


def payload_layout(times, lines):
    mask_at = times * lines * REACH
    return mask_at, mask_at + lines * H


def by_parity(even, odd, work):
    parity = lax.rem(lax.axis_index("inline"), 2)

    @pl.when(parity == 0)
    def _():
        work(even, False)
        work(odd, True)

    @pl.when(parity != 0)
    def _():
        work(even, True)
        work(odd, False)


def payloads(src, rcv, sat, limit):
    cells, depth = src.shape[2:]
    first = lax.axis_index("inline") % 2 == 0

    def edges(value, axis, width):
        low = lax.slice_in_dim(value, 0, width, axis=axis).reshape(-1, depth)
        high = lax.slice_in_dim(value, value.shape[axis] - width, value.shape[axis], axis=axis).reshape(-1, depth)
        return jnp.where(first, high, low), jnp.where(first, low, high)

    rcv_edges = edges(rcv, 2, REACH)
    *rcv_edges, sat = lax.optimization_barrier((*rcv_edges, sat))
    limits = jnp.full((LIMIT_ROWS, depth), limit[0]).astype(jnp.bfloat16)
    marks = [(mask != 0).astype(jnp.bfloat16) for mask in edges(sat, 1, H)]
    early = [jnp.concatenate([rows, mask, limits], axis=0) for rows, mask in zip(rcv_edges, marks)]
    return early, edges(src, 2, REACH)


def unpack_marks(times, limit, sat, even_in, odd_in, masks, limits):
    lines, cells, depth = sat.shape
    mask_at, limit_at = payload_layout(times, lines)

    def halo(arrived, low):
        row_at = 0 if low else H + cells
        for y in range(lines):
            masks[y, pl.ds(row_at, H), :] = arrived[pl.ds(mask_at + y * H, H), :].astype(jnp.float32)
        value = arrived[pl.ds(limit_at, LIMIT_ROWS), :].astype(jnp.float32)
        for part in range(H // LIMIT_ROWS):
            limits[pl.ds(row_at + part * LIMIT_ROWS, LIMIT_ROWS), :] = value

    by_parity(even_in, odd_in, halo)
    for y in range(lines):
        masks[y, pl.ds(H, cells), :] = (sat[y] != 0).astype(jnp.float32)
    limits[pl.ds(H, cells), :] = jnp.full((cells, depth), limit[0], jnp.int32).astype(jnp.float32)


def unpack_halo(even_in, odd_in, low_out, high_out):
    times, lines, _, depth = low_out.shape
    blank = jnp.zeros((ROWS, depth), jnp.float32)

    def halo(arrived, low):
        out, field_at, blank_at = (low_out, 0, REACH) if low else (high_out, ROWS, 0)
        for t in range(times):
            for y in range(lines):
                at = (t * lines + y) * REACH
                out[t, y, pl.ds(field_at, REACH), :] = arrived[pl.ds(at, REACH), :].astype(jnp.float32)
                out[t, y, pl.ds(blank_at, ROWS), :] = blank

    by_parity(even_in, odd_in, halo)


def image_of(center, far):
    image = center[0] * far[0]
    for c, f in zip(center[1:], far[1:]):
        image = image + c * f
    return image


def accumulate(center, sums, offsets, far_at, masked, mask_at):
    heavy, plain = sums
    times = range(len(center))
    near = {}
    for offset in offsets:
        far = far_at(offset)
        image = masked(image_of(center, far), offset)
        if abs(offset) <= SHARED:
            terms = [image * f for f in far]
            if abs(offset) in near:
                terms = [a + b for a, b in zip(near.pop(abs(offset)), terms)]
            near[abs(offset)] = terms
            if offset == 0 or -offset not in offsets or offset > 0:
                near.pop(abs(offset))
                plain = [plain[t] + terms[t] for t in times]
                if offset:
                    square = square_weight(offset)
                    heavy = [heavy[t] + terms[t] * square for t in times]
        else:
            square = square_weight(offset)
            weighed = image * jnp.where(mask_at(offset) != 0.0, SATURATION * SATURATION, square)
            plain = [plain[t] + image * far[t] for t in times]
            heavy = [heavy[t] + weighed * far[t] for t in times]
    return heavy, plain


def paired(largest, smallest=0):
    return [sign * size for size in range(smallest, largest + 1) for sign in ((-1, 1) if size else (1,))]


def tiles_of(field, y, base):
    times = field.shape[0]
    both = [field[t, y, pl.ds(base, PAIR), :].astype(jnp.float32) for t in range(times)]
    return [[rows[half * ROWS : (half + 1) * ROWS] for rows in both] for half in range(2)]


def inner_kernel(first, limit, middle, field, sat, heavy_out, plain_out, shifted, masks):
    times, lines, cells, depth = field.shape
    zero = jnp.zeros((ROWS, depth), jnp.float32)
    blank = jnp.zeros((REACH, depth), jnp.float32)
    for t in range(times):
        for y in range(lines):
            shifted[t, y, pl.ds(0, REACH), :] = blank
            shifted[t, y, pl.ds(REACH, cells), :] = field[t, y].astype(jnp.float32)
            shifted[t, y, pl.ds(REACH + cells, REACH), :] = blank
    for y in range(lines):
        masks[y, pl.ds(0, H), :] = blank[:H]
        masks[y, pl.ds(H, cells), :] = (sat[y] != 0).astype(jnp.float32)
        masks[y, pl.ds(H + cells, H), :] = blank[:H]
    inside = [(size <= limit[0]).astype(jnp.float32) for size in range(H + 1)]

    def tile(index, carry):
        base = pl.multiple_of(index * PAIR, PAIR)
        for y in range(lines):
            for half, center in enumerate(tiles_of(middle, y, first + base)):
                at = first + base + half * ROWS

                def add(offsets, sums):
                    return accumulate(
                        center,
                        sums,
                        offsets,
                        lambda h: [shifted[t, y, pl.ds(at + REACH + 2 * h, ROWS), :] for t in range(times)],
                        lambda image, h: image * inside[abs(h)] if abs(h) > ALWAYS else image,
                        lambda h: masks[y, pl.ds(at + H + h, ROWS), :],
                    )

                sums = add(paired(SHARED), ([zero] * times, [zero] * times))
                for low in range(SHARED + 1, H + 1, GROUP):
                    sizes = range(low, min(low + GROUP, H + 1))
                    reaches = (
                        first + base + PAIR - 1 - 2 * low >= 0,
                        first + base + 2 * low < cells,
                    )
                    for sign, reach in zip((-1, 1), reaches):
                        offsets = [sign * size for size in sizes]
                        sums = lax.cond(reach, functools.partial(add, offsets), lambda kept: kept, sums)
                heavy, plain = sums
                rows = pl.ds(base + half * ROWS, ROWS)
                for t in range(times):
                    heavy_out[t, y, rows, :] = heavy[t]
                    plain_out[t, y, rows, :] = plain[t]
        return carry

    lax.fori_loop(0, heavy_out.shape[2] // PAIR, tile, 0)


def within(limits, at):
    def masked(image, offset):
        if abs(offset) <= ALWAYS:
            return image
        return jnp.where(limits[pl.ds(at + H + offset, ROWS), :] >= float(abs(offset)), image, 0.0)

    return masked


def add_outer(middle, heavy, plain, low, high, masks, limits):
    times, lines, cells, depth = middle.shape
    count = heavy[0].shape[2]

    for group in range(REACH // PAIR):

        def tile(index, carry, group=group):
            for side, shifted in ((0, low), (1, high)):

                @pl.when(index == side)
                def _():
                    first = cells - (group + 1) * PAIR if side else group * PAIR
                    number = first // count
                    base = pl.multiple_of(first - number * count + (index - side) * PAIR, PAIR)
                    origin = ROWS - cells if side else REACH
                    for y in range(lines):
                        for half, center in enumerate(tiles_of(middle, y, number * count + base)):
                            rows = pl.ds(base + half * ROWS, ROWS)
                            at = number * count + base + half * ROWS
                            rank = 2 * group + (1 - half if side else half)
                            sizes = range(ROWS // 2 * rank + 1, H + 1)
                            new_heavy, new_plain = accumulate(
                                center,
                                (
                                    [heavy[number][t, y, rows, :] for t in range(times)],
                                    [plain[number][t, y, rows, :] for t in range(times)],
                                ),
                                [size if side else -size for size in sizes],
                                lambda h: [shifted[t, y, pl.ds(at + origin + 2 * h, ROWS), :] for t in range(times)],
                                within(limits, at),
                                lambda h: masks[y, pl.ds(at + H + h, ROWS), :],
                            )
                            for t in range(times):
                                heavy[number][t, y, rows, :] = new_heavy[t]
                                plain[number][t, y, rows, :] = new_plain[t]

            return carry

        lax.fori_loop(0, 2, tile, 0)


def src_outer_kernel(limit, src, sat, even_in, odd_in, heavy_in, plain_in, heavy, plain, sums, low, high, masks, limits):
    times, lines, cells, depth = src.shape
    unpack_marks(times, limit, sat, even_in, odd_in, masks, limits)
    unpack_halo(even_in, odd_in, low, high)
    add_outer(src, [heavy], [plain], low, high, masks, limits)
    zero = jnp.zeros((ROWS, depth), jnp.float32)

    def add(index, totals):
        energy, weighted = totals
        base = pl.multiple_of(index * PAIR, PAIR)
        for y in range(lines):
            for half, center in enumerate(tiles_of(src, y, base)):
                rows = pl.ds(base + half * ROWS, ROWS)
                energy = energy + image_of(center, [plain[t, y, rows, :] for t in range(times)])
                weighted = weighted + image_of(center, [heavy[t, y, rows, :] for t in range(times)])
        return energy, weighted

    energy, weighted = lax.fori_loop(0, cells // PAIR, add, (zero, zero))
    sums[0:1, :] = jnp.full((1, depth), jnp.sum(energy), jnp.float32)
    sums[1:2, :] = jnp.full((1, depth), jnp.sum(weighted), jnp.float32)


def rcv_outer_kernel(limit, rcv, sat, even_marks, odd_marks, even_in, odd_in, *refs):
    parts, (low, high, masks, limits) = refs[len(refs) // 2 - 2 : -4], refs[-4:]
    unpack_marks(rcv.shape[0], limit, sat, even_marks, odd_marks, masks, limits)
    unpack_halo(even_in, odd_in, low, high)
    add_outer(rcv, parts[::2], parts[1::2], low, high, masks, limits)


def combine_kernel(cell_count, sums, src_heavy, src_plain, *refs):
    pieces, (src_out, rcv_out, semblance_out) = refs[:-3], refs[-3:]
    energy, weighted = sums[0:1, :], sums[1:2, :]
    semblance = weighted / energy
    inverse_rms = 1.0 / jnp.sqrt(energy / cell_count + EPSILON)
    semblance_out[...] = semblance

    def put(out, start, heavy, plain):
        times, lines, count, _ = heavy.shape
        for t in range(times):
            for y in range(lines):
                value = inverse_rms * (heavy[t, y] - semblance * plain[t, y])
                out[t, y, pl.ds(start, count), :] = value.astype(jnp.bfloat16)

    put(src_out, 0, src_heavy, src_plain)
    start = 0
    for heavy, plain in zip(pieces[::2], pieces[1::2]):
        put(rcv_out, start, heavy, plain)
        start += heavy.shape[2]


def exchanges(size):
    even = [(i, i + 1) for i in range(0, size - 1, 2)]
    odd = [(i, i + 1) for i in range(1, size - 1, 2)]
    return [pairs + [(j, i) for i, j in pairs] for pairs in (even, odd)]


def reduction_steps(lines, slabs):
    assert lines % 2 == 0 and lines & (lines - 1) == 0 and slabs & (slabs - 1) == 0
    devices = range(lines * slabs)
    give = [(i, i + 1) for i in devices[::2]]
    steps = [give]
    distance = 2
    while distance < len(devices):
        steps.append([(i, i ^ distance) for i in devices[1::2]])
        distance *= 2
    return steps, [(j, i) for i, j in give]


def local(source_field, receiver_field, sat_mask, offset_range):
    times, lines, cells, depth = source_field.shape
    size = lax.axis_size("inline")
    grant = pltpu.CompilerParams(vmem_limit_bytes=GRANT)
    image_cells = lines * cells * depth * (2 * H + 1)
    shape = jax.ShapeDtypeStruct
    total = shape((times, lines, cells, depth), jnp.float32)
    piece = shape((times, lines, cells // PIECES, depth), jnp.float32)
    field_out = shape(source_field.shape, jnp.bfloat16)
    extended = pltpu.VMEM((times, lines, cells + 2 * REACH, depth), jnp.float32)
    edge = pltpu.VMEM((times, lines, ROWS + REACH, depth), jnp.float32)
    masks = pltpu.VMEM((lines, cells + 2 * H, depth), jnp.float32)
    limits = pltpu.VMEM((cells + 2 * H, depth), jnp.float32)

    def call(kernel, name, out_shape, operands, scratch=(), share=0.0, aliases={}):
        return pl.pallas_call(
            kernel,
            out_shape=out_shape,
            in_specs=[SMEM if operand is offset_range else VMEM for operand in operands],
            out_specs=jax.tree.map(lambda _: VMEM, out_shape),
            scratch_shapes=scratch,
            input_output_aliases=aliases,
            cost_estimate=pl.CostEstimate(
                flops=int(24 * image_cells * share), bytes_accessed=1 << 20, transcendentals=0
            ),
            compiler_params=grant,
            name=name,
        )(*operands)

    src, rcv, sat = source_field, receiver_field, sat_mask
    (even, odd), (even_late, odd_late) = payloads(src, rcv, sat, offset_range)
    even_route, odd_route = exchanges(size)
    odd = lax.ppermute(odd, "inline", odd_route)
    even = lax.ppermute(even, "inline", even_route)

    heavy, plain = call(
        functools.partial(inner_kernel, 0),
        "src_inner",
        (total, total),
        (offset_range, src, rcv, sat),
        [extended, masks],
        0.85,
    )
    heavy, plain, sums = call(
        src_outer_kernel,
        "src_outer",
        (total, total, shape((2, depth), jnp.float32)),
        (offset_range, src, sat, even, odd, heavy, plain),
        [edge, edge, masks, limits],
        0.25,
        {5: 0, 6: 1},
    )

    def piece_at(number, src, rcv):
        return call(
            functools.partial(inner_kernel, number * (cells // PIECES)),
            "rcv_inner",
            (piece, piece),
            (offset_range, rcv, src, sat),
            [extended, masks],
            0.85 / PIECES,
        )

    def beside(exchange, sums, operands, work):
        sums, operands = lax.optimization_barrier((sums, operands))
        arrived = lax.ppermute(sums, ("inline", "xline"), exchange)
        return lax.optimization_barrier((sums, arrived, work(*operands)))

    steps, give_back = reduction_steps(lax.axis_size("xline"), size)
    late = [(odd_late, odd_route), (even_late, even_route)]
    works = [(functools.partial(piece_at, number), (src, rcv)) for number in range(PIECES)]
    pieces = []
    for number, exchange in enumerate(steps):
        work, operands = works[number] if number < PIECES else (lambda: (), ())
        sums, arrived, result = beside(exchange, sums, operands, work)
        sums = sums + arrived
        pieces += result
        if number < len(late):
            rows, route = late[number]
            rows, pieces[-1] = lax.optimization_barrier((rows, pieces[-1]))
            late[number] = lax.ppermute(rows, "inline", route)
    odd_late, even_late = late
    for work, operands in works[len(steps) :]:
        pieces += work(*operands)

    def finish(*pieces):
        return call(
            rcv_outer_kernel,
            "rcv_outer",
            [piece] * len(pieces),
            (offset_range, rcv, sat, even, odd, even_late, odd_late, *pieces),
            [edge, edge, masks, limits],
            0.25,
            {7 + i: i for i in range(len(pieces))},
        )

    sums, arrived, pieces = beside(give_back, sums, pieces, finish)
    sums = jnp.where(lax.axis_index("xline") % 2 == 0, arrived, sums)

    cell_count = float(lines * lax.axis_size("xline") * cells * size * depth * (2 * H + 1))
    src_adj, rcv_adj, semblance = call(
        functools.partial(combine_kernel, cell_count),
        "combine",
        (field_out, field_out, shape((1, depth), jnp.float32)),
        (sums, heavy, plain, *pieces),
    )
    return src_adj, rcv_adj, semblance[0, 0]


def solution(mesh):
    return jax.shard_map(
        local,
        mesh=mesh,
        in_specs=(
            P(None, "xline", "inline", None),
            P(None, "xline", "inline", None),
            P("xline", "inline", None),
            P("inline"),
        ),
        out_specs=(P(None, "xline", "inline", None), P(None, "xline", "inline", None), P()),
        check_vma=False,
    )
```

```python
import functools

import jax
import jax.numpy as jnp
from jax import lax
from jax.experimental import pallas as pl
from jax.experimental.pallas import tpu as pltpu
from jax.sharding import PartitionSpec as P

H = 32
EPSILON = 1e-06
SATURATION = 0.25
REACH = 2 * H
ALWAYS = 8
SHARED = H // 2
ROWS = 8
PAIR = 2 * ROWS
LIMIT_ROWS = 16
PIECES = 4
GROUP = 8
GRANT = 12 << 20
VMEM = pl.BlockSpec(memory_space=pltpu.VMEM)
SMEM = pl.BlockSpec(memory_space=pltpu.SMEM)


def square_weight(offset):
    relative = (offset / H) ** 2
    return relative * relative


def payload_layout(times, lines):
    mask_at = times * lines * REACH
    return mask_at, mask_at + lines * H


def by_parity(even, odd, work):
    here, size = lax.axis_index("inline"), lax.axis_size("inline")
    parity = lax.rem(here, 2)
    below, above = (here > 0).astype(jnp.float32), (here < size - 1).astype(jnp.float32)

    @pl.when(parity == 0)
    def _():
        work(even, False, above)
        work(odd, True, below)

    @pl.when(parity != 0)
    def _():
        work(even, True, below)
        work(odd, False, above)


def edges(value, axis, width):
    depth = value.shape[-1]
    length = value.shape[axis]
    low = lax.slice_in_dim(value, 0, width, axis=axis).reshape(-1, depth)
    return low, lax.slice_in_dim(value, length - width, length, axis=axis).reshape(-1, depth)


def for_even(low, high):
    return jnp.where(lax.axis_index("inline") % 2 == 0, high, low)


def for_odd(low, high):
    return for_even(high, low)


def payloads(rcv, sat, limit):
    depth = rcv.shape[-1]
    rows = edges(rcv, 2, REACH)
    rows = for_even(*rows), for_odd(*rows)
    *rows, sat = lax.optimization_barrier((*rows, sat))
    masks = edges((sat != 0).astype(jnp.bfloat16), 1, H)
    limits = jnp.full((LIMIT_ROWS, depth), limit[0]).astype(jnp.bfloat16)
    return [
        jnp.concatenate([part, choose(*masks), limits], axis=0) for part, choose in zip(rows, (for_even, for_odd))
    ]


def unpack_marks(times, limit, sat, even_in, odd_in, masks, limits):
    lines, cells, depth = sat.shape
    mask_at, limit_at = payload_layout(times, lines)

    def halo(arrived, low, there):
        row_at = 0 if low else H + cells
        for y in range(lines):
            masks[y, pl.ds(row_at, H), :] = arrived[pl.ds(mask_at + y * H, H), :].astype(jnp.float32)
        value = arrived[pl.ds(limit_at, LIMIT_ROWS), :].astype(jnp.float32)
        for part in range(H // LIMIT_ROWS):
            limits[pl.ds(row_at + part * LIMIT_ROWS, LIMIT_ROWS), :] = value

    by_parity(even_in, odd_in, halo)
    for y in range(lines):
        masks[y, pl.ds(H, cells), :] = (sat[y] != 0).astype(jnp.float32)
    limits[pl.ds(H, cells), :] = jnp.full((cells, depth), limit[0], jnp.int32).astype(jnp.float32)


def unpack_halo(even_in, odd_in, low_out, high_out):
    times, lines, _, depth = low_out.shape
    blank = jnp.zeros((ROWS, depth), jnp.float32)

    def halo(arrived, low, there):
        out, field_at, blank_at = (low_out, 0, REACH) if low else (high_out, ROWS, 0)
        for t in range(times):
            for y in range(lines):
                at = (t * lines + y) * REACH
                out[t, y, pl.ds(field_at, REACH), :] = arrived[pl.ds(at, REACH), :].astype(jnp.float32) * there
                out[t, y, pl.ds(blank_at, ROWS), :] = blank

    by_parity(even_in, odd_in, halo)


def image_of(center, far):
    image = center[0] * far[0]
    for c, f in zip(center[1:], far[1:]):
        image = image + c * f
    return image


def accumulate(center, sums, offsets, far_at, masked, mask_at):
    heavy, plain = sums
    times = range(len(center))
    near = {}
    for offset in offsets:
        far = far_at(offset)
        image = masked(image_of(center, far), offset)
        if abs(offset) <= SHARED:
            terms = [image * f for f in far]
            if abs(offset) in near:
                terms = [a + b for a, b in zip(near.pop(abs(offset)), terms)]
            near[abs(offset)] = terms
            if offset == 0 or -offset not in offsets or offset > 0:
                near.pop(abs(offset))
                plain = [plain[t] + terms[t] for t in times]
                if offset:
                    square = square_weight(offset)
                    heavy = [heavy[t] + terms[t] * square for t in times]
        else:
            square = square_weight(offset)
            weighed = image * jnp.where(mask_at(offset) != 0.0, SATURATION * SATURATION, square)
            plain = [plain[t] + image * far[t] for t in times]
            heavy = [heavy[t] + weighed * far[t] for t in times]
    return heavy, plain


def paired(largest, smallest=0):
    return [sign * size for size in range(smallest, largest + 1) for sign in ((-1, 1) if size else (1,))]


def tiles_of(field, y, base):
    times = field.shape[0]
    both = [field[t, y, pl.ds(base, PAIR), :].astype(jnp.float32) for t in range(times)]
    return [[rows[half * ROWS : (half + 1) * ROWS] for rows in both] for half in range(2)]


def inner_kernel(first, limit, middle, field, sat, heavy_out, plain_out, shifted, masks):
    times, lines, cells, depth = field.shape
    zero = jnp.zeros((ROWS, depth), jnp.float32)
    blank = jnp.zeros((REACH, depth), jnp.float32)
    for t in range(times):
        for y in range(lines):
            shifted[t, y, pl.ds(0, REACH), :] = blank
            shifted[t, y, pl.ds(REACH, cells), :] = field[t, y].astype(jnp.float32)
            shifted[t, y, pl.ds(REACH + cells, REACH), :] = blank
    for y in range(lines):
        masks[y, pl.ds(0, H), :] = blank[:H]
        masks[y, pl.ds(H, cells), :] = (sat[y] != 0).astype(jnp.float32)
        masks[y, pl.ds(H + cells, H), :] = blank[:H]
    inside = [(size <= limit[0]).astype(jnp.float32) for size in range(H + 1)]

    def tile(index, carry):
        base = pl.multiple_of(index * PAIR, PAIR)
        for y in range(lines):
            for half, center in enumerate(tiles_of(middle, y, first + base)):
                at = first + base + half * ROWS

                def add(offsets, sums):
                    return accumulate(
                        center,
                        sums,
                        offsets,
                        lambda h: [shifted[t, y, pl.ds(at + REACH + 2 * h, ROWS), :] for t in range(times)],
                        lambda image, h: image * inside[abs(h)] if abs(h) > ALWAYS else image,
                        lambda h: masks[y, pl.ds(at + H + h, ROWS), :],
                    )

                sums = add(paired(SHARED), ([zero] * times, [zero] * times))
                for low in range(SHARED + 1, H + 1, GROUP):
                    sizes = range(low, min(low + GROUP, H + 1))
                    reaches = (
                        first + base + PAIR - 1 - 2 * low >= 0,
                        first + base + 2 * low < cells,
                    )
                    for sign, reach in zip((-1, 1), reaches):
                        offsets = [sign * size for size in sizes]
                        sums = lax.cond(reach, functools.partial(add, offsets), lambda kept: kept, sums)
                heavy, plain = sums
                rows = pl.ds(base + half * ROWS, ROWS)
                for t in range(times):
                    heavy_out[t, y, rows, :] = heavy[t]
                    plain_out[t, y, rows, :] = plain[t]
        return carry

    lax.fori_loop(0, heavy_out.shape[2] // PAIR, tile, 0)


def within(limits, at):
    def masked(image, offset):
        if abs(offset) <= ALWAYS:
            return image
        return jnp.where(limits[pl.ds(at + H + offset, ROWS), :] >= float(abs(offset)), image, 0.0)

    return masked


def add_outer(middle, heavy, plain, low, high, masks, limits):
    times, lines, cells, depth = middle.shape
    count = heavy[0].shape[2]

    for group in range(REACH // PAIR):

        def tile(index, carry, group=group):
            for side, shifted in ((0, low), (1, high)):

                @pl.when(index == side)
                def _():
                    first = cells - (group + 1) * PAIR if side else group * PAIR
                    number = first // count
                    base = pl.multiple_of(first - number * count + (index - side) * PAIR, PAIR)
                    origin = ROWS - cells if side else REACH
                    for y in range(lines):
                        for half, center in enumerate(tiles_of(middle, y, number * count + base)):
                            rows = pl.ds(base + half * ROWS, ROWS)
                            at = number * count + base + half * ROWS
                            rank = 2 * group + (1 - half if side else half)
                            sizes = range(ROWS // 2 * rank + 1, H + 1)
                            new_heavy, new_plain = accumulate(
                                center,
                                (
                                    [heavy[number][t, y, rows, :] for t in range(times)],
                                    [plain[number][t, y, rows, :] for t in range(times)],
                                ),
                                [size if side else -size for size in sizes],
                                lambda h: [shifted[t, y, pl.ds(at + origin + 2 * h, ROWS), :] for t in range(times)],
                                within(limits, at),
                                lambda h: masks[y, pl.ds(at + H + h, ROWS), :],
                            )
                            for t in range(times):
                                heavy[number][t, y, rows, :] = new_heavy[t]
                                plain[number][t, y, rows, :] = new_plain[t]

            return carry

        lax.fori_loop(0, 2, tile, 0)


def src_outer_kernel(limit, src, sat, even_in, odd_in, heavy_in, plain_in, heavy, plain, sums, low, high, masks, limits):
    times, lines, cells, depth = src.shape
    unpack_marks(times, limit, sat, even_in, odd_in, masks, limits)
    unpack_halo(even_in, odd_in, low, high)
    add_outer(src, [heavy], [plain], low, high, masks, limits)
    zero = jnp.zeros((ROWS, depth), jnp.float32)

    def add(index, totals):
        energy, weighted = totals
        base = pl.multiple_of(index * PAIR, PAIR)
        for y in range(lines):
            for half, center in enumerate(tiles_of(src, y, base)):
                rows = pl.ds(base + half * ROWS, ROWS)
                energy = energy + image_of(center, [plain[t, y, rows, :] for t in range(times)])
                weighted = weighted + image_of(center, [heavy[t, y, rows, :] for t in range(times)])
        return energy, weighted

    energy, weighted = lax.fori_loop(0, cells // PAIR, add, (zero, zero))
    sums[0:1, :] = jnp.full((1, depth), jnp.sum(energy), jnp.float32)
    sums[1:2, :] = jnp.full((1, depth), jnp.sum(weighted), jnp.float32)


def rcv_outer_kernel(limit, rcv, sat, even_marks, odd_marks, even_in, odd_in, *refs):
    parts, (low, high, masks, limits) = refs[len(refs) // 2 - 2 : -4], refs[-4:]
    unpack_marks(rcv.shape[0], limit, sat, even_marks, odd_marks, masks, limits)
    unpack_halo(even_in, odd_in, low, high)
    add_outer(rcv, parts[::2], parts[1::2], low, high, masks, limits)


def combine_kernel(cell_count, sums, src_heavy, src_plain, *refs):
    pieces, (src_out, rcv_out, semblance_out) = refs[:-3], refs[-3:]
    energy, weighted = sums[0:1, :], sums[1:2, :]
    semblance = weighted / energy
    inverse_rms = 1.0 / jnp.sqrt(energy / cell_count + EPSILON)
    semblance_out[...] = semblance

    def put(out, start, heavy, plain):
        times, lines, count, _ = heavy.shape
        for t in range(times):
            for y in range(lines):
                value = inverse_rms * (heavy[t, y] - semblance * plain[t, y])
                out[t, y, pl.ds(start, count), :] = value.astype(jnp.bfloat16)

    put(src_out, 0, src_heavy, src_plain)
    start = 0
    for heavy, plain in zip(pieces[::2], pieces[1::2]):
        put(rcv_out, start, heavy, plain)
        start += heavy.shape[2]


def exchanges(size):
    even = [(i, i + 1) for i in range(0, size - 1, 2)]
    odd = [(i, i + 1) for i in range(1, size - 1, 2)]
    routes = []
    for pairs in (even, odd):
        partner = dict(pairs + [(j, i) for i, j in pairs])
        routes.append([(i, partner.get(i, i)) for i in range(size)])
    return routes


def reduction_steps(count):
    assert count & (count - 1) == 0
    return [[(i, i ^ (1 << bit)) for i in range(count)] for bit in range(count.bit_length() - 1)]


def local(source_field, receiver_field, sat_mask, offset_range):
    times, lines, cells, depth = source_field.shape
    size = lax.axis_size("inline")
    grant = pltpu.CompilerParams(vmem_limit_bytes=GRANT)
    image_cells = lines * cells * depth * (2 * H + 1)
    shape = jax.ShapeDtypeStruct
    total = shape((times, lines, cells, depth), jnp.float32)
    piece = shape((times, lines, cells // PIECES, depth), jnp.float32)
    field_out = shape(source_field.shape, jnp.bfloat16)
    extended = pltpu.VMEM((times, lines, cells + 2 * REACH, depth), jnp.float32)
    edge = pltpu.VMEM((times, lines, ROWS + REACH, depth), jnp.float32)
    masks = pltpu.VMEM((lines, cells + 2 * H, depth), jnp.float32)
    limits = pltpu.VMEM((cells + 2 * H, depth), jnp.float32)

    def call(kernel, name, out_shape, operands, scratch=(), share=0.0, aliases={}):
        return pl.pallas_call(
            kernel,
            out_shape=out_shape,
            in_specs=[SMEM if operand is offset_range else VMEM for operand in operands],
            out_specs=jax.tree.map(lambda _: VMEM, out_shape),
            scratch_shapes=scratch,
            input_output_aliases=aliases,
            cost_estimate=pl.CostEstimate(
                flops=int(24 * image_cells * share), bytes_accessed=1 << 20, transcendentals=0
            ),
            compiler_params=grant,
            name=name,
        )(*operands)

    src, rcv, sat = source_field, receiver_field, sat_mask
    even, odd = payloads(rcv, sat, offset_range)
    even_route, odd_route = exchanges(size)
    odd = lax.ppermute(odd, "inline", odd_route)
    even = lax.ppermute(even, "inline", even_route)

    heavy, plain = call(
        functools.partial(inner_kernel, 0),
        "src_inner",
        (total, total),
        (offset_range, src, rcv, sat),
        [extended, masks],
        0.85,
    )
    heavy, plain, sums = call(
        src_outer_kernel,
        "src_outer",
        (total, total, shape((2, depth), jnp.float32)),
        (offset_range, src, sat, even, odd, heavy, plain),
        [edge, edge, masks, limits],
        0.25,
        {5: 0, 6: 1},
    )

    def piece_at(number, src, rcv):
        return call(
            functools.partial(inner_kernel, number * (cells // PIECES)),
            "rcv_inner",
            (piece, piece),
            (offset_range, rcv, src, sat),
            [extended, masks],
            0.85 / PIECES,
        )

    def beside(exchange, sums, operands, work):
        sums, operands = lax.optimization_barrier((sums, operands))
        arrived = lax.ppermute(sums, ("inline", "xline"), exchange)
        sums, result = lax.optimization_barrier((sums + arrived, work(*operands)))
        return sums, result

    def finish(odd_late, even_late, *pieces):
        return call(
            rcv_outer_kernel,
            "rcv_outer",
            [piece] * len(pieces),
            (offset_range, rcv, sat, even, odd, even_late, odd_late, *pieces),
            [edge, edge, masks, limits],
            0.25,
            {7 + i: i for i in range(len(pieces))},
        )

    steps = reduction_steps(lax.axis_size("xline") * size)
    assert len(steps) >= 3
    late, pieces = [], []
    for number, exchange in enumerate(steps):
        last = number == len(steps) - 1
        if number < 2:
            sums, ahead = lax.optimization_barrier((sums, src))
            choose, route = ((for_odd, odd_route), (for_even, even_route))[number]
            late.append(lax.ppermute(choose(*edges(ahead, 2, REACH)), "inline", route))
        if last:
            sums, pieces = beside(exchange, sums, (*late, *pieces), finish)
        else:
            share = range(PIECES * number // (len(steps) - 1), PIECES * (number + 1) // (len(steps) - 1))
            sums, result = beside(
                exchange, sums, (src, rcv), lambda *fields: [part for i in share for part in piece_at(i, *fields)]
            )
            pieces += result

    cell_count = float(lines * lax.axis_size("xline") * cells * size * depth * (2 * H + 1))
    src_adj, rcv_adj, semblance = call(
        functools.partial(combine_kernel, cell_count),
        "combine",
        (field_out, field_out, shape((1, depth), jnp.float32)),
        (sums, heavy, plain, *pieces),
    )
    return src_adj, rcv_adj, semblance[0, 0]


def solution(mesh):
    return jax.shard_map(
        local,
        mesh=mesh,
        in_specs=(
            P(None, "xline", "inline", None),
            P(None, "xline", "inline", None),
            P("xline", "inline", None),
            P("inline"),
        ),
        out_specs=(P(None, "xline", "inline", None), P(None, "xline", "inline", None), P()),
        check_vma=False,
    )
```

```python
import functools

import jax
import jax.numpy as jnp
from jax import lax
from jax.experimental import pallas as pl
from jax.experimental.pallas import tpu as pltpu
from jax.sharding import PartitionSpec as P

H = 32
EPSILON = 1e-06
SATURATION = 0.25
REACH = 2 * H
ALWAYS = 8
SHARED = H // 2
ROWS = 8
PAIR = 2 * ROWS
LIMIT_ROWS = 16
PIECES = 4
GROUP = 8
GRANT = 12 << 20
VMEM = pl.BlockSpec(memory_space=pltpu.VMEM)
SMEM = pl.BlockSpec(memory_space=pltpu.SMEM)


def square_weight(offset):
    relative = (offset / H) ** 2
    return relative * relative


def payload_layout(times, lines):
    mask_at = times * lines * REACH
    return mask_at, mask_at + lines * H


def by_parity(even, odd, work):
    here, size = lax.axis_index("inline"), lax.axis_size("inline")
    parity = lax.rem(here, 2)
    below, above = (here > 0).astype(jnp.float32), (here < size - 1).astype(jnp.float32)

    @pl.when(parity == 0)
    def _():
        work(even, False, above)
        work(odd, True, below)

    @pl.when(parity != 0)
    def _():
        work(even, True, below)
        work(odd, False, above)


def edges(value, axis, width):
    depth = value.shape[-1]
    length = value.shape[axis]
    low = lax.slice_in_dim(value, 0, width, axis=axis).reshape(-1, depth)
    return low, lax.slice_in_dim(value, length - width, length, axis=axis).reshape(-1, depth)


def for_even(low, high):
    return jnp.where(lax.axis_index("inline") % 2 == 0, high, low)


def for_odd(low, high):
    return for_even(high, low)


def payloads(rcv, sat, limit):
    depth = rcv.shape[-1]
    rows = edges(rcv, 2, REACH)
    rows = for_even(*rows), for_odd(*rows)
    *rows, sat = lax.optimization_barrier((*rows, sat))
    masks = edges((sat != 0).astype(jnp.bfloat16), 1, H)
    limits = jnp.full((LIMIT_ROWS, depth), limit[0]).astype(jnp.bfloat16)
    return [
        jnp.concatenate([part, choose(*masks), limits], axis=0) for part, choose in zip(rows, (for_even, for_odd))
    ]


def unpack_marks(times, limit, sat, even_in, odd_in, masks, limits):
    lines, cells, depth = sat.shape
    mask_at, limit_at = payload_layout(times, lines)

    def halo(arrived, low, there):
        row_at = 0 if low else H + cells
        for y in range(lines):
            masks[y, pl.ds(row_at, H), :] = arrived[pl.ds(mask_at + y * H, H), :].astype(jnp.float32)
        value = arrived[pl.ds(limit_at, LIMIT_ROWS), :].astype(jnp.float32)
        for part in range(H // LIMIT_ROWS):
            limits[pl.ds(row_at + part * LIMIT_ROWS, LIMIT_ROWS), :] = value

    by_parity(even_in, odd_in, halo)
    for y in range(lines):
        masks[y, pl.ds(H, cells), :] = (sat[y] != 0).astype(jnp.float32)
    limits[pl.ds(H, cells), :] = jnp.full((cells, depth), limit[0], jnp.int32).astype(jnp.float32)


def unpack_halo(even_in, odd_in, low_out, high_out):
    times, lines, _, depth = low_out.shape
    blank = jnp.zeros((ROWS, depth), jnp.float32)

    def halo(arrived, low, there):
        out, field_at, blank_at = (low_out, 0, REACH) if low else (high_out, ROWS, 0)
        for t in range(times):
            for y in range(lines):
                at = (t * lines + y) * REACH
                out[t, y, pl.ds(field_at, REACH), :] = arrived[pl.ds(at, REACH), :].astype(jnp.float32) * there
                out[t, y, pl.ds(blank_at, ROWS), :] = blank

    by_parity(even_in, odd_in, halo)


def image_of(center, far):
    image = center[0] * far[0]
    for c, f in zip(center[1:], far[1:]):
        image = image + c * f
    return image


def accumulate(center, sums, offsets, far_at, masked, mask_at):
    heavy, plain = sums
    times = range(len(center))
    near = {}
    for offset in offsets:
        far = far_at(offset)
        image = masked(image_of(center, far), offset)
        if abs(offset) <= SHARED:
            terms = [image * f for f in far]
            if abs(offset) in near:
                terms = [a + b for a, b in zip(near.pop(abs(offset)), terms)]
            near[abs(offset)] = terms
            if offset == 0 or -offset not in offsets or offset > 0:
                near.pop(abs(offset))
                plain = [plain[t] + terms[t] for t in times]
                if offset:
                    square = square_weight(offset)
                    heavy = [heavy[t] + terms[t] * square for t in times]
        else:
            square = square_weight(offset)
            weighed = image * jnp.where(mask_at(offset) != 0.0, SATURATION * SATURATION, square)
            plain = [plain[t] + image * far[t] for t in times]
            heavy = [heavy[t] + weighed * far[t] for t in times]
    return heavy, plain


def paired(largest, smallest=0):
    return [sign * size for size in range(smallest, largest + 1) for sign in ((-1, 1) if size else (1,))]


def tiles_of(field, y, base):
    times = field.shape[0]
    both = [field[t, y, pl.ds(base, PAIR), :].astype(jnp.float32) for t in range(times)]
    return [[rows[half * ROWS : (half + 1) * ROWS] for rows in both] for half in range(2)]


def inner_kernel(first, limit, middle, field, sat, heavy_out, plain_out, shifted, masks):
    times, lines, cells, depth = field.shape
    zero = jnp.zeros((ROWS, depth), jnp.float32)
    blank = jnp.zeros((REACH, depth), jnp.float32)
    for t in range(times):
        for y in range(lines):
            shifted[t, y, pl.ds(0, REACH), :] = blank
            shifted[t, y, pl.ds(REACH, cells), :] = field[t, y].astype(jnp.float32)
            shifted[t, y, pl.ds(REACH + cells, REACH), :] = blank
    for y in range(lines):
        masks[y, pl.ds(0, H), :] = blank[:H]
        masks[y, pl.ds(H, cells), :] = (sat[y] != 0).astype(jnp.float32)
        masks[y, pl.ds(H + cells, H), :] = blank[:H]
    inside = [(size <= limit[0]).astype(jnp.float32) for size in range(H + 1)]

    def tile(index, carry):
        base = pl.multiple_of(index * PAIR, PAIR)
        for y in range(lines):
            for half, center in enumerate(tiles_of(middle, y, first + base)):
                at = first + base + half * ROWS

                def add(offsets, sums):
                    return accumulate(
                        center,
                        sums,
                        offsets,
                        lambda h: [shifted[t, y, pl.ds(at + REACH + 2 * h, ROWS), :] for t in range(times)],
                        lambda image, h: image * inside[abs(h)] if abs(h) > ALWAYS else image,
                        lambda h: masks[y, pl.ds(at + H + h, ROWS), :],
                    )

                sums = add(paired(SHARED), ([zero] * times, [zero] * times))
                for low in range(SHARED + 1, H + 1, GROUP):
                    sizes = range(low, min(low + GROUP, H + 1))
                    reaches = (
                        first + base + PAIR - 1 - 2 * low >= 0,
                        first + base + 2 * low < cells,
                    )
                    for sign, reach in zip((-1, 1), reaches):
                        offsets = [sign * size for size in sizes]
                        sums = lax.cond(reach, functools.partial(add, offsets), lambda kept: kept, sums)
                heavy, plain = sums
                rows = pl.ds(base + half * ROWS, ROWS)
                for t in range(times):
                    heavy_out[t, y, rows, :] = heavy[t]
                    plain_out[t, y, rows, :] = plain[t]
        return carry

    lax.fori_loop(0, heavy_out.shape[2] // PAIR, tile, 0)


def within(limits, at):
    def masked(image, offset):
        if abs(offset) <= ALWAYS:
            return image
        return jnp.where(limits[pl.ds(at + H + offset, ROWS), :] >= float(abs(offset)), image, 0.0)

    return masked


def add_outer(middle, heavy, plain, low, high, masks, limits):
    times, lines, cells, depth = middle.shape
    count = heavy[0].shape[2]

    for group in range(REACH // PAIR):

        def tile(index, carry, group=group):
            for side, shifted in ((0, low), (1, high)):

                @pl.when(index == side)
                def _():
                    first = cells - (group + 1) * PAIR if side else group * PAIR
                    number = first // count
                    base = pl.multiple_of(first - number * count + (index - side) * PAIR, PAIR)
                    origin = ROWS - cells if side else REACH
                    for y in range(lines):
                        for half, center in enumerate(tiles_of(middle, y, number * count + base)):
                            rows = pl.ds(base + half * ROWS, ROWS)
                            at = number * count + base + half * ROWS
                            rank = 2 * group + (1 - half if side else half)
                            sizes = range(ROWS // 2 * rank + 1, H + 1)
                            new_heavy, new_plain = accumulate(
                                center,
                                (
                                    [heavy[number][t, y, rows, :] for t in range(times)],
                                    [plain[number][t, y, rows, :] for t in range(times)],
                                ),
                                [size if side else -size for size in sizes],
                                lambda h: [shifted[t, y, pl.ds(at + origin + 2 * h, ROWS), :] for t in range(times)],
                                within(limits, at),
                                lambda h: masks[y, pl.ds(at + H + h, ROWS), :],
                            )
                            for t in range(times):
                                heavy[number][t, y, rows, :] = new_heavy[t]
                                plain[number][t, y, rows, :] = new_plain[t]

            return carry

        lax.fori_loop(0, 2, tile, 0)


def src_outer_kernel(limit, src, sat, even_in, odd_in, heavy_in, plain_in, heavy, plain, sums, low, high, masks, limits):
    times, lines, cells, depth = src.shape
    unpack_marks(times, limit, sat, even_in, odd_in, masks, limits)
    unpack_halo(even_in, odd_in, low, high)
    add_outer(src, [heavy], [plain], low, high, masks, limits)
    zero = jnp.zeros((ROWS, depth), jnp.float32)

    def add(index, totals):
        energy, weighted = totals
        base = pl.multiple_of(index * PAIR, PAIR)
        for y in range(lines):
            for half, center in enumerate(tiles_of(src, y, base)):
                rows = pl.ds(base + half * ROWS, ROWS)
                energy = energy + image_of(center, [plain[t, y, rows, :] for t in range(times)])
                weighted = weighted + image_of(center, [heavy[t, y, rows, :] for t in range(times)])
        return energy, weighted

    energy, weighted = lax.fori_loop(0, cells // PAIR, add, (zero, zero))
    sums[0:1, :] = jnp.full((1, depth), jnp.sum(energy), jnp.float32)
    sums[1:2, :] = jnp.full((1, depth), jnp.sum(weighted), jnp.float32)


def rcv_outer_kernel(limit, rcv, sat, even_marks, odd_marks, even_in, odd_in, *refs):
    parts, (low, high, masks, limits) = refs[len(refs) // 2 - 2 : -4], refs[-4:]
    unpack_marks(rcv.shape[0], limit, sat, even_marks, odd_marks, masks, limits)
    unpack_halo(even_in, odd_in, low, high)
    add_outer(rcv, parts[::2], parts[1::2], low, high, masks, limits)


def combine_kernel(cell_count, sums, src_heavy, src_plain, *refs):
    pieces, (src_out, rcv_out, semblance_out) = refs[:-3], refs[-3:]
    energy, weighted = sums[0:1, :], sums[1:2, :]
    semblance = weighted / energy
    inverse_rms = 1.0 / jnp.sqrt(energy / cell_count + EPSILON)
    semblance_out[...] = semblance

    def put(out, start, heavy, plain):
        times, lines, count, _ = heavy.shape
        for t in range(times):
            for y in range(lines):
                value = inverse_rms * (heavy[t, y] - semblance * plain[t, y])
                out[t, y, pl.ds(start, count), :] = value.astype(jnp.bfloat16)

    put(src_out, 0, src_heavy, src_plain)
    start = 0
    for heavy, plain in zip(pieces[::2], pieces[1::2]):
        put(rcv_out, start, heavy, plain)
        start += heavy.shape[2]


def exchanges(size):
    assert size % 2 == 0
    even = [(i, i + 1) for i in range(0, size, 2)]
    odd = [(i, (i + 1) % size) for i in range(1, size, 2)]
    return [pairs + [(j, i) for i, j in pairs] for pairs in (even, odd)]


def reduction_steps(count):
    assert count & (count - 1) == 0
    return [[(i, i ^ (1 << bit | 1)) for i in range(count)] for bit in range(count.bit_length() - 1)]


def local(source_field, receiver_field, sat_mask, offset_range):
    times, lines, cells, depth = source_field.shape
    size = lax.axis_size("inline")
    grant = pltpu.CompilerParams(vmem_limit_bytes=GRANT)
    image_cells = lines * cells * depth * (2 * H + 1)
    shape = jax.ShapeDtypeStruct
    total = shape((times, lines, cells, depth), jnp.float32)
    piece = shape((times, lines, cells // PIECES, depth), jnp.float32)
    field_out = shape(source_field.shape, jnp.bfloat16)
    extended = pltpu.VMEM((times, lines, cells + 2 * REACH, depth), jnp.float32)
    edge = pltpu.VMEM((times, lines, ROWS + REACH, depth), jnp.float32)
    masks = pltpu.VMEM((lines, cells + 2 * H, depth), jnp.float32)
    limits = pltpu.VMEM((cells + 2 * H, depth), jnp.float32)

    def call(kernel, name, out_shape, operands, scratch=(), share=0.0, aliases={}):
        return pl.pallas_call(
            kernel,
            out_shape=out_shape,
            in_specs=[SMEM if operand is offset_range else VMEM for operand in operands],
            out_specs=jax.tree.map(lambda _: VMEM, out_shape),
            scratch_shapes=scratch,
            input_output_aliases=aliases,
            cost_estimate=pl.CostEstimate(
                flops=int(24 * image_cells * share), bytes_accessed=1 << 20, transcendentals=0
            ),
            compiler_params=grant,
            name=name,
        )(*operands)

    src, rcv, sat = source_field, receiver_field, sat_mask
    even, odd = payloads(rcv, sat, offset_range)
    even_route, odd_route = exchanges(size)
    odd = lax.ppermute(odd, "inline", odd_route)
    even = lax.ppermute(even, "inline", even_route)
    low_high = edges(src, 2, REACH)
    odd_late = lax.ppermute(for_odd(*low_high), "inline", odd_route)
    even_late = lax.ppermute(for_even(*low_high), "inline", even_route)

    heavy, plain = call(
        functools.partial(inner_kernel, 0),
        "src_inner",
        (total, total),
        (offset_range, src, rcv, sat),
        [extended, masks],
        0.85,
    )
    heavy, plain, sums = call(
        src_outer_kernel,
        "src_outer",
        (total, total, shape((2, depth), jnp.float32)),
        (offset_range, src, sat, even, odd, heavy, plain),
        [edge, edge, masks, limits],
        0.25,
        {5: 0, 6: 1},
    )

    def piece_at(number, src, rcv):
        return call(
            functools.partial(inner_kernel, number * (cells // PIECES)),
            "rcv_inner",
            (piece, piece),
            (offset_range, rcv, src, sat),
            [extended, masks],
            0.85 / PIECES,
        )

    def beside(exchange, sums, operands, work):
        sums, operands = lax.optimization_barrier((sums, operands))
        arrived = lax.ppermute(sums, ("inline", "xline"), exchange)
        sums, result = lax.optimization_barrier((sums + arrived, work(*operands)))
        return sums, result

    def finish(odd_late, even_late, *pieces):
        return call(
            rcv_outer_kernel,
            "rcv_outer",
            [piece] * len(pieces),
            (offset_range, rcv, sat, even, odd, even_late, odd_late, *pieces),
            [edge, edge, masks, limits],
            0.25,
            {7 + i: i for i in range(len(pieces))},
        )

    steps = reduction_steps(lax.axis_size("xline") * size)
    pieces = []
    for number, exchange in enumerate(steps):
        if number == len(steps) - 1:
            sums, pieces = beside(exchange, sums, (odd_late, even_late, *pieces), finish)
        else:
            share = range(PIECES * number // (len(steps) - 1), PIECES * (number + 1) // (len(steps) - 1))
            sums, result = beside(
                exchange, sums, (src, rcv), lambda *fields: [part for i in share for part in piece_at(i, *fields)]
            )
            pieces += result

    cell_count = float(lines * lax.axis_size("xline") * cells * size * depth * (2 * H + 1))
    src_adj, rcv_adj, semblance = call(
        functools.partial(combine_kernel, cell_count),
        "combine",
        (field_out, field_out, shape((1, depth), jnp.float32)),
        (sums, heavy, plain, *pieces),
    )
    return src_adj, rcv_adj, semblance[0, 0]


def solution(mesh):
    return jax.shard_map(
        local,
        mesh=mesh,
        in_specs=(
            P(None, "xline", "inline", None),
            P(None, "xline", "inline", None),
            P("xline", "inline", None),
            P("inline"),
        ),
        out_specs=(P(None, "xline", "inline", None), P(None, "xline", "inline", None), P()),
        check_vma=False,
    )
```

```python
import functools

import jax
import jax.numpy as jnp
from jax import lax
from jax.experimental import pallas as pl
from jax.experimental.pallas import tpu as pltpu
from jax.sharding import PartitionSpec as P

H = 32
EPSILON = 1e-06
SATURATION = 0.25
REACH = 2 * H
ALWAYS = 8
SHARED = H // 2
ROWS = 8
PAIR = 2 * ROWS
LIMIT_ROWS = 16
PIECES = 4
DEVICES = ("inline", "xline")
GROUP = 8
GRANT = 12 << 20
VMEM = pl.BlockSpec(memory_space=pltpu.VMEM)
SMEM = pl.BlockSpec(memory_space=pltpu.SMEM)


def square_weight(offset):
    relative = (offset / H) ** 2
    return relative * relative


def payload_layout(times, lines):
    mask_at = times * lines * REACH
    return mask_at, mask_at + lines * H


def by_parity(even, odd, work):
    here, size = lax.axis_index("inline"), lax.axis_size("inline")
    parity = lax.rem(here, 2)
    below, above = (here > 0).astype(jnp.float32), (here < size - 1).astype(jnp.float32)

    @pl.when(parity == 0)
    def _():
        work(even, False, above)
        work(odd, True, below)

    @pl.when(parity != 0)
    def _():
        work(even, True, below)
        work(odd, False, above)


def edges(value, axis, width):
    depth = value.shape[-1]
    length = value.shape[axis]
    low = lax.slice_in_dim(value, 0, width, axis=axis).reshape(-1, depth)
    return low, lax.slice_in_dim(value, length - width, length, axis=axis).reshape(-1, depth)


def for_even(low, high):
    return jnp.where(lax.axis_index("inline") % 2 == 0, high, low)


def for_odd(low, high):
    return for_even(high, low)


def payloads(rcv, sat, limit):
    depth = rcv.shape[-1]
    rows = edges(rcv, 2, REACH)
    rows = for_even(*rows), for_odd(*rows)
    *rows, sat = lax.optimization_barrier((*rows, sat))
    masks = edges((sat != 0).astype(jnp.bfloat16), 1, H)
    limits = jnp.full((LIMIT_ROWS, depth), limit[0]).astype(jnp.bfloat16)
    return [
        jnp.concatenate([part, choose(*masks), limits], axis=0) for part, choose in zip(rows, (for_even, for_odd))
    ]


def unpack_marks(times, limit, sat, even_in, odd_in, masks, limits):
    lines, cells, depth = sat.shape
    mask_at, limit_at = payload_layout(times, lines)

    def halo(arrived, low, there):
        row_at = 0 if low else H + cells
        for y in range(lines):
            masks[y, pl.ds(row_at, H), :] = arrived[pl.ds(mask_at + y * H, H), :].astype(jnp.float32)
        value = arrived[pl.ds(limit_at, LIMIT_ROWS), :].astype(jnp.float32)
        for part in range(H // LIMIT_ROWS):
            limits[pl.ds(row_at + part * LIMIT_ROWS, LIMIT_ROWS), :] = value

    by_parity(even_in, odd_in, halo)
    for y in range(lines):
        masks[y, pl.ds(H, cells), :] = (sat[y] != 0).astype(jnp.float32)
    limits[pl.ds(H, cells), :] = jnp.full((cells, depth), limit[0], jnp.int32).astype(jnp.float32)


def unpack_halo(even_in, odd_in, low_out, high_out):
    times, lines, _, depth = low_out.shape
    blank = jnp.zeros((ROWS, depth), jnp.float32)

    def halo(arrived, low, there):
        out, field_at, blank_at = (low_out, 0, REACH) if low else (high_out, ROWS, 0)
        for t in range(times):
            for y in range(lines):
                at = (t * lines + y) * REACH
                out[t, y, pl.ds(field_at, REACH), :] = arrived[pl.ds(at, REACH), :].astype(jnp.float32) * there
                out[t, y, pl.ds(blank_at, ROWS), :] = blank

    by_parity(even_in, odd_in, halo)


def image_of(center, far):
    image = center[0] * far[0]
    for c, f in zip(center[1:], far[1:]):
        image = image + c * f
    return image


def accumulate(center, sums, offsets, far_at, masked, mask_at):
    heavy, plain = sums
    times = range(len(center))
    near = {}
    for offset in offsets:
        far = far_at(offset)
        image = masked(image_of(center, far), offset)
        if abs(offset) <= SHARED:
            terms = [image * f for f in far]
            if abs(offset) in near:
                terms = [a + b for a, b in zip(near.pop(abs(offset)), terms)]
            near[abs(offset)] = terms
            if offset == 0 or -offset not in offsets or offset > 0:
                near.pop(abs(offset))
                plain = [plain[t] + terms[t] for t in times]
                if offset:
                    square = square_weight(offset)
                    heavy = [heavy[t] + terms[t] * square for t in times]
        else:
            square = square_weight(offset)
            weighed = image * jnp.where(mask_at(offset) != 0.0, SATURATION * SATURATION, square)
            plain = [plain[t] + image * far[t] for t in times]
            heavy = [heavy[t] + weighed * far[t] for t in times]
    return heavy, plain


def paired(largest, smallest=0):
    return [sign * size for size in range(smallest, largest + 1) for sign in ((-1, 1) if size else (1,))]


def tiles_of(field, y, base):
    times = field.shape[0]
    both = [field[t, y, pl.ds(base, PAIR), :].astype(jnp.float32) for t in range(times)]
    return [[rows[half * ROWS : (half + 1) * ROWS] for rows in both] for half in range(2)]


def inner_kernel(first, limit, middle, field, sat, heavy_out, plain_out, shifted, masks):
    times, lines, cells, depth = field.shape
    zero = jnp.zeros((ROWS, depth), jnp.float32)
    blank = jnp.zeros((REACH, depth), jnp.float32)
    for t in range(times):
        for y in range(lines):
            shifted[t, y, pl.ds(0, REACH), :] = blank
            shifted[t, y, pl.ds(REACH, cells), :] = field[t, y].astype(jnp.float32)
            shifted[t, y, pl.ds(REACH + cells, REACH), :] = blank
    for y in range(lines):
        masks[y, pl.ds(0, H), :] = blank[:H]
        masks[y, pl.ds(H, cells), :] = (sat[y] != 0).astype(jnp.float32)
        masks[y, pl.ds(H + cells, H), :] = blank[:H]
    inside = [(size <= limit[0]).astype(jnp.float32) for size in range(H + 1)]

    def tile(index, carry):
        base = pl.multiple_of(index * PAIR, PAIR)
        for y in range(lines):
            for half, center in enumerate(tiles_of(middle, y, first + base)):
                at = first + base + half * ROWS

                def add(offsets, sums):
                    return accumulate(
                        center,
                        sums,
                        offsets,
                        lambda h: [shifted[t, y, pl.ds(at + REACH + 2 * h, ROWS), :] for t in range(times)],
                        lambda image, h: image * inside[abs(h)] if abs(h) > ALWAYS else image,
                        lambda h: masks[y, pl.ds(at + H + h, ROWS), :],
                    )

                sums = add(paired(SHARED), ([zero] * times, [zero] * times))
                for low in range(SHARED + 1, H + 1, GROUP):
                    sizes = range(low, min(low + GROUP, H + 1))
                    reaches = (
                        first + base + PAIR - 1 - 2 * low >= 0,
                        first + base + 2 * low < cells,
                    )
                    for sign, reach in zip((-1, 1), reaches):
                        offsets = [sign * size for size in sizes]
                        sums = lax.cond(reach, functools.partial(add, offsets), lambda kept: kept, sums)
                heavy, plain = sums
                rows = pl.ds(base + half * ROWS, ROWS)
                for t in range(times):
                    heavy_out[t, y, rows, :] = heavy[t]
                    plain_out[t, y, rows, :] = plain[t]
        return carry

    lax.fori_loop(0, heavy_out.shape[2] // PAIR, tile, 0)


def within(limits, at):
    def masked(image, offset):
        if abs(offset) <= ALWAYS:
            return image
        return jnp.where(limits[pl.ds(at + H + offset, ROWS), :] >= float(abs(offset)), image, 0.0)

    return masked


def add_outer(middle, heavy, plain, low, high, masks, limits):
    times, lines, cells, depth = middle.shape
    count = heavy[0].shape[2]

    for group in range(REACH // PAIR):

        def tile(index, carry, group=group):
            for side, shifted in ((0, low), (1, high)):

                @pl.when(index == side)
                def _():
                    first = cells - (group + 1) * PAIR if side else group * PAIR
                    number = first // count
                    base = pl.multiple_of(first - number * count + (index - side) * PAIR, PAIR)
                    origin = ROWS - cells if side else REACH
                    for y in range(lines):
                        for half, center in enumerate(tiles_of(middle, y, number * count + base)):
                            rows = pl.ds(base + half * ROWS, ROWS)
                            at = number * count + base + half * ROWS
                            rank = 2 * group + (1 - half if side else half)
                            sizes = range(ROWS // 2 * rank + 1, H + 1)
                            new_heavy, new_plain = accumulate(
                                center,
                                (
                                    [heavy[number][t, y, rows, :] for t in range(times)],
                                    [plain[number][t, y, rows, :] for t in range(times)],
                                ),
                                [size if side else -size for size in sizes],
                                lambda h: [shifted[t, y, pl.ds(at + origin + 2 * h, ROWS), :] for t in range(times)],
                                within(limits, at),
                                lambda h: masks[y, pl.ds(at + H + h, ROWS), :],
                            )
                            for t in range(times):
                                heavy[number][t, y, rows, :] = new_heavy[t]
                                plain[number][t, y, rows, :] = new_plain[t]

            return carry

        lax.fori_loop(0, 2, tile, 0)


def src_outer_kernel(limit, src, sat, even_in, odd_in, heavy_in, plain_in, heavy, plain, sums, low, high, masks, limits):
    times, lines, cells, depth = src.shape
    unpack_marks(times, limit, sat, even_in, odd_in, masks, limits)
    unpack_halo(even_in, odd_in, low, high)
    add_outer(src, [heavy], [plain], low, high, masks, limits)
    zero = jnp.zeros((ROWS, depth), jnp.float32)

    def add(index, totals):
        energy, weighted = totals
        base = pl.multiple_of(index * PAIR, PAIR)
        for y in range(lines):
            for half, center in enumerate(tiles_of(src, y, base)):
                rows = pl.ds(base + half * ROWS, ROWS)
                energy = energy + image_of(center, [plain[t, y, rows, :] for t in range(times)])
                weighted = weighted + image_of(center, [heavy[t, y, rows, :] for t in range(times)])
        return energy, weighted

    energy, weighted = lax.fori_loop(0, cells // PAIR, add, (zero, zero))
    sums[0:1, :] = jnp.full((1, depth), jnp.sum(energy), jnp.float32)
    sums[1:2, :] = jnp.full((1, depth), jnp.sum(weighted), jnp.float32)


def rcv_outer_kernel(limit, rcv, sat, even_marks, odd_marks, even_in, odd_in, *refs):
    parts, (low, high, masks, limits) = refs[len(refs) // 2 - 2 : -4], refs[-4:]
    unpack_marks(rcv.shape[0], limit, sat, even_marks, odd_marks, masks, limits)
    unpack_halo(even_in, odd_in, low, high)
    add_outer(rcv, parts[::2], parts[1::2], low, high, masks, limits)


def combine_kernel(cell_count, sums, src_heavy, src_plain, *refs):
    pieces, (src_out, rcv_out, semblance_out) = refs[:-3], refs[-3:]
    energy, weighted = sums[0:1, :], sums[1:2, :]
    semblance = weighted / energy
    inverse_rms = 1.0 / jnp.sqrt(energy / cell_count + EPSILON)
    semblance_out[...] = semblance

    def put(out, start, heavy, plain):
        times, lines, count, _ = heavy.shape
        for t in range(times):
            for y in range(lines):
                value = inverse_rms * (heavy[t, y] - semblance * plain[t, y])
                out[t, y, pl.ds(start, count), :] = value.astype(jnp.bfloat16)

    put(src_out, 0, src_heavy, src_plain)
    start = 0
    for heavy, plain in zip(pieces[::2], pieces[1::2]):
        put(rcv_out, start, heavy, plain)
        start += heavy.shape[2]


def exchanges(size, lines):
    assert size % 2 == 0 and lines % 2 == 0
    even = [(i, i + 1) for i in range(0, size, 2)]
    odd = [(i, i + 1) for i in range(1, size - 1, 2)]
    routes = []
    for pairs in (even, odd):
        partner = dict(pairs + [(j, i) for i, j in pairs])
        routes.append(
            [
                (i * lines + line, partner[i] * lines + line if i in partner else i * lines + (line ^ 1))
                for i in range(size)
                for line in range(lines)
            ]
        )
    return routes


def reduction_steps(count):
    assert count & (count - 1) == 0
    bits = [1 << bit for bit in range(1, count.bit_length() - 1)]
    groups = [[1]]
    for at in range(0, len(bits), 2):
        low, *high = bits[at : at + 2]
        groups.append([low | high[0], high[0], low] if high else [low])
    return [[[(i, i ^ (mask | 1)) for i in range(count)] for mask in group] for group in groups]


def local(source_field, receiver_field, sat_mask, offset_range):
    times, lines, cells, depth = source_field.shape
    size = lax.axis_size("inline")
    grant = pltpu.CompilerParams(vmem_limit_bytes=GRANT)
    image_cells = lines * cells * depth * (2 * H + 1)
    shape = jax.ShapeDtypeStruct
    total = shape((times, lines, cells, depth), jnp.float32)
    piece = shape((times, lines, cells // PIECES, depth), jnp.float32)
    field_out = shape(source_field.shape, jnp.bfloat16)
    extended = pltpu.VMEM((times, lines, cells + 2 * REACH, depth), jnp.float32)
    edge = pltpu.VMEM((times, lines, ROWS + REACH, depth), jnp.float32)
    masks = pltpu.VMEM((lines, cells + 2 * H, depth), jnp.float32)
    limits = pltpu.VMEM((cells + 2 * H, depth), jnp.float32)

    def call(kernel, name, out_shape, operands, scratch=(), share=0.0, aliases={}):
        return pl.pallas_call(
            kernel,
            out_shape=out_shape,
            in_specs=[SMEM if operand is offset_range else VMEM for operand in operands],
            out_specs=jax.tree.map(lambda _: VMEM, out_shape),
            scratch_shapes=scratch,
            input_output_aliases=aliases,
            cost_estimate=pl.CostEstimate(
                flops=int(24 * image_cells * share), bytes_accessed=1 << 20, transcendentals=0
            ),
            compiler_params=grant,
            name=name,
        )(*operands)

    src, rcv, sat = source_field, receiver_field, sat_mask
    even, odd = payloads(rcv, sat, offset_range)
    even_route, odd_route = exchanges(size, lax.axis_size("xline"))
    odd = lax.ppermute(odd, DEVICES, odd_route)
    even = lax.ppermute(even, DEVICES, even_route)
    heavy, plain = call(
        functools.partial(inner_kernel, 0),
        "src_inner",
        (total, total),
        (offset_range, src, rcv, sat),
        [extended, masks],
        0.85,
    )
    def piece_at(number, src, rcv):
        return call(
            functools.partial(inner_kernel, number * (cells // PIECES)),
            "rcv_inner",
            (piece, piece),
            (offset_range, rcv, src, sat),
            [extended, masks],
            0.85 / PIECES,
        )

    (heavy, plain), ahead = lax.optimization_barrier(((heavy, plain), rcv))
    pieces = list(piece_at(0, src, ahead))
    (heavy, plain), pieces = lax.optimization_barrier(((heavy, plain), pieces))
    pieces = list(pieces)
    heavy, plain, sums = call(
        src_outer_kernel,
        "src_outer",
        (total, total, shape((2, depth), jnp.float32)),
        (offset_range, src, sat, even, odd, heavy, plain),
        [edge, edge, masks, limits],
        0.25,
        {5: 0, 6: 1},
    )

    def late_rows(src):
        low_high = edges(src, 2, REACH)
        return (
            lax.ppermute(for_odd(*low_high), DEVICES, odd_route),
            lax.ppermute(for_even(*low_high), DEVICES, even_route),
        )

    def finish(odd_late, even_late, *pieces):
        return call(
            rcv_outer_kernel,
            "rcv_outer",
            [piece] * len(pieces),
            (offset_range, rcv, sat, even, odd, even_late, odd_late, *pieces),
            [edge, edge, masks, limits],
            0.25,
            {7 + i: i for i in range(len(pieces))},
        )

    steps = reduction_steps(size * lax.axis_size("xline"))
    assert len(steps) >= 3
    for number, routes in enumerate(steps):
        if number == len(steps) - 1:
            sums, late = lax.optimization_barrier((sums, late))
        sums, ahead = lax.optimization_barrier((sums, src))
        arrived = [lax.ppermute(sums, DEVICES, route) for route in routes]
        if number == 0:
            late = late_rows(ahead)
            result = ()
        elif number < len(steps) - 1:
            share = range(1 + (PIECES - 1) * (number - 1) // (len(steps) - 2), 1 + (PIECES - 1) * number // (len(steps) - 2))
            result = [part for i in share for part in piece_at(i, ahead, rcv)]
            pieces += result
        else:
            result = pieces = list(finish(*late, *pieces))
        if len(arrived) == 3:
            both, high, low = arrived
            sums = (sums + low) + (high + both)
        else:
            sums = sums + arrived[0]
        if number:
            sums, result = lax.optimization_barrier((sums, result))
            pieces[len(pieces) - len(result) :] = result

    cell_count = float(lines * lax.axis_size("xline") * cells * size * depth * (2 * H + 1))
    src_adj, rcv_adj, semblance = call(
        functools.partial(combine_kernel, cell_count),
        "combine",
        (field_out, field_out, shape((1, depth), jnp.float32)),
        (sums, heavy, plain, *pieces),
    )
    return src_adj, rcv_adj, semblance[0, 0]


def solution(mesh):
    return jax.shard_map(
        local,
        mesh=mesh,
        in_specs=(
            P(None, "xline", "inline", None),
            P(None, "xline", "inline", None),
            P("xline", "inline", None),
            P("inline"),
        ),
        out_specs=(P(None, "xline", "inline", None), P(None, "xline", "inline", None), P()),
        check_vma=False,
    )
```

```python
import functools

import jax
import jax.numpy as jnp
from jax import lax
from jax.experimental import pallas as pl
from jax.experimental.pallas import tpu as pltpu
from jax.sharding import PartitionSpec as P

H = 32
EPSILON = 1e-06
SATURATION = 0.25
REACH = 2 * H
ALWAYS = 8
SHARED = H // 2
ROWS = 8
PAIR = 2 * ROWS
LIMIT_ROWS = 16
PIECES = 4
DEVICES = ("inline", "xline")
GROUP = 8
GRANT = 12 << 20
VMEM = pl.BlockSpec(memory_space=pltpu.VMEM)
SMEM = pl.BlockSpec(memory_space=pltpu.SMEM)


def square_weight(offset):
    relative = (offset / H) ** 2
    return relative * relative


def payload_layout(times, lines):
    mask_at = times * lines * REACH
    return mask_at, mask_at + lines * H


def by_parity(even, odd, work):
    here, size = lax.axis_index("inline"), lax.axis_size("inline")
    parity = lax.rem(here, 2)
    below, above = (here > 0).astype(jnp.float32), (here < size - 1).astype(jnp.float32)

    @pl.when(parity == 0)
    def _():
        work(even, False, above)
        work(odd, True, below)

    @pl.when(parity != 0)
    def _():
        work(even, True, below)
        work(odd, False, above)


def edges(value, axis, width):
    depth = value.shape[-1]
    length = value.shape[axis]
    low = lax.slice_in_dim(value, 0, width, axis=axis).reshape(-1, depth)
    return low, lax.slice_in_dim(value, length - width, length, axis=axis).reshape(-1, depth)


def for_even(low, high):
    return jnp.where(lax.axis_index("inline") % 2 == 0, high, low)


def for_odd(low, high):
    return for_even(high, low)


def payloads(rcv, sat, limit):
    depth = rcv.shape[-1]
    rows = edges(rcv, 2, REACH)
    rows = for_even(*rows), for_odd(*rows)
    *rows, sat = lax.optimization_barrier((*rows, sat))
    masks = edges((sat != 0).astype(jnp.bfloat16), 1, H)
    limits = jnp.full((LIMIT_ROWS, depth), limit[0]).astype(jnp.bfloat16)
    even = jnp.concatenate([rows[0], for_even(*masks), limits], axis=0)
    even, odd_rows = lax.optimization_barrier((even, rows[1]))
    return even, jnp.concatenate([odd_rows, for_odd(*masks), limits], axis=0)


def unpack_marks(times, limit, sat, even_in, odd_in, masks, limits):
    lines, cells, depth = sat.shape
    mask_at, limit_at = payload_layout(times, lines)

    def halo(arrived, low, there):
        row_at = 0 if low else H + cells
        for y in range(lines):
            masks[y, pl.ds(row_at, H), :] = arrived[pl.ds(mask_at + y * H, H), :].astype(jnp.float32)
        value = arrived[pl.ds(limit_at, LIMIT_ROWS), :].astype(jnp.float32)
        for part in range(H // LIMIT_ROWS):
            limits[pl.ds(row_at + part * LIMIT_ROWS, LIMIT_ROWS), :] = value

    by_parity(even_in, odd_in, halo)
    for y in range(lines):
        masks[y, pl.ds(H, cells), :] = (sat[y] != 0).astype(jnp.float32)
    limits[pl.ds(H, cells), :] = jnp.full((cells, depth), limit[0], jnp.int32).astype(jnp.float32)


def unpack_halo(even_in, odd_in, low_out, high_out):
    times, lines, _, depth = low_out.shape
    blank = jnp.zeros((ROWS, depth), jnp.float32)

    def halo(arrived, low, there):
        out, field_at, blank_at = (low_out, 0, REACH) if low else (high_out, ROWS, 0)
        for t in range(times):
            for y in range(lines):
                at = (t * lines + y) * REACH
                out[t, y, pl.ds(field_at, REACH), :] = arrived[pl.ds(at, REACH), :].astype(jnp.float32) * there
                out[t, y, pl.ds(blank_at, ROWS), :] = blank

    by_parity(even_in, odd_in, halo)


def image_of(center, far):
    image = center[0] * far[0]
    for c, f in zip(center[1:], far[1:]):
        image = image + c * f
    return image


def accumulate(center, sums, offsets, far_at, masked, mask_at):
    heavy, plain = sums
    times = range(len(center))
    near = {}
    for offset in offsets:
        far = far_at(offset)
        image = masked(image_of(center, far), offset)
        if abs(offset) <= SHARED:
            terms = [image * f for f in far]
            if abs(offset) in near:
                terms = [a + b for a, b in zip(near.pop(abs(offset)), terms)]
            near[abs(offset)] = terms
            if offset == 0 or -offset not in offsets or offset > 0:
                near.pop(abs(offset))
                plain = [plain[t] + terms[t] for t in times]
                if offset:
                    square = square_weight(offset)
                    heavy = [heavy[t] + terms[t] * square for t in times]
        else:
            square = square_weight(offset)
            weighed = image * jnp.where(mask_at(offset) != 0.0, SATURATION * SATURATION, square)
            plain = [plain[t] + image * far[t] for t in times]
            heavy = [heavy[t] + weighed * far[t] for t in times]
    return heavy, plain


def paired(largest, smallest=0):
    return [sign * size for size in range(smallest, largest + 1) for sign in ((-1, 1) if size else (1,))]


def tiles_of(field, y, base):
    times = field.shape[0]
    both = [field[t, y, pl.ds(base, PAIR), :].astype(jnp.float32) for t in range(times)]
    return [[rows[half * ROWS : (half + 1) * ROWS] for rows in both] for half in range(2)]


def inner_kernel(first, limit, middle, field, sat, heavy_out, plain_out, shifted, masks):
    times, lines, cells, depth = field.shape
    zero = jnp.zeros((ROWS, depth), jnp.float32)
    blank = jnp.zeros((REACH, depth), jnp.float32)
    for t in range(times):
        for y in range(lines):
            shifted[t, y, pl.ds(0, REACH), :] = blank
            shifted[t, y, pl.ds(REACH, cells), :] = field[t, y].astype(jnp.float32)
            shifted[t, y, pl.ds(REACH + cells, REACH), :] = blank
    for y in range(lines):
        masks[y, pl.ds(0, H), :] = blank[:H]
        masks[y, pl.ds(H, cells), :] = (sat[y] != 0).astype(jnp.float32)
        masks[y, pl.ds(H + cells, H), :] = blank[:H]
    inside = [(size <= limit[0]).astype(jnp.float32) for size in range(H + 1)]

    def tile(index, carry):
        base = pl.multiple_of(index * PAIR, PAIR)
        for y in range(lines):
            for half, center in enumerate(tiles_of(middle, y, first + base)):
                at = first + base + half * ROWS

                def add(offsets, sums):
                    return accumulate(
                        center,
                        sums,
                        offsets,
                        lambda h: [shifted[t, y, pl.ds(at + REACH + 2 * h, ROWS), :] for t in range(times)],
                        lambda image, h: image * inside[abs(h)] if abs(h) > ALWAYS else image,
                        lambda h: masks[y, pl.ds(at + H + h, ROWS), :],
                    )

                sums = add(paired(ALWAYS), ([zero] * times, [zero] * times))
                for low in range(ALWAYS + 1, H + 1, GROUP):
                    high = min(low + GROUP - 1, H)
                    if high <= SHARED:
                        parts = [(paired(high, low), limit[0] >= low)]
                    else:
                        below = first + base + PAIR - 1 - 2 * low >= 0
                        above = first + base + 2 * low < cells
                        parts = [
                            ([sign * size for size in range(low, high + 1)], jnp.logical_and(reach, limit[0] >= low))
                            for sign, reach in ((-1, below), (1, above))
                        ]
                    for offsets, needed in parts:
                        sums = lax.cond(needed, functools.partial(add, offsets), lambda kept: kept, sums)
                heavy, plain = sums
                rows = pl.ds(base + half * ROWS, ROWS)
                for t in range(times):
                    heavy_out[t, y, rows, :] = heavy[t]
                    plain_out[t, y, rows, :] = plain[t]
        return carry

    lax.fori_loop(0, heavy_out.shape[2] // PAIR, tile, 0)


def within(limits, at):
    def masked(image, offset):
        if abs(offset) <= ALWAYS:
            return image
        return jnp.where(limits[pl.ds(at + H + offset, ROWS), :] >= float(abs(offset)), image, 0.0)

    return masked


def add_outer(middle, heavy, plain, low, high, masks, limits):
    times, lines, cells, depth = middle.shape
    count = heavy[0].shape[2]
    widest = [
        jnp.max(jnp.maximum(limits[pl.ds(H if side else 0, ROWS), :], limits[pl.ds(H + cells * side, ROWS), :]))
        for side in range(2)
    ]

    for group in range(REACH // PAIR):

        def tile(index, carry, group=group):
            for side, shifted in ((0, low), (1, high)):

                @pl.when(index == side)
                def _():
                    first = cells - (group + 1) * PAIR if side else group * PAIR
                    number = first // count
                    base = pl.multiple_of(first - number * count + (index - side) * PAIR, PAIR)
                    origin = ROWS - cells if side else REACH
                    for y in range(lines):
                        for half, center in enumerate(tiles_of(middle, y, number * count + base)):
                            rows = pl.ds(base + half * ROWS, ROWS)
                            at = number * count + base + half * ROWS
                            rank = 2 * group + (1 - half if side else half)
                            nearest = ROWS // 2 * rank + 1

                            def add(offsets, sums):
                                return accumulate(
                                    center,
                                    sums,
                                    offsets,
                                    lambda h: [shifted[t, y, pl.ds(at + origin + 2 * h, ROWS), :] for t in range(times)],
                                    within(limits, at),
                                    lambda h: masks[y, pl.ds(at + H + h, ROWS), :],
                                )

                            sums = (
                                [heavy[number][t, y, rows, :] for t in range(times)],
                                [plain[number][t, y, rows, :] for t in range(times)],
                            )
                            for low in range(1, H + 1, GROUP):
                                sizes = range(max(low, nearest), min(low + GROUP, H + 1))
                                if sizes:
                                    sums = lax.cond(
                                        widest[side] >= float(sizes[0]),
                                        functools.partial(add, [size if side else -size for size in sizes]),
                                        lambda kept: kept,
                                        sums,
                                    )
                            new_heavy, new_plain = sums
                            for t in range(times):
                                heavy[number][t, y, rows, :] = new_heavy[t]
                                plain[number][t, y, rows, :] = new_plain[t]

            return carry

        lax.fori_loop(0, 2, tile, 0)


def src_outer_kernel(limit, src, sat, even_in, odd_in, heavy_in, plain_in, heavy, plain, sums, low, high, masks, limits):
    times, lines, cells, depth = src.shape
    unpack_marks(times, limit, sat, even_in, odd_in, masks, limits)
    unpack_halo(even_in, odd_in, low, high)
    add_outer(src, [heavy], [plain], low, high, masks, limits)
    zero = jnp.zeros((ROWS, depth), jnp.float32)

    def add(index, totals):
        energy, weighted = totals
        base = pl.multiple_of(index * PAIR, PAIR)
        for y in range(lines):
            for half, center in enumerate(tiles_of(src, y, base)):
                rows = pl.ds(base + half * ROWS, ROWS)
                energy = energy + image_of(center, [plain[t, y, rows, :] for t in range(times)])
                weighted = weighted + image_of(center, [heavy[t, y, rows, :] for t in range(times)])
        return energy, weighted

    energy, weighted = lax.fori_loop(0, cells // PAIR, add, (zero, zero))
    sums[0:1, :] = jnp.full((1, depth), jnp.sum(energy), jnp.float32)
    sums[1:2, :] = jnp.full((1, depth), jnp.sum(weighted), jnp.float32)


def rcv_outer_kernel(limit, rcv, sat, even_marks, odd_marks, even_in, odd_in, *refs):
    parts, (low, high, masks, limits) = refs[len(refs) // 2 - 2 : -4], refs[-4:]
    unpack_marks(rcv.shape[0], limit, sat, even_marks, odd_marks, masks, limits)
    unpack_halo(even_in, odd_in, low, high)
    add_outer(rcv, parts[::2], parts[1::2], low, high, masks, limits)


def combine_kernel(cell_count, sums, src_heavy, src_plain, *refs):
    pieces, (src_out, rcv_out, semblance_out) = refs[:-3], refs[-3:]
    energy, weighted = sums[0:1, :], sums[1:2, :]
    semblance = weighted / energy
    inverse_rms = 1.0 / jnp.sqrt(energy / cell_count + EPSILON)
    semblance_out[...] = semblance

    def put(out, start, heavy, plain):
        times, lines, count, _ = heavy.shape
        for t in range(times):
            for y in range(lines):
                value = inverse_rms * (heavy[t, y] - semblance * plain[t, y])
                out[t, y, pl.ds(start, count), :] = value.astype(jnp.bfloat16)

    put(src_out, 0, src_heavy, src_plain)
    start = 0
    for heavy, plain in zip(pieces[::2], pieces[1::2]):
        put(rcv_out, start, heavy, plain)
        start += heavy.shape[2]


def ride_kernel(rows_in, sums, rows):
    count = sums.shape[0]
    parts, rest = [], sums[...]
    for _ in range(3):
        parts.append(rest.astype(jnp.bfloat16).astype(jnp.float32))
        rest = rest - parts[-1]
    parts.append(jnp.zeros((LIMIT_ROWS - 3 * count, sums.shape[1]), jnp.float32))
    below = pl.ds(rows.shape[0] - LIMIT_ROWS, LIMIT_ROWS)
    rows[below, :] = jnp.concatenate(parts, axis=0).astype(jnp.bfloat16)


def sums_below(rows, count):
    at = rows.shape[0] - LIMIT_ROWS
    first, second, third = (
        lax.slice_in_dim(rows, at + i * count, at + (i + 1) * count).astype(jnp.float32) for i in range(3)
    )
    return first + second + third


def exchanges(size, lines):
    assert size % 2 == 0 and lines % 2 == 0
    even = [(i, i + 1) for i in range(0, size, 2)]
    odd = [(i, i + 1) for i in range(1, size - 1, 2)]
    routes = []
    for pairs in (even, odd):
        partner = dict(pairs + [(j, i) for i, j in pairs])
        routes.append(
            [
                (i * lines + line, partner[i] * lines + line if i in partner else i * lines + (line ^ 1))
                for i in range(size)
                for line in range(lines)
            ]
        )
    return routes


def reduction_steps(count):
    assert count & (count - 1) == 0
    bits = [1 << bit for bit in range(1, count.bit_length() - 1)]
    groups = [[1]]
    for at in range(0, len(bits), 2):
        low, *high = bits[at : at + 2]
        groups.append([low, high[0], low | high[0]] if high else [low])
    return groups


def local(source_field, receiver_field, sat_mask, offset_range):
    times, lines, cells, depth = source_field.shape
    size = lax.axis_size("inline")
    grant = pltpu.CompilerParams(vmem_limit_bytes=GRANT)
    image_cells = lines * cells * depth * (2 * H + 1)
    shape = jax.ShapeDtypeStruct
    total = shape((times, lines, cells, depth), jnp.float32)
    piece = shape((times, lines, cells // PIECES, depth), jnp.float32)
    field_out = shape(source_field.shape, jnp.bfloat16)
    extended = pltpu.VMEM((times, lines, cells + 2 * REACH, depth), jnp.float32)
    edge = pltpu.VMEM((times, lines, ROWS + REACH, depth), jnp.float32)
    masks = pltpu.VMEM((lines, cells + 2 * H, depth), jnp.float32)
    limits = pltpu.VMEM((cells + 2 * H, depth), jnp.float32)

    def call(kernel, name, out_shape, operands, scratch=(), share=0.0, aliases={}):
        return pl.pallas_call(
            kernel,
            out_shape=out_shape,
            in_specs=[SMEM if operand is offset_range else VMEM for operand in operands],
            out_specs=jax.tree.map(lambda _: VMEM, out_shape),
            scratch_shapes=scratch,
            input_output_aliases=aliases,
            cost_estimate=pl.CostEstimate(
                flops=int(24 * image_cells * share), bytes_accessed=1 << 20, transcendentals=0
            ),
            compiler_params=grant,
            name=name,
        )(*operands)

    src, rcv, sat = source_field, receiver_field, sat_mask
    even, odd = payloads(rcv, sat, offset_range)
    even_route, odd_route = exchanges(size, lax.axis_size("xline"))
    even = lax.ppermute(even, DEVICES, even_route)
    odd = lax.ppermute(odd, DEVICES, odd_route)
    heavy, plain = call(
        functools.partial(inner_kernel, 0),
        "src_inner",
        (total, total),
        (offset_range, src, rcv, sat),
        [extended, masks],
        0.85,
    )
    def piece_at(number, src, rcv):
        return call(
            functools.partial(inner_kernel, number * (cells // PIECES)),
            "rcv_inner",
            (piece, piece),
            (offset_range, rcv, src, sat),
            [extended, masks],
            0.85 / PIECES,
        )

    (heavy, plain), ahead = lax.optimization_barrier(((heavy, plain), rcv))
    pieces = list(piece_at(0, src, ahead))
    (heavy, plain), pieces = lax.optimization_barrier(((heavy, plain), pieces))
    pieces = list(pieces)
    heavy, plain, sums = call(
        src_outer_kernel,
        "src_outer",
        (total, total, shape((2, depth), jnp.float32)),
        (offset_range, src, sat, even, odd, heavy, plain),
        [edge, edge, masks, limits],
        0.25,
        {5: 0, 6: 1},
    )

    def finish(odd_late, even_late, *pieces):
        return call(
            rcv_outer_kernel,
            "rcv_outer",
            [piece] * len(pieces),
            (offset_range, rcv, sat, even, odd, even_late, odd_late, *pieces),
            [edge, edge, masks, limits],
            0.25,
            {7 + i: i for i in range(len(pieces))},
        )

    lines_all = lax.axis_size("xline")
    steps = reduction_steps(size * lines_all)
    assert len(steps) >= 3 and not any(lines_all in group for group in (steps[0], steps[-1]))
    low_high = edges(src, 2, REACH)
    ride = jnp.concatenate([for_even(*low_high), jnp.zeros((LIMIT_ROWS, depth), jnp.bfloat16)], axis=0)
    for number, group in enumerate(steps):
        last = number == len(steps) - 1
        if last:
            sums, *late = lax.optimization_barrier((sums, odd_late, even_late))
        sums, ahead = lax.optimization_barrier((sums, src))
        arrived = []
        for changed in group:
            if changed == lines_all:
                ride = call(
                    ride_kernel,
                    "ride",
                    shape(ride.shape, ride.dtype),
                    (ride, sums),
                    aliases={0: 0},
                )
                even_late = lax.ppermute(ride, DEVICES, even_route)
                arrived.append(sums_below(even_late, sums.shape[0]))
            else:
                route = [(i, i ^ (changed | 1)) for i in range(size * lines_all)]
                arrived.append(lax.ppermute(sums, DEVICES, route))
        if number == 0:
            odd_late = lax.ppermute(for_odd(*edges(ahead, 2, REACH)), DEVICES, odd_route)
        if not last:
            share = range(1 + (PIECES - 1) * number // (len(steps) - 1), 1 + (PIECES - 1) * (number + 1) // (len(steps) - 1))
            result = [part for i in share for part in piece_at(i, ahead, rcv)]
            pieces += result
        else:
            result = pieces = list(finish(*late, *pieces))
        if len(arrived) == 3:
            low, high, both = arrived
            sums = (sums + low) + (high + both)
        else:
            sums = sums + arrived[0]
        sums, result = lax.optimization_barrier((sums, result))
        pieces[len(pieces) - len(result) :] = result

    cell_count = float(lines * lax.axis_size("xline") * cells * size * depth * (2 * H + 1))
    src_adj, rcv_adj, semblance = call(
        functools.partial(combine_kernel, cell_count),
        "combine",
        (field_out, field_out, shape((1, depth), jnp.float32)),
        (sums, heavy, plain, *pieces),
    )
    return src_adj, rcv_adj, semblance[0, 0]


def solution(mesh):
    return jax.shard_map(
        local,
        mesh=mesh,
        in_specs=(
            P(None, "xline", "inline", None),
            P(None, "xline", "inline", None),
            P("xline", "inline", None),
            P("inline"),
        ),
        out_specs=(P(None, "xline", "inline", None), P(None, "xline", "inline", None), P()),
        check_vma=False,
    )
```

```python
import functools

import jax
import jax.numpy as jnp
from jax import lax
from jax.experimental import pallas as pl
from jax.experimental.pallas import tpu as pltpu
from jax.sharding import PartitionSpec as P

H = 32
EPSILON = 1e-06
SATURATION = 0.25
REACH = 2 * H
ALWAYS = 8
SHARED = H // 2
ROWS = 8
PAIR = 2 * ROWS
LIMIT_ROWS = 16
PIECES = 4
DEVICES = ("inline", "xline")
GROUP = 8
GRANT = 12 << 20
VMEM = pl.BlockSpec(memory_space=pltpu.VMEM)
SMEM = pl.BlockSpec(memory_space=pltpu.SMEM)


def square_weight(offset):
    relative = (offset / H) ** 2
    return relative * relative


def payload_layout(times, lines):
    mask_at = times * lines * REACH
    return mask_at, mask_at + lines * H


def by_parity(even, odd, work):
    here, size = lax.axis_index("inline"), lax.axis_size("inline")
    parity = lax.rem(here, 2)
    below, above = (here > 0).astype(jnp.float32), (here < size - 1).astype(jnp.float32)

    @pl.when(parity == 0)
    def _():
        work(even, False, above)
        work(odd, True, below)

    @pl.when(parity != 0)
    def _():
        work(even, True, below)
        work(odd, False, above)


def edges(value, axis, width):
    depth = value.shape[-1]
    length = value.shape[axis]
    low = lax.slice_in_dim(value, 0, width, axis=axis).reshape(-1, depth)
    return low, lax.slice_in_dim(value, length - width, length, axis=axis).reshape(-1, depth)


def for_even(low, high):
    return jnp.where(lax.axis_index("inline") % 2 == 0, high, low)


def for_odd(low, high):
    return for_even(high, low)


def payloads(rcv, sat, limit):
    depth = rcv.shape[-1]
    rows = edges(rcv, 2, REACH)
    rows = for_even(*rows), for_odd(*rows)
    *rows, sat = lax.optimization_barrier((*rows, sat))
    masks = edges((sat != 0).astype(jnp.bfloat16), 1, H)
    limits = jnp.full((LIMIT_ROWS, depth), limit[0]).astype(jnp.bfloat16)
    even = jnp.concatenate([rows[0], for_even(*masks), limits], axis=0)
    return even, jnp.concatenate([rows[1], for_odd(*masks), limits], axis=0)


def unpack_marks(times, limit, sat, even_in, odd_in, masks, limits):
    lines, cells, depth = sat.shape
    mask_at, limit_at = payload_layout(times, lines)

    def halo(arrived, low, there):
        row_at = 0 if low else H + cells
        for y in range(lines):
            masks[y, pl.ds(row_at, H), :] = arrived[pl.ds(mask_at + y * H, H), :].astype(jnp.float32)
        value = arrived[pl.ds(limit_at, LIMIT_ROWS), :].astype(jnp.float32)
        for part in range(H // LIMIT_ROWS):
            limits[pl.ds(row_at + part * LIMIT_ROWS, LIMIT_ROWS), :] = value

    by_parity(even_in, odd_in, halo)
    for y in range(lines):
        masks[y, pl.ds(H, cells), :] = (sat[y] != 0).astype(jnp.float32)
    limits[pl.ds(H, cells), :] = jnp.full((cells, depth), limit[0], jnp.int32).astype(jnp.float32)


def unpack_halo(even_in, odd_in, low_out, high_out):
    times, lines, _, depth = low_out.shape
    blank = jnp.zeros((ROWS, depth), jnp.float32)

    def halo(arrived, low, there):
        out, field_at, blank_at = (low_out, 0, REACH) if low else (high_out, ROWS, 0)
        for t in range(times):
            for y in range(lines):
                at = (t * lines + y) * REACH
                out[t, y, pl.ds(field_at, REACH), :] = arrived[pl.ds(at, REACH), :].astype(jnp.float32) * there
                out[t, y, pl.ds(blank_at, ROWS), :] = blank

    by_parity(even_in, odd_in, halo)


def image_of(center, far):
    image = center[0] * far[0]
    for c, f in zip(center[1:], far[1:]):
        image = image + c * f
    return image


def accumulate(center, sums, offsets, far_at, masked, mask_at):
    heavy, plain = sums
    times = range(len(center))
    near = {}
    for offset in offsets:
        far = far_at(offset)
        image = masked(image_of(center, far), offset)
        if abs(offset) <= SHARED:
            terms = [image * f for f in far]
            if abs(offset) in near:
                terms = [a + b for a, b in zip(near.pop(abs(offset)), terms)]
            near[abs(offset)] = terms
            if offset == 0 or -offset not in offsets or offset > 0:
                near.pop(abs(offset))
                plain = [plain[t] + terms[t] for t in times]
                if offset:
                    square = square_weight(offset)
                    heavy = [heavy[t] + terms[t] * square for t in times]
        else:
            square = square_weight(offset)
            weighed = image * jnp.where(mask_at(offset) != 0.0, SATURATION * SATURATION, square)
            plain = [plain[t] + image * far[t] for t in times]
            heavy = [heavy[t] + weighed * far[t] for t in times]
    return heavy, plain


def paired(largest, smallest=0):
    return [sign * size for size in range(smallest, largest + 1) for sign in ((-1, 1) if size else (1,))]


def tiles_of(field, y, base):
    times = field.shape[0]
    both = [field[t, y, pl.ds(base, PAIR), :].astype(jnp.float32) for t in range(times)]
    return [[rows[half * ROWS : (half + 1) * ROWS] for rows in both] for half in range(2)]


def inner_kernel(first, limit, middle, field, sat, heavy_out, plain_out, shifted, masks):
    times, lines, cells, depth = field.shape
    zero = jnp.zeros((ROWS, depth), jnp.float32)
    blank = jnp.zeros((REACH, depth), jnp.float32)
    for t in range(times):
        for y in range(lines):
            shifted[t, y, pl.ds(0, REACH), :] = blank
            shifted[t, y, pl.ds(REACH, cells), :] = field[t, y].astype(jnp.float32)
            shifted[t, y, pl.ds(REACH + cells, REACH), :] = blank
    for y in range(lines):
        masks[y, pl.ds(0, H), :] = blank[:H]
        masks[y, pl.ds(H, cells), :] = (sat[y] != 0).astype(jnp.float32)
        masks[y, pl.ds(H + cells, H), :] = blank[:H]
    inside = [(size <= limit[0]).astype(jnp.float32) for size in range(H + 1)]

    def tile(index, carry):
        base = pl.multiple_of(index * PAIR, PAIR)
        for y in range(lines):
            for half, center in enumerate(tiles_of(middle, y, first + base)):
                at = first + base + half * ROWS

                def add(offsets, sums):
                    return accumulate(
                        center,
                        sums,
                        offsets,
                        lambda h: [shifted[t, y, pl.ds(at + REACH + 2 * h, ROWS), :] for t in range(times)],
                        lambda image, h: image * inside[abs(h)] if abs(h) > ALWAYS else image,
                        lambda h: masks[y, pl.ds(at + H + h, ROWS), :],
                    )

                sums = add(paired(ALWAYS), ([zero] * times, [zero] * times))
                for low in range(ALWAYS + 1, H + 1, GROUP):
                    high = min(low + GROUP - 1, H)
                    if high <= SHARED:
                        parts = [(paired(high, low), limit[0] >= low)]
                    else:
                        below = first + base + PAIR - 1 - 2 * low >= 0
                        above = first + base + 2 * low < cells
                        parts = [
                            ([sign * size for size in range(low, high + 1)], jnp.logical_and(reach, limit[0] >= low))
                            for sign, reach in ((-1, below), (1, above))
                        ]
                    for offsets, needed in parts:
                        sums = lax.cond(needed, functools.partial(add, offsets), lambda kept: kept, sums)
                heavy, plain = sums
                rows = pl.ds(base + half * ROWS, ROWS)
                for t in range(times):
                    heavy_out[t, y, rows, :] = heavy[t]
                    plain_out[t, y, rows, :] = plain[t]
        return carry

    lax.fori_loop(0, heavy_out.shape[2] // PAIR, tile, 0)


def within(limits, at):
    def masked(image, offset):
        if abs(offset) <= ALWAYS:
            return image
        return jnp.where(limits[pl.ds(at + H + offset, ROWS), :] >= float(abs(offset)), image, 0.0)

    return masked


def add_outer(middle, heavy, plain, low, high, masks, limits):
    times, lines, cells, depth = middle.shape
    count = heavy[0].shape[2]
    for group in range(REACH // PAIR):

        def tile(index, carry, group=group):
            for side, shifted in ((0, low), (1, high)):

                @pl.when(index == side)
                def _():
                    first = cells - (group + 1) * PAIR if side else group * PAIR
                    number = first // count
                    base = pl.multiple_of(first - number * count + (index - side) * PAIR, PAIR)
                    origin = ROWS - cells if side else REACH
                    for y in range(lines):
                        for half, center in enumerate(tiles_of(middle, y, number * count + base)):
                            rows = pl.ds(base + half * ROWS, ROWS)
                            at = number * count + base + half * ROWS
                            rank = 2 * group + (1 - half if side else half)
                            sizes = range(ROWS // 2 * rank + 1, H + 1)
                            new_heavy, new_plain = accumulate(
                                center,
                                (
                                    [heavy[number][t, y, rows, :] for t in range(times)],
                                    [plain[number][t, y, rows, :] for t in range(times)],
                                ),
                                [size if side else -size for size in sizes],
                                lambda h: [shifted[t, y, pl.ds(at + origin + 2 * h, ROWS), :] for t in range(times)],
                                within(limits, at),
                                lambda h: masks[y, pl.ds(at + H + h, ROWS), :],
                            )
                            for t in range(times):
                                heavy[number][t, y, rows, :] = new_heavy[t]
                                plain[number][t, y, rows, :] = new_plain[t]

            return carry

        lax.fori_loop(0, 2, tile, 0)


def src_outer_kernel(limit, src, sat, even_in, odd_in, heavy_in, plain_in, heavy, plain, sums, low, high, masks, limits):
    times, lines, cells, depth = src.shape
    unpack_marks(times, limit, sat, even_in, odd_in, masks, limits)
    unpack_halo(even_in, odd_in, low, high)
    add_outer(src, [heavy], [plain], low, high, masks, limits)
    zero = jnp.zeros((ROWS, depth), jnp.float32)

    def add(index, totals):
        energy, weighted = totals
        base = pl.multiple_of(index * PAIR, PAIR)
        for y in range(lines):
            for half, center in enumerate(tiles_of(src, y, base)):
                rows = pl.ds(base + half * ROWS, ROWS)
                energy = energy + image_of(center, [plain[t, y, rows, :] for t in range(times)])
                weighted = weighted + image_of(center, [heavy[t, y, rows, :] for t in range(times)])
        return energy, weighted

    energy, weighted = lax.fori_loop(0, cells // PAIR, add, (zero, zero))
    sums[0:1, :] = jnp.sum(energy, axis=0, keepdims=True)
    sums[1:2, :] = jnp.sum(weighted, axis=0, keepdims=True)


def rcv_outer_kernel(limit, rcv, sat, even_marks, odd_marks, even_in, odd_in, *refs):
    parts, (low, high, masks, limits) = refs[len(refs) // 2 - 2 : -4], refs[-4:]
    unpack_marks(rcv.shape[0], limit, sat, even_marks, odd_marks, masks, limits)
    unpack_halo(even_in, odd_in, low, high)
    add_outer(rcv, parts[::2], parts[1::2], low, high, masks, limits)


def combine_kernel(cell_count, sums, src_heavy, src_plain, *refs):
    pieces, (src_out, rcv_out, semblance_out) = refs[:-3], refs[-3:]
    total = jnp.broadcast_to(jnp.sum(sums[...], axis=1, keepdims=True), sums.shape)
    energy, weighted = total[0:1], total[1:2]
    semblance = weighted / energy
    inverse_rms = 1.0 / jnp.sqrt(energy / cell_count + EPSILON)
    semblance_out[...] = semblance

    def put(out, start, heavy, plain):
        times, lines, count, _ = heavy.shape
        for t in range(times):
            for y in range(lines):
                value = inverse_rms * (heavy[t, y] - semblance * plain[t, y])
                out[t, y, pl.ds(start, count), :] = value.astype(jnp.bfloat16)

    put(src_out, 0, src_heavy, src_plain)
    start = 0
    for heavy, plain in zip(pieces[::2], pieces[1::2]):
        put(rcv_out, start, heavy, plain)
        start += heavy.shape[2]


def ride_kernel(rows_in, sums, rows):
    count = sums.shape[0]
    parts, rest = [], sums[...]
    for _ in range(3):
        parts.append(rest.astype(jnp.bfloat16).astype(jnp.float32))
        rest = rest - parts[-1]
    parts.append(jnp.zeros((LIMIT_ROWS - 3 * count, sums.shape[1]), jnp.float32))
    below = pl.ds(rows.shape[0] - LIMIT_ROWS, LIMIT_ROWS)
    rows[below, :] = jnp.concatenate(parts, axis=0).astype(jnp.bfloat16)


def sums_below(rows, count):
    at = rows.shape[0] - LIMIT_ROWS
    first, second, third = (
        lax.slice_in_dim(rows, at + i * count, at + (i + 1) * count).astype(jnp.float32) for i in range(3)
    )
    return first + second + third


def exchanges(size, lines):
    assert size % 2 == 0 and lines % 2 == 0
    even = [(i, i + 1) for i in range(0, size, 2)]
    odd = [(i, i + 1) for i in range(1, size - 1, 2)]
    routes = []
    for pairs in (even, odd):
        partner = dict(pairs + [(j, i) for i, j in pairs])
        routes.append(
            [
                (i * lines + line, partner[i] * lines + line if i in partner else i * lines + (line ^ 1))
                for i in range(size)
                for line in range(lines)
            ]
        )
    return routes


def reduction_steps(count):
    assert count & (count - 1) == 0
    bits = [1 << bit for bit in range(1, count.bit_length() - 1)]
    groups = [[1]]
    for at in range(0, len(bits), 2):
        low, *high = bits[at : at + 2]
        groups.append([low, high[0], low | high[0]] if high else [low])
    return groups


def local(source_field, receiver_field, sat_mask, offset_range):
    times, lines, cells, depth = source_field.shape
    size = lax.axis_size("inline")
    grant = pltpu.CompilerParams(vmem_limit_bytes=GRANT)
    image_cells = lines * cells * depth * (2 * H + 1)
    shape = jax.ShapeDtypeStruct
    total = shape((times, lines, cells, depth), jnp.float32)
    piece = shape((times, lines, cells // PIECES, depth), jnp.float32)
    field_out = shape(source_field.shape, jnp.bfloat16)
    extended = pltpu.VMEM((times, lines, cells + 2 * REACH, depth), jnp.float32)
    edge = pltpu.VMEM((times, lines, ROWS + REACH, depth), jnp.float32)
    masks = pltpu.VMEM((lines, cells + 2 * H, depth), jnp.float32)
    limits = pltpu.VMEM((cells + 2 * H, depth), jnp.float32)

    def call(kernel, name, out_shape, operands, scratch=(), share=0.0, aliases={}):
        return pl.pallas_call(
            kernel,
            out_shape=out_shape,
            in_specs=[SMEM if operand is offset_range else VMEM for operand in operands],
            out_specs=jax.tree.map(lambda _: VMEM, out_shape),
            scratch_shapes=scratch,
            input_output_aliases=aliases,
            cost_estimate=pl.CostEstimate(
                flops=int(24 * image_cells * share), bytes_accessed=1 << 20, transcendentals=0
            ),
            compiler_params=grant,
            name=name,
        )(*operands)

    src, rcv, sat = source_field, receiver_field, sat_mask
    even, odd = payloads(rcv, sat, offset_range)
    even_route, odd_route = exchanges(size, lax.axis_size("xline"))
    even = lax.ppermute(even, DEVICES, even_route)
    odd = lax.ppermute(odd, DEVICES, odd_route)
    odd_late = lax.ppermute(for_odd(*edges(src, 2, REACH)), DEVICES, odd_route)
    heavy, plain = call(
        functools.partial(inner_kernel, 0),
        "src_inner",
        (total, total),
        (offset_range, src, rcv, sat),
        [extended, masks],
        0.85,
    )
    def piece_at(number, src, rcv):
        return call(
            functools.partial(inner_kernel, number * (cells // PIECES)),
            "rcv_inner",
            (piece, piece),
            (offset_range, rcv, src, sat),
            [extended, masks],
            0.85 / PIECES,
        )

    heavy, plain, sums = call(
        src_outer_kernel,
        "src_outer",
        (total, total, shape((2, depth), jnp.float32)),
        (offset_range, src, sat, even, odd, heavy, plain),
        [edge, edge, masks, limits],
        0.25,
        {5: 0, 6: 1},
    )

    def finish(odd_late, even_late, *pieces):
        return call(
            rcv_outer_kernel,
            "rcv_outer",
            [piece] * len(pieces),
            (offset_range, rcv, sat, even, odd, even_late, odd_late, *pieces),
            [edge, edge, masks, limits],
            0.25,
            {7 + i: i for i in range(len(pieces))},
        )

    lines_all = lax.axis_size("xline")
    steps = reduction_steps(size * lines_all)
    assert len(steps) >= 3 and not any(lines_all in group for group in (steps[0], steps[-1]))
    sums, ahead = lax.optimization_barrier((sums, src))
    ride = jnp.concatenate([for_even(*edges(ahead, 2, REACH)), jnp.zeros((LIMIT_ROWS, depth), jnp.bfloat16)], axis=0)
    pieces = []
    for number, group in enumerate(steps):
        last = number == len(steps) - 1
        if number == 1:
            sums, odd_late = lax.optimization_barrier((sums, odd_late))
        if last:
            sums, even_late = lax.optimization_barrier((sums, even_late))
        sums, ahead = lax.optimization_barrier((sums, src))
        arrived = []
        for changed in group:
            if changed == lines_all:
                ride = call(
                    ride_kernel,
                    "ride",
                    shape(ride.shape, ride.dtype),
                    (ride, sums),
                    aliases={0: 0},
                )
                even_late = lax.ppermute(ride, DEVICES, even_route)
                arrived.append(sums_below(even_late, sums.shape[0]))
            else:
                route = [(i, i ^ (changed | 1)) for i in range(size * lines_all)]
                arrived.append(lax.ppermute(sums, DEVICES, route))
        if not last:
            share = range(1) if number == 0 else range(
                1 + (PIECES - 1) * (number - 1) // (len(steps) - 2), 1 + (PIECES - 1) * number // (len(steps) - 2)
            )
            result = [part for i in share for part in piece_at(i, ahead, rcv)]
            pieces += result
        else:
            result = pieces = list(finish(odd_late, even_late, *pieces))
        if len(arrived) == 3:
            low, high, both = arrived
            sums = (sums + low) + (high + both)
        else:
            sums = sums + arrived[0]
        sums, result = lax.optimization_barrier((sums, result))
        pieces[len(pieces) - len(result) :] = result

    cell_count = float(lines * lax.axis_size("xline") * cells * size * depth * (2 * H + 1))
    src_adj, rcv_adj, semblance = call(
        functools.partial(combine_kernel, cell_count),
        "combine",
        (field_out, field_out, shape((1, depth), jnp.float32)),
        (sums, heavy, plain, *pieces),
    )
    return src_adj, rcv_adj, semblance[0, 0]


def solution(mesh):
    return jax.shard_map(
        local,
        mesh=mesh,
        in_specs=(
            P(None, "xline", "inline", None),
            P(None, "xline", "inline", None),
            P("xline", "inline", None),
            P("inline"),
        ),
        out_specs=(P(None, "xline", "inline", None), P(None, "xline", "inline", None), P()),
        check_vma=False,
    )
```

```python
import functools

import jax
import jax.numpy as jnp
from jax import lax
from jax.experimental import pallas as pl
from jax.experimental.pallas import tpu as pltpu
from jax.sharding import PartitionSpec as P

H = 32
EPSILON = 1e-06
SATURATION = 0.25
REACH = 2 * H
ALWAYS = 8
SHARED = H // 2
ROWS = 8
PAIR = 2 * ROWS
LIMIT_ROWS = 16
PIECES = 4
DEVICES = ("inline", "xline")
GROUP = 8
GRANT = 12 << 20
VMEM = pl.BlockSpec(memory_space=pltpu.VMEM)
SMEM = pl.BlockSpec(memory_space=pltpu.SMEM)


def square_weight(offset):
    relative = (offset / H) ** 2
    return relative * relative


def payload_layout(times, lines):
    mask_at = times * lines * REACH
    return mask_at, mask_at + lines * H


def by_parity(even, odd, work):
    here, size = lax.axis_index("inline"), lax.axis_size("inline")
    parity = lax.rem(here, 2)
    below, above = (here > 0).astype(jnp.float32), (here < size - 1).astype(jnp.float32)

    @pl.when(parity == 0)
    def _():
        work(even, False, above)
        work(odd, True, below)

    @pl.when(parity != 0)
    def _():
        work(even, True, below)
        work(odd, False, above)


def edges(value, axis, width):
    depth = value.shape[-1]
    length = value.shape[axis]
    low = lax.slice_in_dim(value, 0, width, axis=axis).reshape(-1, depth)
    return low, lax.slice_in_dim(value, length - width, length, axis=axis).reshape(-1, depth)


def for_even(low, high):
    return jnp.where(lax.axis_index("inline") % 2 == 0, high, low)


def for_odd(low, high):
    return for_even(high, low)


def payloads(rcv, sat, limit):
    depth = rcv.shape[-1]
    rows = edges(rcv, 2, REACH)
    rows = for_even(*rows), for_odd(*rows)
    *rows, sat = lax.optimization_barrier((*rows, sat))
    masks = edges((sat != 0).astype(jnp.bfloat16), 1, H)
    limits = jnp.full((LIMIT_ROWS, depth), limit[0]).astype(jnp.bfloat16)
    even = jnp.concatenate([rows[0], for_even(*masks), limits], axis=0)
    return even, jnp.concatenate([rows[1], for_odd(*masks), limits], axis=0)


def unpack_marks(times, limit, sat, even_in, odd_in, masks, limits):
    lines, cells, depth = sat.shape
    mask_at, limit_at = payload_layout(times, lines)

    def halo(arrived, low, there):
        row_at = 0 if low else H + cells
        for y in range(lines):
            masks[y, pl.ds(row_at, H), :] = arrived[pl.ds(mask_at + y * H, H), :].astype(jnp.float32)
        value = arrived[pl.ds(limit_at, LIMIT_ROWS), :].astype(jnp.float32)
        for part in range(H // LIMIT_ROWS):
            limits[pl.ds(row_at + part * LIMIT_ROWS, LIMIT_ROWS), :] = value

    by_parity(even_in, odd_in, halo)
    for y in range(lines):
        masks[y, pl.ds(H, cells), :] = (sat[y] != 0).astype(jnp.float32)
    limits[pl.ds(H, cells), :] = jnp.full((cells, depth), limit[0], jnp.int32).astype(jnp.float32)


def unpack_halo(even_in, odd_in, low_out, high_out):
    times, lines, _, depth = low_out.shape
    blank = jnp.zeros((ROWS, depth), jnp.float32)

    def halo(arrived, low, there):
        out, field_at, blank_at = (low_out, 0, REACH) if low else (high_out, ROWS, 0)
        for t in range(times):
            for y in range(lines):
                at = (t * lines + y) * REACH
                out[t, y, pl.ds(field_at, REACH), :] = arrived[pl.ds(at, REACH), :].astype(jnp.float32) * there
                out[t, y, pl.ds(blank_at, ROWS), :] = blank

    by_parity(even_in, odd_in, halo)


def image_of(center, far):
    image = center[0] * far[0]
    for c, f in zip(center[1:], far[1:]):
        image = image + c * f
    return image


def accumulate(center, sums, offsets, far_at, masked, mask_at):
    heavy, plain = sums
    times = range(len(center))
    near = {}
    for offset in offsets:
        far = far_at(offset)
        image = masked(image_of(center, far), offset)
        if abs(offset) <= SHARED:
            terms = [image * f for f in far]
            if abs(offset) in near:
                terms = [a + b for a, b in zip(near.pop(abs(offset)), terms)]
            near[abs(offset)] = terms
            if offset == 0 or -offset not in offsets or offset > 0:
                near.pop(abs(offset))
                plain = [plain[t] + terms[t] for t in times]
                if offset:
                    square = square_weight(offset)
                    heavy = [heavy[t] + terms[t] * square for t in times]
        else:
            square = square_weight(offset)
            weighed = image * jnp.where(mask_at(offset) != 0.0, SATURATION * SATURATION, square)
            plain = [plain[t] + image * far[t] for t in times]
            heavy = [heavy[t] + weighed * far[t] for t in times]
    return heavy, plain


def paired(largest, smallest=0):
    return [sign * size for size in range(smallest, largest + 1) for sign in ((-1, 1) if size else (1,))]


def tiles_of(field, y, base):
    times = field.shape[0]
    both = [field[t, y, pl.ds(base, PAIR), :].astype(jnp.float32) for t in range(times)]
    return [[rows[half * ROWS : (half + 1) * ROWS] for rows in both] for half in range(2)]


def inner_kernel(first, limit, middle, field, sat, heavy_out, plain_out, shifted, masks):
    times, lines, cells, depth = field.shape
    zero = jnp.zeros((ROWS, depth), jnp.float32)
    blank = jnp.zeros((REACH, depth), jnp.float32)
    for t in range(times):
        for y in range(lines):
            shifted[t, y, pl.ds(0, REACH), :] = blank
            shifted[t, y, pl.ds(REACH, cells), :] = field[t, y].astype(jnp.float32)
            shifted[t, y, pl.ds(REACH + cells, REACH), :] = blank
    for y in range(lines):
        masks[y, pl.ds(0, H), :] = blank[:H]
        masks[y, pl.ds(H, cells), :] = (sat[y] != 0).astype(jnp.float32)
        masks[y, pl.ds(H + cells, H), :] = blank[:H]
    inside = [(size <= limit[0]).astype(jnp.float32) for size in range(H + 1)]

    def tile(index, carry):
        base = pl.multiple_of(index * PAIR, PAIR)
        for y in range(lines):
            for half, center in enumerate(tiles_of(middle, y, first + base)):
                at = first + base + half * ROWS

                def add(offsets, sums):
                    return accumulate(
                        center,
                        sums,
                        offsets,
                        lambda h: [shifted[t, y, pl.ds(at + REACH + 2 * h, ROWS), :] for t in range(times)],
                        lambda image, h: image * inside[abs(h)] if abs(h) > ALWAYS else image,
                        lambda h: masks[y, pl.ds(at + H + h, ROWS), :],
                    )

                sums = add(paired(ALWAYS), ([zero] * times, [zero] * times))
                for low in range(ALWAYS + 1, H + 1, GROUP):
                    high = min(low + GROUP - 1, H)
                    if high <= SHARED:
                        parts = [(paired(high, low), limit[0] >= low)]
                    else:
                        below = first + base + PAIR - 1 - 2 * low >= 0
                        above = first + base + 2 * low < cells
                        parts = [
                            ([sign * size for size in range(low, high + 1)], jnp.logical_and(reach, limit[0] >= low))
                            for sign, reach in ((-1, below), (1, above))
                        ]
                    for offsets, needed in parts:
                        sums = lax.cond(needed, functools.partial(add, offsets), lambda kept: kept, sums)
                heavy, plain = sums
                rows = pl.ds(base + half * ROWS, ROWS)
                for t in range(times):
                    heavy_out[t, y, rows, :] = heavy[t]
                    plain_out[t, y, rows, :] = plain[t]
        return carry

    lax.fori_loop(0, heavy_out.shape[2] // PAIR, tile, 0)


def within(limits, at):
    def masked(image, offset):
        if abs(offset) <= ALWAYS:
            return image
        return jnp.where(limits[pl.ds(at + H + offset, ROWS), :] >= float(abs(offset)), image, 0.0)

    return masked


def add_outer(middle, heavy, plain, low, high, masks, limits):
    times, lines, cells, depth = middle.shape
    count = heavy[0].shape[2]
    for group in range(REACH // PAIR):

        def tile(index, carry, group=group):
            for side, shifted in ((0, low), (1, high)):

                @pl.when(index == side)
                def _():
                    first = cells - (group + 1) * PAIR if side else group * PAIR
                    number = first // count
                    base = pl.multiple_of(first - number * count + (index - side) * PAIR, PAIR)
                    origin = ROWS - cells if side else REACH
                    for y in range(lines):
                        for half, center in enumerate(tiles_of(middle, y, number * count + base)):
                            rows = pl.ds(base + half * ROWS, ROWS)
                            at = number * count + base + half * ROWS
                            rank = 2 * group + (1 - half if side else half)
                            sizes = range(ROWS // 2 * rank + 1, H + 1)
                            new_heavy, new_plain = accumulate(
                                center,
                                (
                                    [heavy[number][t, y, rows, :] for t in range(times)],
                                    [plain[number][t, y, rows, :] for t in range(times)],
                                ),
                                [size if side else -size for size in sizes],
                                lambda h: [shifted[t, y, pl.ds(at + origin + 2 * h, ROWS), :] for t in range(times)],
                                within(limits, at),
                                lambda h: masks[y, pl.ds(at + H + h, ROWS), :],
                            )
                            for t in range(times):
                                heavy[number][t, y, rows, :] = new_heavy[t]
                                plain[number][t, y, rows, :] = new_plain[t]

            return carry

        lax.fori_loop(0, 2, tile, 0)


def src_outer_kernel(limit, src, sat, even_in, odd_in, heavy_in, plain_in, heavy, plain, sums, low, high, masks, limits):
    times, lines, cells, depth = src.shape
    unpack_marks(times, limit, sat, even_in, odd_in, masks, limits)
    unpack_halo(even_in, odd_in, low, high)
    add_outer(src, [heavy], [plain], low, high, masks, limits)
    zero = jnp.zeros((ROWS, depth), jnp.float32)

    def add(index, totals):
        energy, weighted = totals
        base = pl.multiple_of(index * PAIR, PAIR)
        for y in range(lines):
            for half, center in enumerate(tiles_of(src, y, base)):
                rows = pl.ds(base + half * ROWS, ROWS)
                energy = energy + image_of(center, [plain[t, y, rows, :] for t in range(times)])
                weighted = weighted + image_of(center, [heavy[t, y, rows, :] for t in range(times)])
        return energy, weighted

    energy, weighted = lax.fori_loop(0, cells // PAIR, add, (zero, zero))
    sums[0:1, :] = jnp.sum(energy, axis=0, keepdims=True)
    sums[1:2, :] = jnp.sum(weighted, axis=0, keepdims=True)


def rcv_outer_kernel(limit, rcv, sat, even_marks, odd_marks, even_in, odd_in, *refs):
    parts, (low, high, masks, limits) = refs[len(refs) // 2 - 2 : -4], refs[-4:]
    unpack_marks(rcv.shape[0], limit, sat, even_marks, odd_marks, masks, limits)
    unpack_halo(even_in, odd_in, low, high)
    add_outer(rcv, parts[::2], parts[1::2], low, high, masks, limits)


def combine_kernel(cell_count, sums, src_heavy, src_plain, *refs):
    pieces, (src_out, rcv_out, semblance_out) = refs[:-3], refs[-3:]
    total = jnp.broadcast_to(jnp.sum(sums[...], axis=1, keepdims=True), sums.shape)
    energy, weighted = total[0:1], total[1:2]
    semblance = weighted / energy
    inverse_rms = 1.0 / jnp.sqrt(energy / cell_count + EPSILON)
    semblance_out[...] = semblance

    def put(out, start, heavy, plain):
        times, lines, count, _ = heavy.shape
        for t in range(times):
            for y in range(lines):
                value = inverse_rms * (heavy[t, y] - semblance * plain[t, y])
                out[t, y, pl.ds(start, count), :] = value.astype(jnp.bfloat16)

    put(src_out, 0, src_heavy, src_plain)
    start = 0
    for heavy, plain in zip(pieces[::2], pieces[1::2]):
        put(rcv_out, start, heavy, plain)
        start += heavy.shape[2]


def ride_kernel(rows_in, sums, rows):
    count = sums.shape[0]
    parts, rest = [], sums[...]
    for _ in range(3):
        parts.append(rest.astype(jnp.bfloat16).astype(jnp.float32))
        rest = rest - parts[-1]
    parts.append(jnp.zeros((LIMIT_ROWS - 3 * count, sums.shape[1]), jnp.float32))
    below = pl.ds(rows.shape[0] - LIMIT_ROWS, LIMIT_ROWS)
    rows[below, :] = jnp.concatenate(parts, axis=0).astype(jnp.bfloat16)


def sums_below(rows, count):
    at = rows.shape[0] - LIMIT_ROWS
    first, second, third = (
        lax.slice_in_dim(rows, at + i * count, at + (i + 1) * count).astype(jnp.float32) for i in range(3)
    )
    return first + second + third


def exchanges(size, lines):
    assert size % 2 == 0 and lines % 2 == 0
    even = [(i, i + 1) for i in range(0, size, 2)]
    odd = [(i, i + 1) for i in range(1, size - 1, 2)]
    routes = []
    for pairs in (even, odd):
        partner = dict(pairs + [(j, i) for i, j in pairs])
        routes.append(
            [
                (i * lines + line, partner[i] * lines + line if i in partner else i * lines + (line ^ 1))
                for i in range(size)
                for line in range(lines)
            ]
        )
    return routes


def reduction_steps(count):
    assert count & (count - 1) == 0
    bits = [1 << bit for bit in range(1, count.bit_length() - 1)]
    groups = [[1]]
    for at in range(0, len(bits), 2):
        low, *high = bits[at : at + 2]
        groups.append([low, high[0], low | high[0]] if high else [low])
    return groups


def local(source_field, receiver_field, sat_mask, offset_range):
    times, lines, cells, depth = source_field.shape
    size = lax.axis_size("inline")
    grant = pltpu.CompilerParams(vmem_limit_bytes=GRANT)
    image_cells = lines * cells * depth * (2 * H + 1)
    shape = jax.ShapeDtypeStruct
    total = shape((times, lines, cells, depth), jnp.float32)
    piece = shape((times, lines, cells // PIECES, depth), jnp.float32)
    field_out = shape(source_field.shape, jnp.bfloat16)
    extended = pltpu.VMEM((times, lines, cells + 2 * REACH, depth), jnp.float32)
    edge = pltpu.VMEM((times, lines, ROWS + REACH, depth), jnp.float32)
    masks = pltpu.VMEM((lines, cells + 2 * H, depth), jnp.float32)
    limits = pltpu.VMEM((cells + 2 * H, depth), jnp.float32)

    def call(kernel, name, out_shape, operands, scratch=(), share=0.0, aliases={}):
        return pl.pallas_call(
            kernel,
            out_shape=out_shape,
            in_specs=[SMEM if operand is offset_range else VMEM for operand in operands],
            out_specs=jax.tree.map(lambda _: VMEM, out_shape),
            scratch_shapes=scratch,
            input_output_aliases=aliases,
            cost_estimate=pl.CostEstimate(
                flops=int(24 * image_cells * share), bytes_accessed=1 << 20, transcendentals=0
            ),
            compiler_params=grant,
            name=name,
        )(*operands)

    src, rcv, sat = source_field, receiver_field, sat_mask
    even, odd = payloads(rcv, sat, offset_range)
    even_route, odd_route = exchanges(size, lax.axis_size("xline"))
    even = lax.ppermute(even, DEVICES, even_route)
    odd = lax.ppermute(odd, DEVICES, odd_route)
    low_high = edges(src, 2, REACH)
    odd_late = lax.ppermute(for_odd(*low_high), DEVICES, odd_route)
    even_late = lax.ppermute(for_even(*low_high), DEVICES, even_route)
    heavy, plain = call(
        functools.partial(inner_kernel, 0),
        "src_inner",
        (total, total),
        (offset_range, src, rcv, sat),
        [extended, masks],
        0.85,
    )
    def piece_at(number, src, rcv):
        return call(
            functools.partial(inner_kernel, number * (cells // PIECES)),
            "rcv_inner",
            (piece, piece),
            (offset_range, rcv, src, sat),
            [extended, masks],
            0.85 / PIECES,
        )

    heavy, plain, sums = call(
        src_outer_kernel,
        "src_outer",
        (total, total, shape((2, depth), jnp.float32)),
        (offset_range, src, sat, even, odd, heavy, plain),
        [edge, edge, masks, limits],
        0.25,
        {5: 0, 6: 1},
    )

    def finish(odd_late, even_late, *pieces):
        return call(
            rcv_outer_kernel,
            "rcv_outer",
            [piece] * len(pieces),
            (offset_range, rcv, sat, even, odd, even_late, odd_late, *pieces),
            [edge, edge, masks, limits],
            0.25,
            {7 + i: i for i in range(len(pieces))},
        )

    lines_all = lax.axis_size("xline")
    count = size * lines_all
    spread = jnp.broadcast_to(sums[None], (count, *sums.shape))
    gathered = lax.all_to_all(spread, DEVICES, 0, 0, tiled=True)
    sums, ahead = lax.optimization_barrier((sums, src))
    pieces = [part for i in range(PIECES) for part in piece_at(i, ahead, rcv)]
    pieces = finish(odd_late, even_late, *pieces)
    sums = jnp.sum(gathered, axis=0)

    cell_count = float(lines * lax.axis_size("xline") * cells * size * depth * (2 * H + 1))
    src_adj, rcv_adj, semblance = call(
        functools.partial(combine_kernel, cell_count),
        "combine",
        (field_out, field_out, shape((1, depth), jnp.float32)),
        (sums, heavy, plain, *pieces),
    )
    return src_adj, rcv_adj, semblance[0, 0]


def solution(mesh):
    return jax.shard_map(
        local,
        mesh=mesh,
        in_specs=(
            P(None, "xline", "inline", None),
            P(None, "xline", "inline", None),
            P("xline", "inline", None),
            P("inline"),
        ),
        out_specs=(P(None, "xline", "inline", None), P(None, "xline", "inline", None), P()),
        check_vma=False,
    )
```

```python
import functools

import jax
import jax.numpy as jnp
from jax import lax
from jax.experimental import pallas as pl
from jax.experimental.pallas import tpu as pltpu
from jax.sharding import PartitionSpec as P

H = 32
EPSILON = 1e-06
SATURATION = 0.25
REACH = 2 * H
ALWAYS = 8
SHARED = H // 2
ROWS = 8
PAIR = 2 * ROWS
LIMIT_ROWS = 16
DEVICES = ("inline", "xline")
GROUP = 8
GRANT = 12 << 20
VMEM = pl.BlockSpec(memory_space=pltpu.VMEM)
SMEM = pl.BlockSpec(memory_space=pltpu.SMEM)


def square_weight(offset):
    relative = (offset / H) ** 2
    return relative * relative


def cap_of(mask):
    return jnp.where(mask != 0, SATURATION * SATURATION, 2.0)


def payload_layout(times, lines):
    mask_at = times * lines * REACH
    return mask_at, mask_at + lines * H


def by_parity(even, odd, work):
    here, size = lax.axis_index("inline"), lax.axis_size("inline")
    parity = lax.rem(here, 2)
    below, above = (here > 0).astype(jnp.float32), (here < size - 1).astype(jnp.float32)

    @pl.when(parity == 0)
    def _():
        work(even, False, above)
        work(odd, True, below)

    @pl.when(parity != 0)
    def _():
        work(even, True, below)
        work(odd, False, above)


def edges(value, axis, width):
    depth = value.shape[-1]
    length = value.shape[axis]
    low = lax.slice_in_dim(value, 0, width, axis=axis).reshape(-1, depth)
    return low, lax.slice_in_dim(value, length - width, length, axis=axis).reshape(-1, depth)


def for_even(low, high):
    return jnp.where(lax.axis_index("inline") % 2 == 0, high, low)


def for_odd(low, high):
    return for_even(high, low)


def payloads(rcv, sat, limit):
    depth = rcv.shape[-1]
    rows = edges(rcv, 2, REACH)
    rows = for_even(*rows), for_odd(*rows)
    *rows, sat, limit = lax.optimization_barrier((*rows, sat, limit))
    masks = edges((sat != 0).astype(jnp.bfloat16), 1, H)
    limits = jnp.full((LIMIT_ROWS, depth), limit[0]).astype(jnp.bfloat16)
    even = jnp.concatenate([rows[0], for_even(*masks), limits], axis=0)
    return limit, even, jnp.concatenate([rows[1], for_odd(*masks), limits], axis=0)


def unpack_marks(times, limit, sat, even_in, odd_in, caps, limits):
    lines, cells, depth = sat.shape
    mask_at, limit_at = payload_layout(times, lines)

    def halo(arrived, low, there):
        row_at = 0 if low else H + cells
        for y in range(lines):
            caps[y, pl.ds(row_at, H), :] = cap_of(arrived[pl.ds(mask_at + y * H, H), :].astype(jnp.float32))
        value = arrived[pl.ds(limit_at, LIMIT_ROWS), :].astype(jnp.float32)
        for part in range(H // LIMIT_ROWS):
            limits[pl.ds(row_at + part * LIMIT_ROWS, LIMIT_ROWS), :] = value

    by_parity(even_in, odd_in, halo)
    for y in range(lines):
        caps[y, pl.ds(H, cells), :] = cap_of(sat[y])
    limits[pl.ds(H, cells), :] = jnp.full((cells, depth), limit[0], jnp.int32).astype(jnp.float32)


def unpack_halo(even_in, odd_in, low_out, high_out):
    times, lines, _, depth = low_out.shape
    blank = jnp.zeros((ROWS, depth), jnp.float32)

    def halo(arrived, low, there):
        out, field_at, blank_at = (low_out, 0, REACH) if low else (high_out, ROWS, 0)
        for t in range(times):
            for y in range(lines):
                at = (t * lines + y) * REACH
                out[t, y, pl.ds(field_at, REACH), :] = arrived[pl.ds(at, REACH), :].astype(jnp.float32) * there
                out[t, y, pl.ds(blank_at, ROWS), :] = blank

    by_parity(even_in, odd_in, halo)


def image_of(center, far):
    image = center[0] * far[0]
    for c, f in zip(center[1:], far[1:]):
        image = image + c * f
    return image


def accumulate(center, sums, offsets, far_at, masked, cap_at):
    heavy, plain = sums
    times = range(len(center))
    near = {}
    for offset in offsets:
        far = far_at(offset)
        image = masked(image_of(center, far), offset)
        if abs(offset) <= SHARED:
            terms = [image * f for f in far]
            if abs(offset) in near:
                terms = [a + b for a, b in zip(near.pop(abs(offset)), terms)]
            near[abs(offset)] = terms
            if offset == 0 or -offset not in offsets or offset > 0:
                near.pop(abs(offset))
                plain = [plain[t] + terms[t] for t in times]
                if offset:
                    square = square_weight(offset)
                    heavy = [heavy[t] + terms[t] * square for t in times]
        else:
            square = square_weight(offset)
            weighed = image * jnp.minimum(cap_at(offset), square)
            plain = [plain[t] + image * far[t] for t in times]
            heavy = [heavy[t] + weighed * far[t] for t in times]
    return heavy, plain


def paired(largest, smallest=0):
    return [sign * size for size in range(smallest, largest + 1) for sign in ((-1, 1) if size else (1,))]


def tiles_of(field, y, base):
    times = field.shape[0]
    both = [field[t, y, pl.ds(base, PAIR), :].astype(jnp.float32) for t in range(times)]
    return [[rows[half * ROWS : (half + 1) * ROWS] for rows in both] for half in range(2)]


def inner_kernel(limit, middle, field, sat, heavy_out, plain_out, shifted, caps):
    times, lines, cells, depth = field.shape
    zero = jnp.zeros((ROWS, depth), jnp.float32)
    blank = jnp.zeros((REACH, depth), jnp.float32)
    for t in range(times):
        for y in range(lines):
            shifted[t, y, pl.ds(0, REACH), :] = blank
            shifted[t, y, pl.ds(REACH, cells), :] = field[t, y].astype(jnp.float32)
            shifted[t, y, pl.ds(REACH + cells, REACH), :] = blank
    for y in range(lines):
        caps[y, pl.ds(0, H), :] = blank[:H]
        caps[y, pl.ds(H, cells), :] = cap_of(sat[y])
        caps[y, pl.ds(H + cells, H), :] = blank[:H]
    inside = [(size <= limit[0]).astype(jnp.float32) for size in range(H + 1)]

    def tile(index, carry):
        base = pl.multiple_of(index * PAIR, PAIR)
        for y in range(lines):
            for half, center in enumerate(tiles_of(middle, y, base)):
                at = base + half * ROWS

                def add(offsets, masked, sums):
                    return accumulate(
                        center,
                        sums,
                        offsets,
                        lambda h: [shifted[t, y, pl.ds(at + REACH + 2 * h, ROWS), :] for t in range(times)],
                        lambda image, h: image * inside[abs(h)] if masked else image,
                        lambda h: caps[y, pl.ds(at + H + h, ROWS), :],
                    )

                sums = add(paired(ALWAYS), False, ([zero] * times, [zero] * times))
                for low in range(ALWAYS + 1, H + 1, GROUP):
                    high = min(low + GROUP - 1, H)
                    if high <= SHARED:
                        parts = [(paired(high, low), limit[0] >= low)]
                    else:
                        below = base + PAIR - 1 - 2 * low >= 0
                        above = base + 2 * low < cells
                        parts = [
                            ([sign * size for size in range(low, high + 1)], jnp.logical_and(reach, limit[0] >= low))
                            for sign, reach in ((-1, below), (1, above))
                        ]
                    for offsets, needed in parts:
                        sums = lax.cond(
                            needed,
                            lambda sums: lax.cond(
                                limit[0] >= high,
                                functools.partial(add, offsets, False),
                                functools.partial(add, offsets, True),
                                sums,
                            ),
                            lambda kept: kept,
                            sums,
                        )
                heavy, plain = sums
                rows = pl.ds(base + half * ROWS, ROWS)
                for t in range(times):
                    heavy_out[t, y, rows, :] = heavy[t]
                    plain_out[t, y, rows, :] = plain[t]
        return carry

    lax.fori_loop(0, heavy_out.shape[2] // PAIR, tile, 0)


def within(limits, at):
    def masked(image, offset):
        if abs(offset) <= ALWAYS:
            return image
        return jnp.where(limits[pl.ds(at + H + offset, ROWS), :] >= float(abs(offset)), image, 0.0)

    return masked


def add_outer(middle, heavy, plain, low, high, caps, limits):
    times, lines, cells, depth = middle.shape
    count = heavy[0].shape[2]
    for group in range(REACH // PAIR):

        def tile(index, carry, group=group):
            for side, shifted in ((0, low), (1, high)):

                @pl.when(index == side)
                def _():
                    first = cells - (group + 1) * PAIR if side else group * PAIR
                    number = first // count
                    base = pl.multiple_of(first - number * count + (index - side) * PAIR, PAIR)
                    origin = ROWS - cells if side else REACH
                    for y in range(lines):
                        for half, center in enumerate(tiles_of(middle, y, number * count + base)):
                            rows = pl.ds(base + half * ROWS, ROWS)
                            at = number * count + base + half * ROWS
                            rank = 2 * group + (1 - half if side else half)
                            sizes = range(ROWS // 2 * rank + 1, H + 1)
                            new_heavy, new_plain = accumulate(
                                center,
                                (
                                    [heavy[number][t, y, rows, :] for t in range(times)],
                                    [plain[number][t, y, rows, :] for t in range(times)],
                                ),
                                [size if side else -size for size in sizes],
                                lambda h: [shifted[t, y, pl.ds(at + origin + 2 * h, ROWS), :] for t in range(times)],
                                within(limits, at),
                                lambda h: caps[y, pl.ds(at + H + h, ROWS), :],
                            )
                            for t in range(times):
                                heavy[number][t, y, rows, :] = new_heavy[t]
                                plain[number][t, y, rows, :] = new_plain[t]

            return carry

        lax.fori_loop(0, 2, tile, 0)


def src_outer_kernel(limit, src, sat, even_in, odd_in, heavy_in, plain_in, heavy, plain, sums, low, high, caps, limits):
    times, lines, cells, depth = src.shape
    unpack_marks(times, limit, sat, even_in, odd_in, caps, limits)
    unpack_halo(even_in, odd_in, low, high)
    add_outer(src, [heavy], [plain], low, high, caps, limits)
    zero = jnp.zeros((ROWS, depth), jnp.float32)

    def add(index, totals):
        energy, weighted = totals
        base = pl.multiple_of(index * PAIR, PAIR)
        for y in range(lines):
            for half, center in enumerate(tiles_of(src, y, base)):
                rows = pl.ds(base + half * ROWS, ROWS)
                energy = energy + image_of(center, [plain[t, y, rows, :] for t in range(times)])
                weighted = weighted + image_of(center, [heavy[t, y, rows, :] for t in range(times)])
        return energy, weighted

    energy, weighted = lax.fori_loop(0, cells // PAIR, add, (zero, zero))
    sums[...] = jnp.broadcast_to(
        jnp.concatenate([jnp.sum(part, axis=0, keepdims=True) for part in (energy, weighted)], axis=0)[None], sums.shape
    )


def rcv_outer_kernel(limit, rcv, sat, even_marks, odd_marks, even_in, odd_in, *refs):
    parts, (low, high, caps, limits) = refs[len(refs) // 2 - 2 : -4], refs[-4:]
    unpack_marks(rcv.shape[0], limit, sat, even_marks, odd_marks, caps, limits)
    unpack_halo(even_in, odd_in, low, high)
    add_outer(rcv, parts[::2], parts[1::2], low, high, caps, limits)


def combine_kernel(cell_count, sums, src_heavy, src_plain, *refs):
    pieces, (src_out, rcv_out, semblance_out) = refs[:-3], refs[-3:]
    total = jnp.sum(sums[...], axis=0)
    total = jnp.broadcast_to(jnp.sum(total, axis=1, keepdims=True), total.shape)
    energy, weighted = total[0:1], total[1:2]
    semblance = weighted / energy
    inverse_rms = 1.0 / jnp.sqrt(energy / cell_count + EPSILON)
    semblance_out[...] = semblance

    def put(out, start, heavy, plain):
        times, lines, count, _ = heavy.shape
        for t in range(times):
            for y in range(lines):
                value = inverse_rms * (heavy[t, y] - semblance * plain[t, y])
                out[t, y, pl.ds(start, count), :] = value.astype(jnp.bfloat16)

    put(src_out, 0, src_heavy, src_plain)
    start = 0
    for heavy, plain in zip(pieces[::2], pieces[1::2]):
        put(rcv_out, start, heavy, plain)
        start += heavy.shape[2]


def exchanges(size, lines):
    assert size % 2 == 0 and lines % 2 == 0
    even = [(i, i + 1) for i in range(0, size, 2)]
    odd = [(i, i + 1) for i in range(1, size - 1, 2)]
    routes = []
    for pairs in (even, odd):
        partner = dict(pairs + [(j, i) for i, j in pairs])
        routes.append(
            [
                (i * lines + line, partner[i] * lines + line if i in partner else i * lines + (line ^ 1))
                for i in range(size)
                for line in range(lines)
            ]
        )
    return routes


def local(source_field, receiver_field, sat_mask, offset_range):
    times, lines, cells, depth = source_field.shape
    size = lax.axis_size("inline")
    grant = pltpu.CompilerParams(vmem_limit_bytes=GRANT)
    image_cells = lines * cells * depth * (2 * H + 1)
    shape = jax.ShapeDtypeStruct
    total = shape((times, lines, cells, depth), jnp.float32)
    field_out = shape(source_field.shape, jnp.bfloat16)
    extended = pltpu.VMEM((times, lines, cells + 2 * REACH, depth), jnp.float32)
    edge = pltpu.VMEM((times, lines, ROWS + REACH, depth), jnp.float32)
    caps = pltpu.VMEM((lines, cells + 2 * H, depth), jnp.float32)
    limits = pltpu.VMEM((cells + 2 * H, depth), jnp.float32)

    def call(kernel, name, out_shape, operands, scratch=(), share=0.0, aliases={}):
        return pl.pallas_call(
            kernel,
            out_shape=out_shape,
            in_specs=[SMEM if operand is offset_range else VMEM for operand in operands],
            out_specs=jax.tree.map(lambda _: VMEM, out_shape),
            scratch_shapes=scratch,
            input_output_aliases=aliases,
            cost_estimate=pl.CostEstimate(
                flops=int(24 * image_cells * share), bytes_accessed=1 << 20, transcendentals=0
            ),
            compiler_params=grant,
            name=name,
        )(*operands)

    src, rcv, sat = source_field, receiver_field, sat_mask
    offset_range, even, odd = payloads(rcv, sat, offset_range)
    even_route, odd_route = exchanges(size, lax.axis_size("xline"))
    even = lax.ppermute(even, DEVICES, even_route)
    odd = lax.ppermute(odd, DEVICES, odd_route)
    odd_late = lax.ppermute(for_odd(*edges(src, 2, REACH)), DEVICES, odd_route)

    heavy, plain = call(
        inner_kernel,
        "src_inner",
        (total, total),
        (offset_range, src, rcv, sat),
        [extended, caps],
        0.85,
    )
    count = size * lax.axis_size("xline")
    heavy, plain, sums = call(
        src_outer_kernel,
        "src_outer",
        (total, total, shape((count, 2, depth), jnp.float32)),
        (offset_range, src, sat, even, odd, heavy, plain),
        [edge, edge, caps, limits],
        0.25,
        {5: 0, 6: 1},
    )

    def finish(odd_late, even_late, *pieces):
        return call(
            rcv_outer_kernel,
            "rcv_outer",
            [piece] * len(pieces),
            (offset_range, rcv, sat, even, odd, even_late, odd_late, *pieces),
            [edge, edge, caps, limits],
            0.25,
            {7 + i: i for i in range(len(pieces))},
        )

    gathered = lax.all_to_all(sums, DEVICES, 0, 0, tiled=True)
    sums, ahead = lax.optimization_barrier((sums, src))
    even_late = lax.ppermute(for_even(*edges(ahead, 2, REACH)), DEVICES, even_route)
    pieces = call(
        inner_kernel,
        "rcv_inner",
        (total, total),
        (offset_range, rcv, ahead, sat),
        [extended, caps],
        0.85,
    )
    pieces = call(
        rcv_outer_kernel,
        "rcv_outer",
        (total, total),
        (offset_range, rcv, sat, even, odd, even_late, odd_late, *pieces),
        [edge, edge, caps, limits],
        0.25,
        {7: 0, 8: 1},
    )

    cell_count = float(lines * lax.axis_size("xline") * cells * size * depth * (2 * H + 1))
    src_adj, rcv_adj, semblance = call(
        functools.partial(combine_kernel, cell_count),
        "combine",
        (field_out, field_out, shape((1, depth), jnp.float32)),
        (gathered, heavy, plain, *pieces),
    )
    return src_adj, rcv_adj, semblance[0, 0]


def solution(mesh):
    return jax.shard_map(
        local,
        mesh=mesh,
        in_specs=(
            P(None, "xline", "inline", None),
            P(None, "xline", "inline", None),
            P("xline", "inline", None),
            P("inline"),
        ),
        out_specs=(P(None, "xline", "inline", None), P(None, "xline", "inline", None), P()),
        check_vma=False,
    )
```

```python
import functools

import jax
import jax.numpy as jnp
from jax import lax
from jax.experimental import pallas as pl
from jax.experimental.pallas import tpu as pltpu
from jax.sharding import PartitionSpec as P

H = 32
EPSILON = 1e-06
SATURATION = 0.25
REACH = 2 * H
ALWAYS = 8
SHARED = H // 2
ROWS = 8
PAIR = 2 * ROWS
LIMIT_ROWS = 16
DEVICES = ("inline", "xline")
GROUP = 8
GRANT = 12 << 20
VMEM = pl.BlockSpec(memory_space=pltpu.VMEM)
SMEM = pl.BlockSpec(memory_space=pltpu.SMEM)


def square_weight(offset):
    relative = (offset / H) ** 2
    return relative * relative


def cap_of(mask):
    return jnp.where(mask != 0, SATURATION * SATURATION, 2.0)


def payload_layout(times, lines):
    mask_at = times * lines * REACH
    return mask_at, mask_at + lines * H


def by_parity(even, odd, work):
    here, size = lax.axis_index("inline"), lax.axis_size("inline")
    parity = lax.rem(here, 2)
    below, above = (here > 0).astype(jnp.float32), (here < size - 1).astype(jnp.float32)

    @pl.when(parity == 0)
    def _():
        work(even, False, above)
        work(odd, True, below)

    @pl.when(parity != 0)
    def _():
        work(even, True, below)
        work(odd, False, above)


def edges(value, axis, width):
    depth = value.shape[-1]
    length = value.shape[axis]
    low = lax.slice_in_dim(value, 0, width, axis=axis).reshape(-1, depth)
    return low, lax.slice_in_dim(value, length - width, length, axis=axis).reshape(-1, depth)


def for_even(low, high):
    return jnp.where(lax.axis_index("inline") % 2 == 0, high, low)


def for_odd(low, high):
    return for_even(high, low)


def payloads(rcv, sat, limit):
    depth = rcv.shape[-1]
    rows = edges(rcv, 2, REACH)
    rows = for_even(*rows), for_odd(*rows)
    *rows, sat, limit = lax.optimization_barrier((*rows, sat, limit))
    masks = edges((sat != 0).astype(jnp.bfloat16), 1, H)
    limits = jnp.full((LIMIT_ROWS, depth), limit[0]).astype(jnp.bfloat16)
    even = jnp.concatenate([rows[0], for_even(*masks), limits], axis=0)
    return limit, even, jnp.concatenate([rows[1], for_odd(*masks), limits], axis=0)


def unpack_marks(times, limit, sat, even_in, odd_in, caps, limits):
    lines, cells, depth = sat.shape
    mask_at, limit_at = payload_layout(times, lines)

    def halo(arrived, low, there):
        row_at = 0 if low else H + cells
        for y in range(lines):
            caps[y, pl.ds(row_at, H), :] = cap_of(arrived[pl.ds(mask_at + y * H, H), :].astype(jnp.float32))
        value = arrived[pl.ds(limit_at, LIMIT_ROWS), :].astype(jnp.float32)
        for part in range(H // LIMIT_ROWS):
            limits[pl.ds(row_at + part * LIMIT_ROWS, LIMIT_ROWS), :] = value

    by_parity(even_in, odd_in, halo)
    for y in range(lines):
        caps[y, pl.ds(H, cells), :] = cap_of(sat[y])
    limits[pl.ds(H, cells), :] = jnp.full((cells, depth), limit[0], jnp.int32).astype(jnp.float32)


def unpack_halo(even_in, odd_in, low_out, high_out):
    times, lines, _, depth = low_out.shape
    blank = jnp.zeros((ROWS, depth), jnp.float32)

    def halo(arrived, low, there):
        out, field_at, blank_at = (low_out, 0, REACH) if low else (high_out, ROWS, 0)
        for t in range(times):
            for y in range(lines):
                at = (t * lines + y) * REACH
                out[t, y, pl.ds(field_at, REACH), :] = arrived[pl.ds(at, REACH), :].astype(jnp.float32) * there
                out[t, y, pl.ds(blank_at, ROWS), :] = blank

    by_parity(even_in, odd_in, halo)


def image_of(center, far):
    image = center[0] * far[0]
    for c, f in zip(center[1:], far[1:]):
        image = image + c * f
    return image


def accumulate(center, sums, offsets, far_at, masked, cap_at):
    heavy, plain = sums
    times = range(len(center))
    near = {}
    for offset in offsets:
        far = far_at(offset)
        image = masked(image_of(center, far), offset)
        if abs(offset) <= SHARED:
            terms = [image * f for f in far]
            if abs(offset) in near:
                terms = [a + b for a, b in zip(near.pop(abs(offset)), terms)]
            near[abs(offset)] = terms
            if offset == 0 or -offset not in offsets or offset > 0:
                near.pop(abs(offset))
                plain = [plain[t] + terms[t] for t in times]
                if offset:
                    square = square_weight(offset)
                    heavy = [heavy[t] + terms[t] * square for t in times]
        else:
            square = square_weight(offset)
            weighed = image * jnp.minimum(cap_at(offset), square)
            plain = [plain[t] + image * far[t] for t in times]
            heavy = [heavy[t] + weighed * far[t] for t in times]
    return heavy, plain


def paired(largest, smallest=0):
    return [sign * size for size in range(smallest, largest + 1) for sign in ((-1, 1) if size else (1,))]


def tiles_of(field, y, base):
    times = field.shape[0]
    both = [field[t, y, pl.ds(base, PAIR), :].astype(jnp.float32) for t in range(times)]
    return [[rows[half * ROWS : (half + 1) * ROWS] for rows in both] for half in range(2)]


def inner_kernel(limit, middle, field, sat, heavy_out, plain_out, shifted, caps):
    times, lines, cells, depth = field.shape
    zero = jnp.zeros((ROWS, depth), jnp.float32)
    blank = jnp.zeros((REACH, depth), jnp.float32)
    for t in range(times):
        for y in range(lines):
            shifted[t, y, pl.ds(0, REACH), :] = blank
            shifted[t, y, pl.ds(REACH, cells), :] = field[t, y].astype(jnp.float32)
            shifted[t, y, pl.ds(REACH + cells, REACH), :] = blank
    for y in range(lines):
        caps[y, pl.ds(0, H), :] = blank[:H]
        caps[y, pl.ds(H, cells), :] = cap_of(sat[y])
        caps[y, pl.ds(H + cells, H), :] = blank[:H]
    inside = [(size <= limit[0]).astype(jnp.float32) for size in range(H + 1)]

    def tile(index, carry):
        base = pl.multiple_of(index * PAIR, PAIR)
        for y in range(lines):
            for half, center in enumerate(tiles_of(middle, y, base)):
                at = base + half * ROWS

                def add(offsets, sums):
                    return accumulate(
                        center,
                        sums,
                        offsets,
                        lambda h: [shifted[t, y, pl.ds(at + REACH + 2 * h, ROWS), :] for t in range(times)],
                        lambda image, h: image * inside[abs(h)] if abs(h) > ALWAYS else image,
                        lambda h: caps[y, pl.ds(at + H + h, ROWS), :],
                    )

                sums = add(paired(SHARED), ([zero] * times, [zero] * times))
                for low in range(SHARED + 1, H + 1, GROUP):
                    below = base + PAIR - 1 - 2 * low >= 0
                    above = base + 2 * low < cells
                    for sign, reach in ((-1, below), (1, above)):
                        offsets = [sign * size for size in range(low, min(low + GROUP, H + 1))]
                        needed = jnp.logical_and(reach, limit[0] >= low)
                        sums = lax.cond(needed, functools.partial(add, offsets), lambda kept: kept, sums)
                heavy, plain = sums
                rows = pl.ds(base + half * ROWS, ROWS)
                for t in range(times):
                    heavy_out[t, y, rows, :] = heavy[t]
                    plain_out[t, y, rows, :] = plain[t]
        return carry

    lax.fori_loop(0, heavy_out.shape[2] // PAIR, tile, 0)


def within(limits, at):
    def masked(image, offset):
        if abs(offset) <= ALWAYS:
            return image
        return jnp.where(limits[pl.ds(at + H + offset, ROWS), :] >= float(abs(offset)), image, 0.0)

    return masked


def add_outer(middle, heavy, plain, low, high, caps, limits):
    times, lines, cells, depth = middle.shape
    count = heavy[0].shape[2]
    for group in range(REACH // PAIR):

        def tile(index, carry, group=group):
            for side, shifted in ((0, low), (1, high)):

                @pl.when(index == side)
                def _():
                    first = cells - (group + 1) * PAIR if side else group * PAIR
                    number = first // count
                    base = pl.multiple_of(first - number * count + (index - side) * PAIR, PAIR)
                    origin = ROWS - cells if side else REACH
                    for y in range(lines):
                        for half, center in enumerate(tiles_of(middle, y, number * count + base)):
                            rows = pl.ds(base + half * ROWS, ROWS)
                            at = number * count + base + half * ROWS
                            rank = 2 * group + (1 - half if side else half)
                            sizes = range(ROWS // 2 * rank + 1, H + 1)
                            new_heavy, new_plain = accumulate(
                                center,
                                (
                                    [heavy[number][t, y, rows, :] for t in range(times)],
                                    [plain[number][t, y, rows, :] for t in range(times)],
                                ),
                                [size if side else -size for size in sizes],
                                lambda h: [shifted[t, y, pl.ds(at + origin + 2 * h, ROWS), :] for t in range(times)],
                                within(limits, at),
                                lambda h: caps[y, pl.ds(at + H + h, ROWS), :],
                            )
                            for t in range(times):
                                heavy[number][t, y, rows, :] = new_heavy[t]
                                plain[number][t, y, rows, :] = new_plain[t]

            return carry

        lax.fori_loop(0, 2, tile, 0)


def src_outer_kernel(limit, src, sat, even_in, odd_in, heavy_in, plain_in, heavy, plain, sums, low, high, caps, limits):
    times, lines, cells, depth = src.shape
    unpack_marks(times, limit, sat, even_in, odd_in, caps, limits)
    unpack_halo(even_in, odd_in, low, high)
    add_outer(src, [heavy], [plain], low, high, caps, limits)
    zero = jnp.zeros((ROWS, depth), jnp.float32)

    def add(index, totals):
        energy, weighted = totals
        base = pl.multiple_of(index * PAIR, PAIR)
        for y in range(lines):
            for half, center in enumerate(tiles_of(src, y, base)):
                rows = pl.ds(base + half * ROWS, ROWS)
                energy = energy + image_of(center, [plain[t, y, rows, :] for t in range(times)])
                weighted = weighted + image_of(center, [heavy[t, y, rows, :] for t in range(times)])
        return energy, weighted

    energy, weighted = lax.fori_loop(0, cells // PAIR, add, (zero, zero))
    sums[...] = jnp.broadcast_to(
        jnp.concatenate([jnp.sum(part, axis=0, keepdims=True) for part in (energy, weighted)], axis=0)[None], sums.shape
    )


def rcv_outer_kernel(limit, rcv, sat, even_marks, odd_marks, even_in, odd_in, *refs):
    parts, (low, high, caps, limits) = refs[len(refs) // 2 - 2 : -4], refs[-4:]
    unpack_marks(rcv.shape[0], limit, sat, even_marks, odd_marks, caps, limits)
    unpack_halo(even_in, odd_in, low, high)
    add_outer(rcv, parts[::2], parts[1::2], low, high, caps, limits)


def combine_kernel(cell_count, sums, src_heavy, src_plain, *refs):
    pieces, (src_out, rcv_out, semblance_out) = refs[:-3], refs[-3:]
    total = jnp.sum(sums[...], axis=0)
    total = jnp.broadcast_to(jnp.sum(total, axis=1, keepdims=True), total.shape)
    energy, weighted = total[0:1], total[1:2]
    semblance = weighted / energy
    inverse_rms = 1.0 / jnp.sqrt(energy / cell_count + EPSILON)
    semblance_out[...] = semblance

    def put(out, start, heavy, plain):
        times, lines, count, _ = heavy.shape
        for t in range(times):
            for y in range(lines):
                value = inverse_rms * (heavy[t, y] - semblance * plain[t, y])
                out[t, y, pl.ds(start, count), :] = value.astype(jnp.bfloat16)

    put(src_out, 0, src_heavy, src_plain)
    start = 0
    for heavy, plain in zip(pieces[::2], pieces[1::2]):
        put(rcv_out, start, heavy, plain)
        start += heavy.shape[2]


def exchanges(size, lines):
    assert size % 2 == 0 and lines % 2 == 0
    even = [(i, i + 1) for i in range(0, size, 2)]
    odd = [(i, i + 1) for i in range(1, size - 1, 2)]
    routes = []
    for pairs in (even, odd):
        partner = dict(pairs + [(j, i) for i, j in pairs])
        routes.append(
            [
                (i * lines + line, partner[i] * lines + line if i in partner else i * lines + (line ^ 1))
                for i in range(size)
                for line in range(lines)
            ]
        )
    return routes


def local(source_field, receiver_field, sat_mask, offset_range):
    times, lines, cells, depth = source_field.shape
    size = lax.axis_size("inline")
    grant = pltpu.CompilerParams(vmem_limit_bytes=GRANT)
    image_cells = lines * cells * depth * (2 * H + 1)
    shape = jax.ShapeDtypeStruct
    total = shape((times, lines, cells, depth), jnp.float32)
    field_out = shape(source_field.shape, jnp.bfloat16)
    extended = pltpu.VMEM((times, lines, cells + 2 * REACH, depth), jnp.float32)
    edge = pltpu.VMEM((times, lines, ROWS + REACH, depth), jnp.float32)
    caps = pltpu.VMEM((lines, cells + 2 * H, depth), jnp.float32)
    limits = pltpu.VMEM((cells + 2 * H, depth), jnp.float32)

    def call(kernel, name, out_shape, operands, scratch=(), share=0.0, aliases={}):
        return pl.pallas_call(
            kernel,
            out_shape=out_shape,
            in_specs=[SMEM if operand is offset_range else VMEM for operand in operands],
            out_specs=jax.tree.map(lambda _: VMEM, out_shape),
            scratch_shapes=scratch,
            input_output_aliases=aliases,
            cost_estimate=pl.CostEstimate(
                flops=int(24 * image_cells * share), bytes_accessed=1 << 20, transcendentals=0
            ),
            compiler_params=grant,
            name=name,
        )(*operands)

    src, rcv, sat = source_field, receiver_field, sat_mask
    offset_range, even, odd = payloads(rcv, sat, offset_range)
    even_route, odd_route = exchanges(size, lax.axis_size("xline"))
    even = lax.ppermute(even, DEVICES, even_route)
    odd = lax.ppermute(odd, DEVICES, odd_route)
    heavy, plain = call(
        inner_kernel,
        "src_inner",
        (total, total),
        (offset_range, src, rcv, sat),
        [extended, caps],
        0.85,
    )
    (heavy, plain), ahead = lax.optimization_barrier(((heavy, plain), src))
    low_high = edges(ahead, 2, REACH)
    odd_late = lax.ppermute(for_odd(*low_high), DEVICES, odd_route)
    even_late = lax.ppermute(for_even(*low_high), DEVICES, even_route)
    count = size * lax.axis_size("xline")
    heavy, plain, sums = call(
        src_outer_kernel,
        "src_outer",
        (total, total, shape((count, 2, depth), jnp.float32)),
        (offset_range, src, sat, even, odd, heavy, plain),
        [edge, edge, caps, limits],
        0.25,
        {5: 0, 6: 1},
    )

    def finish(odd_late, even_late, *pieces):
        return call(
            rcv_outer_kernel,
            "rcv_outer",
            [piece] * len(pieces),
            (offset_range, rcv, sat, even, odd, even_late, odd_late, *pieces),
            [edge, edge, caps, limits],
            0.25,
            {7 + i: i for i in range(len(pieces))},
        )

    gathered = lax.all_to_all(sums, DEVICES, 0, 0, tiled=True)
    sums, ahead, odd_late, even_late = lax.optimization_barrier((sums, src, odd_late, even_late))
    pieces = call(
        inner_kernel,
        "rcv_inner",
        (total, total),
        (offset_range, rcv, ahead, sat),
        [extended, caps],
        0.85,
    )
    pieces = call(
        rcv_outer_kernel,
        "rcv_outer",
        (total, total),
        (offset_range, rcv, sat, even, odd, even_late, odd_late, *pieces),
        [edge, edge, caps, limits],
        0.25,
        {7: 0, 8: 1},
    )

    cell_count = float(lines * lax.axis_size("xline") * cells * size * depth * (2 * H + 1))
    src_adj, rcv_adj, semblance = call(
        functools.partial(combine_kernel, cell_count),
        "combine",
        (field_out, field_out, shape((1, depth), jnp.float32)),
        (gathered, heavy, plain, *pieces),
    )
    return src_adj, rcv_adj, semblance[0, 0]


def solution(mesh):
    return jax.shard_map(
        local,
        mesh=mesh,
        in_specs=(
            P(None, "xline", "inline", None),
            P(None, "xline", "inline", None),
            P("xline", "inline", None),
            P("inline"),
        ),
        out_specs=(P(None, "xline", "inline", None), P(None, "xline", "inline", None), P()),
        check_vma=False,
    )
```

```python
import functools

import jax
import jax.numpy as jnp
from jax import lax
from jax.experimental import pallas as pl
from jax.experimental.pallas import tpu as pltpu
from jax.sharding import PartitionSpec as P

H = 32
EPSILON = 1e-06
SATURATION = 0.25
REACH = 2 * H
ALWAYS = 8
SHARED = H // 2
ROWS = 8
PAIR = 2 * ROWS
LIMIT_ROWS = 16
DEVICES = ("inline", "xline")
GROUP = 8
GRANT = 12 << 20
VMEM = pl.BlockSpec(memory_space=pltpu.VMEM)
SMEM = pl.BlockSpec(memory_space=pltpu.SMEM)


def square_weight(offset):
    relative = (offset / H) ** 2
    return relative * relative


def cap_of(mask):
    return jnp.where(mask != 0, SATURATION * SATURATION, 2.0)


def payload_layout(times, lines):
    mask_at = times * lines * REACH
    limit_at = mask_at + lines * H
    return mask_at, limit_at, limit_at + LIMIT_ROWS


def by_parity(even, odd, work):
    here, size = lax.axis_index("inline"), lax.axis_size("inline")
    parity = lax.rem(here, 2)
    below, above = (here > 0).astype(jnp.float32), (here < size - 1).astype(jnp.float32)

    @pl.when(parity == 0)
    def _():
        work(even, False, above)
        work(odd, True, below)

    @pl.when(parity != 0)
    def _():
        work(even, True, below)
        work(odd, False, above)


def edges(value, axis, width):
    depth = value.shape[-1]
    length = value.shape[axis]
    low = lax.slice_in_dim(value, 0, width, axis=axis).reshape(-1, depth)
    return low, lax.slice_in_dim(value, length - width, length, axis=axis).reshape(-1, depth)


def for_even(low, high):
    return jnp.where(lax.axis_index("inline") % 2 == 0, high, low)


def for_odd(low, high):
    return for_even(high, low)


def payloads(src, rcv, sat, limit):
    depth = rcv.shape[-1]
    rows = edges(rcv, 2, REACH)
    rows = for_even(*rows), for_odd(*rows)
    *rows, sat, src, limit = lax.optimization_barrier((*rows, sat, src, limit))
    masks = edges((sat != 0).astype(jnp.bfloat16), 1, H)
    limits = jnp.full((LIMIT_ROWS, depth), limit[0]).astype(jnp.bfloat16)
    odd = jnp.concatenate([rows[1], for_odd(*masks), limits], axis=0)
    return limit, jnp.concatenate([rows[0], for_even(*masks), limits, for_even(*edges(src, 2, REACH))], axis=0), odd


def unpack_marks(times, limit, sat, even_in, odd_in, caps, limits):
    lines, cells, depth = sat.shape
    mask_at, limit_at, _ = payload_layout(times, lines)

    def halo(arrived, low, there):
        row_at = 0 if low else H + cells
        for y in range(lines):
            caps[y, pl.ds(row_at, H), :] = cap_of(arrived[pl.ds(mask_at + y * H, H), :].astype(jnp.float32))
        value = arrived[pl.ds(limit_at, LIMIT_ROWS), :].astype(jnp.float32)
        for part in range(H // LIMIT_ROWS):
            limits[pl.ds(row_at + part * LIMIT_ROWS, LIMIT_ROWS), :] = value

    by_parity(even_in, odd_in, halo)
    for y in range(lines):
        caps[y, pl.ds(H, cells), :] = cap_of(sat[y])
    limits[pl.ds(H, cells), :] = jnp.full((cells, depth), limit[0], jnp.int32).astype(jnp.float32)


def unpack_halo(even_in, even_at, odd_in, odd_at, low_out, high_out):
    times, lines, _, depth = low_out.shape
    blank = jnp.zeros((ROWS, depth), jnp.float32)

    def halo(arrived, low, there):
        out, field_at, blank_at = (low_out, 0, REACH) if low else (high_out, ROWS, 0)
        start = even_at if arrived is even_in else odd_at
        for t in range(times):
            for y in range(lines):
                at = start + (t * lines + y) * REACH
                out[t, y, pl.ds(field_at, REACH), :] = arrived[pl.ds(at, REACH), :].astype(jnp.float32) * there
                out[t, y, pl.ds(blank_at, ROWS), :] = blank

    by_parity(even_in, odd_in, halo)


def image_of(center, far):
    image = center[0] * far[0]
    for c, f in zip(center[1:], far[1:]):
        image = image + c * f
    return image


def accumulate(center, sums, offsets, far_at, masked, cap_at):
    heavy, plain = sums
    times = range(len(center))
    near = {}
    for offset in offsets:
        far = far_at(offset)
        image = masked(image_of(center, far), offset)
        if abs(offset) <= SHARED:
            terms = [image * f for f in far]
            if abs(offset) in near:
                terms = [a + b for a, b in zip(near.pop(abs(offset)), terms)]
            near[abs(offset)] = terms
            if offset == 0 or -offset not in offsets or offset > 0:
                near.pop(abs(offset))
                plain = [plain[t] + terms[t] for t in times]
                if offset:
                    square = square_weight(offset)
                    heavy = [heavy[t] + terms[t] * square for t in times]
        else:
            square = square_weight(offset)
            weighed = image * jnp.minimum(cap_at(offset), square)
            plain = [plain[t] + image * far[t] for t in times]
            heavy = [heavy[t] + weighed * far[t] for t in times]
    return heavy, plain


def paired(largest, smallest=0):
    return [sign * size for size in range(smallest, largest + 1) for sign in ((-1, 1) if size else (1,))]


def tiles_of(field, y, base):
    times = field.shape[0]
    both = [field[t, y, pl.ds(base, PAIR), :].astype(jnp.float32) for t in range(times)]
    return [[rows[half * ROWS : (half + 1) * ROWS] for rows in both] for half in range(2)]


def inner_kernel(limit, middle, field, sat, heavy_out, plain_out, shifted, caps):
    times, lines, cells, depth = field.shape
    zero = jnp.zeros((ROWS, depth), jnp.float32)
    blank = jnp.zeros((REACH, depth), jnp.float32)
    for t in range(times):
        for y in range(lines):
            shifted[t, y, pl.ds(0, REACH), :] = blank
            shifted[t, y, pl.ds(REACH, cells), :] = field[t, y].astype(jnp.float32)
            shifted[t, y, pl.ds(REACH + cells, REACH), :] = blank
    for y in range(lines):
        caps[y, pl.ds(0, H), :] = blank[:H]
        caps[y, pl.ds(H, cells), :] = cap_of(sat[y])
        caps[y, pl.ds(H + cells, H), :] = blank[:H]
    inside = [(size <= limit[0]).astype(jnp.float32) for size in range(H + 1)]

    def tile(index, carry):
        base = pl.multiple_of(index * PAIR, PAIR)
        for y in range(lines):
            for half, center in enumerate(tiles_of(middle, y, base)):
                at = base + half * ROWS

                def add(offsets, sums):
                    return accumulate(
                        center,
                        sums,
                        offsets,
                        lambda h: [shifted[t, y, pl.ds(at + REACH + 2 * h, ROWS), :] for t in range(times)],
                        lambda image, h: image * inside[abs(h)] if abs(h) > ALWAYS else image,
                        lambda h: caps[y, pl.ds(at + H + h, ROWS), :],
                    )

                sums = add(paired(SHARED), ([zero] * times, [zero] * times))
                for low in range(SHARED + 1, H + 1, GROUP):
                    below = base + PAIR - 1 - 2 * low >= 0
                    above = base + 2 * low < cells
                    for sign, reach in ((-1, below), (1, above)):
                        offsets = [sign * size for size in range(low, min(low + GROUP, H + 1))]
                        needed = jnp.logical_and(reach, limit[0] >= low)
                        sums = lax.cond(needed, functools.partial(add, offsets), lambda kept: kept, sums)
                heavy, plain = sums
                rows = pl.ds(base + half * ROWS, ROWS)
                for t in range(times):
                    heavy_out[t, y, rows, :] = heavy[t]
                    plain_out[t, y, rows, :] = plain[t]
        return carry

    lax.fori_loop(0, heavy_out.shape[2] // PAIR, tile, 0)


def within(limits, at):
    def masked(image, offset):
        if abs(offset) <= ALWAYS:
            return image
        return jnp.where(limits[pl.ds(at + H + offset, ROWS), :] >= float(abs(offset)), image, 0.0)

    return masked


def add_outer(middle, heavy, plain, low, high, caps, limits):
    times, lines, cells, depth = middle.shape
    count = heavy[0].shape[2]
    for group in range(REACH // PAIR):

        def tile(index, carry, group=group):
            for side, shifted in ((0, low), (1, high)):

                @pl.when(index == side)
                def _():
                    first = cells - (group + 1) * PAIR if side else group * PAIR
                    number = first // count
                    base = pl.multiple_of(first - number * count + (index - side) * PAIR, PAIR)
                    origin = ROWS - cells if side else REACH
                    for y in range(lines):
                        for half, center in enumerate(tiles_of(middle, y, number * count + base)):
                            rows = pl.ds(base + half * ROWS, ROWS)
                            at = number * count + base + half * ROWS
                            rank = 2 * group + (1 - half if side else half)
                            sizes = range(ROWS // 2 * rank + 1, H + 1)
                            new_heavy, new_plain = accumulate(
                                center,
                                (
                                    [heavy[number][t, y, rows, :] for t in range(times)],
                                    [plain[number][t, y, rows, :] for t in range(times)],
                                ),
                                [size if side else -size for size in sizes],
                                lambda h: [shifted[t, y, pl.ds(at + origin + 2 * h, ROWS), :] for t in range(times)],
                                within(limits, at),
                                lambda h: caps[y, pl.ds(at + H + h, ROWS), :],
                            )
                            for t in range(times):
                                heavy[number][t, y, rows, :] = new_heavy[t]
                                plain[number][t, y, rows, :] = new_plain[t]

            return carry

        lax.fori_loop(0, 2, tile, 0)


def src_outer_kernel(limit, src, sat, even_in, odd_in, heavy_in, plain_in, heavy, plain, sums, low, high, caps, limits):
    times, lines, cells, depth = src.shape
    unpack_marks(times, limit, sat, even_in, odd_in, caps, limits)
    unpack_halo(even_in, 0, odd_in, 0, low, high)
    add_outer(src, [heavy], [plain], low, high, caps, limits)
    zero = jnp.zeros((ROWS, depth), jnp.float32)

    def add(index, totals):
        energy, weighted = totals
        base = pl.multiple_of(index * PAIR, PAIR)
        for y in range(lines):
            for half, center in enumerate(tiles_of(src, y, base)):
                rows = pl.ds(base + half * ROWS, ROWS)
                energy = energy + image_of(center, [plain[t, y, rows, :] for t in range(times)])
                weighted = weighted + image_of(center, [heavy[t, y, rows, :] for t in range(times)])
        return energy, weighted

    energy, weighted = lax.fori_loop(0, cells // PAIR, add, (zero, zero))
    sums[...] = jnp.broadcast_to(
        jnp.concatenate([jnp.sum(part, axis=0, keepdims=True) for part in (energy, weighted)], axis=0)[None], sums.shape
    )


def rcv_outer_kernel(limit, rcv, sat, even_in, odd_marks, odd_in, *refs):
    parts, (low, high, caps, limits) = refs[len(refs) // 2 - 2 : -4], refs[-4:]
    unpack_marks(rcv.shape[0], limit, sat, even_in, odd_marks, caps, limits)
    unpack_halo(even_in, payload_layout(*rcv.shape[:2])[2], odd_in, 0, low, high)
    add_outer(rcv, parts[::2], parts[1::2], low, high, caps, limits)


def combine_kernel(cell_count, sums, src_heavy, src_plain, *refs):
    pieces, (src_out, rcv_out, semblance_out) = refs[:-3], refs[-3:]
    total = jnp.sum(sums[...], axis=0)
    total = jnp.broadcast_to(jnp.sum(total, axis=1, keepdims=True), total.shape)
    energy, weighted = total[0:1], total[1:2]
    semblance = weighted / energy
    inverse_rms = 1.0 / jnp.sqrt(energy / cell_count + EPSILON)
    semblance_out[...] = semblance

    def put(out, start, heavy, plain):
        times, lines, count, _ = heavy.shape
        for t in range(times):
            for y in range(lines):
                value = inverse_rms * (heavy[t, y] - semblance * plain[t, y])
                out[t, y, pl.ds(start, count), :] = value.astype(jnp.bfloat16)

    put(src_out, 0, src_heavy, src_plain)
    start = 0
    for heavy, plain in zip(pieces[::2], pieces[1::2]):
        put(rcv_out, start, heavy, plain)
        start += heavy.shape[2]


def exchanges(size, lines):
    assert size % 2 == 0 and lines % 2 == 0
    even = [(i, i + 1) for i in range(0, size, 2)]
    odd = [(i, i + 1) for i in range(1, size - 1, 2)]
    routes = []
    for pairs in (even, odd):
        partner = dict(pairs + [(j, i) for i, j in pairs])
        routes.append(
            [
                (i * lines + line, partner[i] * lines + line if i in partner else i * lines + (line ^ 1))
                for i in range(size)
                for line in range(lines)
            ]
        )
    return routes


def local(source_field, receiver_field, sat_mask, offset_range):
    times, lines, cells, depth = source_field.shape
    size = lax.axis_size("inline")
    grant = pltpu.CompilerParams(vmem_limit_bytes=GRANT)
    image_cells = lines * cells * depth * (2 * H + 1)
    shape = jax.ShapeDtypeStruct
    total = shape((times, lines, cells, depth), jnp.float32)
    field_out = shape(source_field.shape, jnp.bfloat16)
    extended = pltpu.VMEM((times, lines, cells + 2 * REACH, depth), jnp.float32)
    edge = pltpu.VMEM((times, lines, ROWS + REACH, depth), jnp.float32)
    caps = pltpu.VMEM((lines, cells + 2 * H, depth), jnp.float32)
    limits = pltpu.VMEM((cells + 2 * H, depth), jnp.float32)

    def call(kernel, name, out_shape, operands, scratch=(), share=0.0, aliases={}):
        return pl.pallas_call(
            kernel,
            out_shape=out_shape,
            in_specs=[SMEM if operand is offset_range else VMEM for operand in operands],
            out_specs=jax.tree.map(lambda _: VMEM, out_shape),
            scratch_shapes=scratch,
            input_output_aliases=aliases,
            cost_estimate=pl.CostEstimate(
                flops=int(24 * image_cells * share), bytes_accessed=1 << 20, transcendentals=0
            ),
            compiler_params=grant,
            name=name,
        )(*operands)

    src, rcv, sat = source_field, receiver_field, sat_mask
    offset_range, even, odd = payloads(src, rcv, sat, offset_range)
    even_route, odd_route = exchanges(size, lax.axis_size("xline"))
    even = lax.ppermute(even, DEVICES, even_route)
    odd = lax.ppermute(odd, DEVICES, odd_route)
    heavy, plain = call(
        inner_kernel,
        "src_inner",
        (total, total),
        (offset_range, src, rcv, sat),
        [extended, caps],
        0.85,
    )
    (heavy, plain), ahead = lax.optimization_barrier(((heavy, plain), src))
    odd_late = lax.ppermute(for_odd(*edges(ahead, 2, REACH)), DEVICES, odd_route)
    count = size * lax.axis_size("xline")
    heavy, plain, sums = call(
        src_outer_kernel,
        "src_outer",
        (total, total, shape((count, 2, depth), jnp.float32)),
        (offset_range, src, sat, even, odd, heavy, plain),
        [edge, edge, caps, limits],
        0.25,
        {5: 0, 6: 1},
    )

    def finish(odd_late, even_late, *pieces):
        return call(
            rcv_outer_kernel,
            "rcv_outer",
            [piece] * len(pieces),
            (offset_range, rcv, sat, even, odd, odd_late, *pieces),
            [edge, edge, caps, limits],
            0.25,
            {7 + i: i for i in range(len(pieces))},
        )

    gathered = lax.all_to_all(sums, DEVICES, 0, 0, tiled=True)
    sums, ahead, odd_late = lax.optimization_barrier((sums, src, odd_late))
    pieces = call(
        inner_kernel,
        "rcv_inner",
        (total, total),
        (offset_range, rcv, ahead, sat),
        [extended, caps],
        0.85,
    )
    pieces = call(
        rcv_outer_kernel,
        "rcv_outer",
        (total, total),
        (offset_range, rcv, sat, even, odd, odd_late, *pieces),
        [edge, edge, caps, limits],
        0.25,
        {6: 0, 7: 1},
    )

    cell_count = float(lines * lax.axis_size("xline") * cells * size * depth * (2 * H + 1))
    src_adj, rcv_adj, semblance = call(
        functools.partial(combine_kernel, cell_count),
        "combine",
        (field_out, field_out, shape((1, depth), jnp.float32)),
        (gathered, heavy, plain, *pieces),
    )
    return src_adj, rcv_adj, semblance[0, 0]


def solution(mesh):
    return jax.shard_map(
        local,
        mesh=mesh,
        in_specs=(
            P(None, "xline", "inline", None),
            P(None, "xline", "inline", None),
            P("xline", "inline", None),
            P("inline"),
        ),
        out_specs=(P(None, "xline", "inline", None), P(None, "xline", "inline", None), P()),
        check_vma=False,
    )
```

```python
import functools

import jax
import jax.numpy as jnp
from jax import lax
from jax.experimental import pallas as pl
from jax.experimental.pallas import tpu as pltpu
from jax.sharding import PartitionSpec as P

H = 32
EPSILON = 1e-06
SATURATION = 0.25
REACH = 2 * H
ALWAYS = 8
SHARED = H // 2
ROWS = 8
PAIR = 2 * ROWS
LIMIT_ROWS = 16
DEVICES = ("inline", "xline")
GROUP = 8
GRANT = 12 << 20
VMEM = pl.BlockSpec(memory_space=pltpu.VMEM)
SMEM = pl.BlockSpec(memory_space=pltpu.SMEM)


def square_weight(offset):
    relative = (offset / H) ** 2
    return relative * relative


def cap_of(mask):
    return jnp.where(mask != 0, SATURATION * SATURATION, 2.0)


def payload_layout(times, lines):
    mask_at = times * lines * REACH
    return mask_at, mask_at + lines * H


def by_parity(even, odd, work):
    here, size = lax.axis_index("inline"), lax.axis_size("inline")
    parity = lax.rem(here, 2)
    below, above = (here > 0).astype(jnp.float32), (here < size - 1).astype(jnp.float32)

    @pl.when(parity == 0)
    def _():
        work(even, False, above)
        work(odd, True, below)

    @pl.when(parity != 0)
    def _():
        work(even, True, below)
        work(odd, False, above)


def edges(value, axis, width):
    depth = value.shape[-1]
    length = value.shape[axis]
    low = lax.slice_in_dim(value, 0, width, axis=axis).reshape(-1, depth)
    return low, lax.slice_in_dim(value, length - width, length, axis=axis).reshape(-1, depth)


def for_even(low, high):
    return jnp.where(lax.axis_index("inline") % 2 == 0, high, low)


def for_odd(low, high):
    return for_even(high, low)


def payloads(rcv, sat, limit):
    depth = rcv.shape[-1]
    rows = edges(rcv, 2, REACH)
    rows = for_even(*rows), for_odd(*rows)
    *rows, sat = lax.optimization_barrier((*rows, sat))
    masks = edges((sat != 0).astype(jnp.bfloat16), 1, H)
    limits = jnp.full((LIMIT_ROWS, depth), limit[0]).astype(jnp.bfloat16)
    return [
        jnp.concatenate([part, choose(*masks), limits], axis=0) for part, choose in zip(rows, (for_even, for_odd))
    ]


def unpack_marks(times, limit, sat, even_in, odd_in, caps, limits):
    lines, cells, depth = sat.shape
    mask_at, limit_at = payload_layout(times, lines)

    def halo(arrived, low, there):
        row_at = 0 if low else H + cells
        for y in range(lines):
            caps[y, pl.ds(row_at, H), :] = cap_of(arrived[pl.ds(mask_at + y * H, H), :].astype(jnp.float32))
        value = arrived[pl.ds(limit_at, LIMIT_ROWS), :].astype(jnp.float32)
        for part in range(H // LIMIT_ROWS):
            limits[pl.ds(row_at + part * LIMIT_ROWS, LIMIT_ROWS), :] = value

    by_parity(even_in, odd_in, halo)
    for y in range(lines):
        caps[y, pl.ds(H, cells), :] = cap_of(sat[y])
    limits[pl.ds(H, cells), :] = jnp.full((cells, depth), limit[0], jnp.int32).astype(jnp.float32)


def unpack_halo(even_in, odd_in, low_out, high_out):
    times, lines, _, depth = low_out.shape
    blank = jnp.zeros((ROWS, depth), jnp.float32)

    def halo(arrived, low, there):
        out, field_at, blank_at = (low_out, 0, REACH) if low else (high_out, ROWS, 0)
        for t in range(times):
            for y in range(lines):
                at = (t * lines + y) * REACH
                out[t, y, pl.ds(field_at, REACH), :] = arrived[pl.ds(at, REACH), :].astype(jnp.float32) * there
                out[t, y, pl.ds(blank_at, ROWS), :] = blank

    by_parity(even_in, odd_in, halo)


def image_of(center, far):
    image = center[0] * far[0]
    for c, f in zip(center[1:], far[1:]):
        image = image + c * f
    return image


def accumulate(center, sums, offsets, far_at, masked, cap_at):
    heavy, plain = sums
    times = range(len(center))
    near = {}
    for offset in offsets:
        far = far_at(offset)
        image = masked(image_of(center, far), offset)
        if abs(offset) <= SHARED:
            terms = [image * f for f in far]
            if abs(offset) in near:
                terms = [a + b for a, b in zip(near.pop(abs(offset)), terms)]
            near[abs(offset)] = terms
            if offset == 0 or -offset not in offsets or offset > 0:
                near.pop(abs(offset))
                plain = [plain[t] + terms[t] for t in times]
                if offset:
                    square = square_weight(offset)
                    heavy = [heavy[t] + terms[t] * square for t in times]
        else:
            square = square_weight(offset)
            weighed = image * jnp.minimum(cap_at(offset), square)
            plain = [plain[t] + image * far[t] for t in times]
            heavy = [heavy[t] + weighed * far[t] for t in times]
    return heavy, plain


def paired(largest, smallest=0):
    return [sign * size for size in range(smallest, largest + 1) for sign in ((-1, 1) if size else (1,))]


def tiles_of(field, y, base):
    times = field.shape[0]
    both = [field[t, y, pl.ds(base, PAIR), :].astype(jnp.float32) for t in range(times)]
    return [[rows[half * ROWS : (half + 1) * ROWS] for rows in both] for half in range(2)]


def inner_kernel(limit, middle, field, sat, heavy_out, plain_out, *refs):
    *sums_out, shifted, caps = refs
    times, lines, cells, depth = field.shape
    zero = jnp.zeros((ROWS, depth), jnp.float32)
    blank = jnp.zeros((REACH, depth), jnp.float32)
    for t in range(times):
        for y in range(lines):
            shifted[t, y, pl.ds(0, REACH), :] = blank
            shifted[t, y, pl.ds(REACH, cells), :] = field[t, y].astype(jnp.float32)
            shifted[t, y, pl.ds(REACH + cells, REACH), :] = blank
    for y in range(lines):
        caps[y, pl.ds(0, H), :] = blank[:H]
        caps[y, pl.ds(H, cells), :] = cap_of(sat[y])
        caps[y, pl.ds(H + cells, H), :] = blank[:H]
    inside = [(size <= limit[0]).astype(jnp.float32) for size in range(H + 1)]

    def tile(index, totals):
        base = pl.multiple_of(index * PAIR, PAIR)
        for y in range(lines):
            for half, center in enumerate(tiles_of(middle, y, base)):
                at = base + half * ROWS

                def add(offsets, sums):
                    return accumulate(
                        center,
                        sums,
                        offsets,
                        lambda h: [shifted[t, y, pl.ds(at + REACH + 2 * h, ROWS), :] for t in range(times)],
                        lambda image, h: image * inside[abs(h)] if abs(h) > ALWAYS else image,
                        lambda h: caps[y, pl.ds(at + H + h, ROWS), :],
                    )

                sums = add(paired(SHARED), ([zero] * times, [zero] * times))
                for low in range(SHARED + 1, H + 1, GROUP):
                    below = base + PAIR - 1 - 2 * low >= 0
                    above = base + 2 * low < cells
                    for sign, reach in ((-1, below), (1, above)):
                        offsets = [sign * size for size in range(low, min(low + GROUP, H + 1))]
                        needed = jnp.logical_and(reach, limit[0] >= low)
                        sums = lax.cond(needed, functools.partial(add, offsets), lambda kept: kept, sums)
                heavy, plain = sums
                rows = pl.ds(base + half * ROWS, ROWS)
                for t in range(times):
                    heavy_out[t, y, rows, :] = heavy[t]
                    plain_out[t, y, rows, :] = plain[t]
                if sums_out:
                    totals = totals[0] + image_of(center, plain), totals[1] + image_of(center, heavy)
        return totals

    totals = lax.fori_loop(0, cells // PAIR, tile, (zero, zero) if sums_out else 0)
    if sums_out:
        sums_out[0][...] = jnp.concatenate(totals, axis=0)


def within(limits, at):
    def masked(image, offset):
        if abs(offset) <= ALWAYS:
            return image
        return jnp.where(limits[pl.ds(at + H + offset, ROWS), :] >= float(abs(offset)), image, 0.0)

    return masked


def each_outer_tile(middle, low, high, visit):
    times, lines, cells, depth = middle.shape

    for group in range(REACH // PAIR):

        def tile(index, carry, group=group):
            for side, shifted in ((0, low), (1, high)):

                @pl.when(index == side)
                def _():
                    first = cells - (group + 1) * PAIR if side else group * PAIR
                    base = pl.multiple_of(first + (index - side) * PAIR, PAIR)
                    origin = ROWS - cells if side else REACH
                    for y in range(lines):
                        for half, center in enumerate(tiles_of(middle, y, base)):
                            at = base + half * ROWS
                            rank = 2 * group + (1 - half if side else half)
                            sizes = range(ROWS // 2 * rank + 1, H + 1)
                            visit(
                                y,
                                at,
                                center,
                                [size if side else -size for size in sizes],
                                lambda h: [shifted[t, y, pl.ds(at + origin + 2 * h, ROWS), :] for t in range(times)],
                            )

            return carry

        lax.fori_loop(0, 2, tile, 0)


def energy_kernel(limit, src, sat, even_in, odd_in, inner, sums, total, low, high, caps, limits):
    times, lines, cells, depth = src.shape
    unpack_marks(times, limit, sat, even_in, odd_in, caps, limits)
    unpack_halo(even_in, odd_in, low, high)
    total[...] = inner[...]

    def visit(y, at, center, offsets, far_at):
        energy, weighted = total[:ROWS, :], total[ROWS:, :]
        masked = within(limits, at)
        for offset in offsets:
            image = masked(image_of(center, far_at(offset)), offset)
            power = image * image
            energy = energy + power
            square = square_weight(offset)
            if abs(offset) > SHARED:
                square = jnp.minimum(caps[y, pl.ds(at + H + offset, ROWS), :], square)
            weighted = weighted + power * square
        total[:ROWS, :] = energy
        total[ROWS:, :] = weighted

    each_outer_tile(src, low, high, visit)
    rows = [jnp.sum(total[pl.ds(part * ROWS, ROWS), :], axis=0, keepdims=True) for part in range(2)]
    sums[...] = jnp.broadcast_to(jnp.concatenate(rows, axis=0)[None], sums.shape)


def outer_kernel(limit, middle, sat, even_marks, odd_marks, even_in, odd_in, heavy_in, plain_in, heavy, plain, *scratch):
    low, high, caps, limits = scratch
    times, lines, cells, depth = middle.shape
    unpack_marks(times, limit, sat, even_marks, odd_marks, caps, limits)
    unpack_halo(even_in, odd_in, low, high)

    def visit(y, at, center, offsets, far_at):
        rows = pl.ds(at, ROWS)
        sums = [heavy[t, y, rows, :] for t in range(times)], [plain[t, y, rows, :] for t in range(times)]
        new_heavy, new_plain = accumulate(
            center, sums, offsets, far_at, within(limits, at), lambda h: caps[y, pl.ds(at + H + h, ROWS), :]
        )
        for t in range(times):
            heavy[t, y, rows, :] = new_heavy[t]
            plain[t, y, rows, :] = new_plain[t]

    each_outer_tile(middle, low, high, visit)


def combine_kernel(cell_count, sums, src_heavy, src_plain, *refs):
    pieces, (src_out, rcv_out, semblance_out) = refs[:-3], refs[-3:]
    total = jnp.sum(sums[...], axis=0)
    total = jnp.broadcast_to(jnp.sum(total, axis=1, keepdims=True), total.shape)
    energy, weighted = total[0:1], total[1:2]
    semblance = weighted / energy
    inverse_rms = 1.0 / jnp.sqrt(energy / cell_count + EPSILON)
    semblance_out[...] = semblance

    def put(out, start, heavy, plain):
        times, lines, count, _ = heavy.shape
        for t in range(times):
            for y in range(lines):
                value = inverse_rms * (heavy[t, y] - semblance * plain[t, y])
                out[t, y, pl.ds(start, count), :] = value.astype(jnp.bfloat16)

    put(src_out, 0, src_heavy, src_plain)
    start = 0
    for heavy, plain in zip(pieces[::2], pieces[1::2]):
        put(rcv_out, start, heavy, plain)
        start += heavy.shape[2]


def exchanges(size, lines):
    assert size % 2 == 0 and lines % 2 == 0
    even = [(i, i + 1) for i in range(0, size, 2)]
    odd = [(i, i + 1) for i in range(1, size - 1, 2)]
    routes = []
    for pairs in (even, odd):
        partner = dict(pairs + [(j, i) for i, j in pairs])
        routes.append(
            [
                (i * lines + line, partner[i] * lines + line if i in partner else i * lines + (line ^ 1))
                for i in range(size)
                for line in range(lines)
            ]
        )
    return routes


def local(source_field, receiver_field, sat_mask, offset_range):
    times, lines, cells, depth = source_field.shape
    size = lax.axis_size("inline")
    grant = pltpu.CompilerParams(vmem_limit_bytes=GRANT)
    image_cells = lines * cells * depth * (2 * H + 1)
    shape = jax.ShapeDtypeStruct
    total = shape((times, lines, cells, depth), jnp.float32)
    field_out = shape(source_field.shape, jnp.bfloat16)
    extended = pltpu.VMEM((times, lines, cells + 2 * REACH, depth), jnp.float32)
    edge = pltpu.VMEM((times, lines, ROWS + REACH, depth), jnp.float32)
    caps = pltpu.VMEM((lines, cells + 2 * H, depth), jnp.float32)
    limits = pltpu.VMEM((cells + 2 * H, depth), jnp.float32)

    def call(kernel, name, out_shape, operands, scratch=(), share=0.0, aliases={}):
        return pl.pallas_call(
            kernel,
            out_shape=out_shape,
            in_specs=[SMEM if operand is offset_range else VMEM for operand in operands],
            out_specs=jax.tree.map(lambda _: VMEM, out_shape),
            scratch_shapes=scratch,
            input_output_aliases=aliases,
            cost_estimate=pl.CostEstimate(
                flops=int(24 * image_cells * share), bytes_accessed=1 << 20, transcendentals=0
            ),
            compiler_params=grant,
            name=name,
        )(*operands)

    src, rcv, sat = source_field, receiver_field, sat_mask
    even, odd = payloads(rcv, sat, offset_range)
    even_route, odd_route = exchanges(size, lax.axis_size("xline"))
    even = lax.ppermute(even, DEVICES, even_route)
    odd = lax.ppermute(odd, DEVICES, odd_route)
    even_late = lax.ppermute(for_even(*edges(src, 2, REACH)), DEVICES, even_route)

    heavy, plain, inner = call(
        inner_kernel,
        "src_inner",
        (total, total, shape((2 * ROWS, depth), jnp.float32)),
        (offset_range, src, rcv, sat),
        [extended, caps],
        0.85,
    )
    sums = call(
        energy_kernel,
        "energy",
        shape((size * lax.axis_size("xline"), 2, depth), jnp.float32),
        (offset_range, src, sat, even, odd, inner),
        [pltpu.VMEM((2 * ROWS, depth), jnp.float32), edge, edge, caps, limits],
        0.15,
    )
    gathered = lax.all_to_all(sums, DEVICES, 0, 0, tiled=True)

    sums, heavy, plain, ahead = lax.optimization_barrier((sums, heavy, plain, src))
    heavy, plain = call(
        outer_kernel,
        "src_outer",
        (total, total),
        (offset_range, ahead, sat, even, odd, even, odd, heavy, plain),
        [edge, edge, caps, limits],
        0.25,
        {7: 0, 8: 1},
    )
    heavy, plain, ahead = lax.optimization_barrier((heavy, plain, ahead))
    odd_late = lax.ppermute(for_odd(*edges(ahead, 2, REACH)), DEVICES, odd_route)
    pieces = call(
        inner_kernel,
        "rcv_inner",
        (total, total),
        (offset_range, rcv, ahead, sat),
        [extended, caps],
        0.85,
    )
    pieces = call(
        outer_kernel,
        "rcv_outer",
        (total, total),
        (offset_range, rcv, sat, even, odd, even_late, odd_late, *pieces),
        [edge, edge, caps, limits],
        0.25,
        {7: 0, 8: 1},
    )

    cell_count = float(lines * lax.axis_size("xline") * cells * size * depth * (2 * H + 1))
    src_adj, rcv_adj, semblance = call(
        functools.partial(combine_kernel, cell_count),
        "combine",
        (field_out, field_out, shape((1, depth), jnp.float32)),
        (gathered, heavy, plain, *pieces),
    )
    return src_adj, rcv_adj, semblance[0, 0]


def solution(mesh):
    return jax.shard_map(
        local,
        mesh=mesh,
        in_specs=(
            P(None, "xline", "inline", None),
            P(None, "xline", "inline", None),
            P("xline", "inline", None),
            P("inline"),
        ),
        out_specs=(P(None, "xline", "inline", None), P(None, "xline", "inline", None), P()),
        check_vma=False,
    )
```

```python
import functools

import jax
import jax.numpy as jnp
from jax import lax
from jax.experimental import pallas as pl
from jax.experimental.pallas import tpu as pltpu
from jax.sharding import PartitionSpec as P

H = 32
EPSILON = 1e-06
SATURATION = 0.25
REACH = 2 * H
ALWAYS = 8
SHARED = H // 2
ROWS = 8
PAIR = 2 * ROWS
LIMIT_ROWS = 16
DEVICES = ("inline", "xline")
GROUP = 8
GRANT = 12 << 20
VMEM = pl.BlockSpec(memory_space=pltpu.VMEM)
SMEM = pl.BlockSpec(memory_space=pltpu.SMEM)


def square_weight(offset):
    relative = (offset / H) ** 2
    return relative * relative


def cap_of(mask):
    return jnp.where(mask != 0, SATURATION * SATURATION, 2.0)


def payload_layout(times, lines):
    mask_at = times * lines * REACH
    return mask_at, mask_at + lines * H


def by_parity(even, odd, work):
    here, size = lax.axis_index("inline"), lax.axis_size("inline")
    parity = lax.rem(here, 2)
    below, above = (here > 0).astype(jnp.float32), (here < size - 1).astype(jnp.float32)

    @pl.when(parity == 0)
    def _():
        work(even, False, above)
        work(odd, True, below)

    @pl.when(parity != 0)
    def _():
        work(even, True, below)
        work(odd, False, above)


def edges(value, axis, width):
    depth = value.shape[-1]
    length = value.shape[axis]
    low = lax.slice_in_dim(value, 0, width, axis=axis).reshape(-1, depth)
    return low, lax.slice_in_dim(value, length - width, length, axis=axis).reshape(-1, depth)


def for_even(low, high):
    return jnp.where(lax.axis_index("inline") % 2 == 0, high, low)


def for_odd(low, high):
    return for_even(high, low)


def payloads(rcv, sat, limit):
    depth = rcv.shape[-1]
    rows = edges(rcv, 2, REACH)
    rows = for_even(*rows), for_odd(*rows)
    *rows, sat = lax.optimization_barrier((*rows, sat))
    masks = edges((sat != 0).astype(jnp.bfloat16), 1, H)
    limits = jnp.full((LIMIT_ROWS, depth), limit[0]).astype(jnp.bfloat16)
    return [
        jnp.concatenate([part, choose(*masks), limits], axis=0) for part, choose in zip(rows, (for_even, for_odd))
    ]


def unpack_marks(times, limit, sat, even_in, odd_in, caps, limits):
    lines, cells, depth = sat.shape
    mask_at, limit_at = payload_layout(times, lines)

    def halo(arrived, low, there):
        row_at = 0 if low else H + cells
        for y in range(lines):
            caps[y, pl.ds(row_at, H), :] = cap_of(arrived[pl.ds(mask_at + y * H, H), :].astype(jnp.float32))
        value = arrived[pl.ds(limit_at, LIMIT_ROWS), :].astype(jnp.float32)
        for part in range(H // LIMIT_ROWS):
            limits[pl.ds(row_at + part * LIMIT_ROWS, LIMIT_ROWS), :] = value

    by_parity(even_in, odd_in, halo)
    for y in range(lines):
        caps[y, pl.ds(H, cells), :] = cap_of(sat[y])
    limits[pl.ds(H, cells), :] = jnp.full((cells, depth), limit[0], jnp.int32).astype(jnp.float32)


def unpack_halo(even_in, odd_in, low_out, high_out):
    times, lines, _, depth = low_out.shape
    blank = jnp.zeros((ROWS, depth), jnp.float32)

    def halo(arrived, low, there):
        out, field_at, blank_at = (low_out, 0, REACH) if low else (high_out, ROWS, 0)
        for t in range(times):
            for y in range(lines):
                at = (t * lines + y) * REACH
                out[t, y, pl.ds(field_at, REACH), :] = arrived[pl.ds(at, REACH), :].astype(jnp.float32) * there
                out[t, y, pl.ds(blank_at, ROWS), :] = blank

    by_parity(even_in, odd_in, halo)


def image_of(center, far):
    image = center[0] * far[0]
    for c, f in zip(center[1:], far[1:]):
        image = image + c * f
    return image


def accumulate(center, sums, offsets, far_at, masked, cap_at):
    heavy, plain = sums
    times = range(len(center))
    near = {}
    for offset in offsets:
        far = far_at(offset)
        image = masked(image_of(center, far), offset)
        if abs(offset) <= SHARED:
            terms = [image * f for f in far]
            if abs(offset) in near:
                terms = [a + b for a, b in zip(near.pop(abs(offset)), terms)]
            near[abs(offset)] = terms
            if offset == 0 or -offset not in offsets or offset > 0:
                near.pop(abs(offset))
                plain = [plain[t] + terms[t] for t in times]
                if offset:
                    square = square_weight(offset)
                    heavy = [heavy[t] + terms[t] * square for t in times]
        else:
            square = square_weight(offset)
            weighed = image * jnp.minimum(cap_at(offset), square)
            plain = [plain[t] + image * far[t] for t in times]
            heavy = [heavy[t] + weighed * far[t] for t in times]
    return heavy, plain


def paired(largest, smallest=0):
    return [sign * size for size in range(smallest, largest + 1) for sign in ((-1, 1) if size else (1,))]


def tiles_of(field, y, base):
    times = field.shape[0]
    both = [field[t, y, pl.ds(base, PAIR), :].astype(jnp.float32) for t in range(times)]
    return [[rows[half * ROWS : (half + 1) * ROWS] for rows in both] for half in range(2)]


def inner_kernel(limit, middle, field, sat, heavy_out, plain_out, *refs):
    *sums_out, shifted, caps = refs
    times, lines, cells, depth = field.shape
    zero = jnp.zeros((ROWS, depth), jnp.float32)
    blank = jnp.zeros((REACH, depth), jnp.float32)
    for t in range(times):
        for y in range(lines):
            shifted[t, y, pl.ds(0, REACH), :] = blank
            shifted[t, y, pl.ds(REACH, cells), :] = field[t, y].astype(jnp.float32)
            shifted[t, y, pl.ds(REACH + cells, REACH), :] = blank
    for y in range(lines):
        caps[y, pl.ds(0, H), :] = blank[:H]
        caps[y, pl.ds(H, cells), :] = cap_of(sat[y])
        caps[y, pl.ds(H + cells, H), :] = blank[:H]
    inside = [(size <= limit[0]).astype(jnp.float32) for size in range(H + 1)]

    def tile(index, totals):
        base = pl.multiple_of(index * PAIR, PAIR)
        for y in range(lines):
            for half, center in enumerate(tiles_of(middle, y, base)):
                at = base + half * ROWS

                def add(offsets, sums):
                    return accumulate(
                        center,
                        sums,
                        offsets,
                        lambda h: [shifted[t, y, pl.ds(at + REACH + 2 * h, ROWS), :] for t in range(times)],
                        lambda image, h: image * inside[abs(h)] if abs(h) > ALWAYS else image,
                        lambda h: caps[y, pl.ds(at + H + h, ROWS), :],
                    )

                sums = add(paired(SHARED), ([zero] * times, [zero] * times))
                for low in range(SHARED + 1, H + 1, GROUP):
                    below = base + PAIR - 1 - 2 * low >= 0
                    above = base + 2 * low < cells
                    for sign, reach in ((-1, below), (1, above)):
                        offsets = [sign * size for size in range(low, min(low + GROUP, H + 1))]
                        needed = jnp.logical_and(reach, limit[0] >= low)
                        sums = lax.cond(needed, functools.partial(add, offsets), lambda kept: kept, sums)
                heavy, plain = sums
                rows = pl.ds(base + half * ROWS, ROWS)
                for t in range(times):
                    heavy_out[t, y, rows, :] = heavy[t]
                    plain_out[t, y, rows, :] = plain[t]
                if sums_out:
                    totals = totals[0] + image_of(center, plain), totals[1] + image_of(center, heavy)
        return totals

    totals = lax.fori_loop(0, cells // PAIR, tile, (zero, zero) if sums_out else 0)
    if sums_out:
        sums_out[0][...] = jnp.concatenate(totals, axis=0)


def within(limits, at):
    def masked(image, offset):
        if abs(offset) <= ALWAYS:
            return image
        return jnp.where(limits[pl.ds(at + H + offset, ROWS), :] >= float(abs(offset)), image, 0.0)

    return masked


def each_outer_tile(middle, low, high, visit):
    times, lines, cells, depth = middle.shape

    for group in range(REACH // PAIR):

        def tile(index, carry, group=group):
            for side, shifted in ((0, low), (1, high)):

                @pl.when(index == side)
                def _():
                    first = cells - (group + 1) * PAIR if side else group * PAIR
                    base = pl.multiple_of(first + (index - side) * PAIR, PAIR)
                    origin = ROWS - cells if side else REACH
                    for y in range(lines):
                        for half, center in enumerate(tiles_of(middle, y, base)):
                            at = base + half * ROWS
                            rank = 2 * group + (1 - half if side else half)
                            sizes = range(ROWS // 2 * rank + 1, H + 1)
                            visit(
                                y,
                                at,
                                center,
                                [size if side else -size for size in sizes],
                                lambda h: [shifted[t, y, pl.ds(at + origin + 2 * h, ROWS), :] for t in range(times)],
                            )

            return carry

        lax.fori_loop(0, 2, tile, 0)


def energy_kernel(limit, src, sat, even_in, odd_in, inner, sums, total, low, high, caps, limits):
    times, lines, cells, depth = src.shape
    unpack_marks(times, limit, sat, even_in, odd_in, caps, limits)
    unpack_halo(even_in, odd_in, low, high)
    total[...] = inner[...]

    def visit(y, at, center, offsets, far_at):
        energy, weighted = total[:ROWS, :], total[ROWS:, :]
        masked = within(limits, at)
        for offset in offsets:
            image = masked(image_of(center, far_at(offset)), offset)
            power = image * image
            energy = energy + power
            square = square_weight(offset)
            if abs(offset) > SHARED:
                square = jnp.minimum(caps[y, pl.ds(at + H + offset, ROWS), :], square)
            weighted = weighted + power * square
        total[:ROWS, :] = energy
        total[ROWS:, :] = weighted

    each_outer_tile(src, low, high, visit)
    rows = [jnp.sum(total[pl.ds(part * ROWS, ROWS), :], axis=0, keepdims=True) for part in range(2)]
    sums[...] = jnp.broadcast_to(jnp.concatenate(rows, axis=0)[None], sums.shape)


def outer_kernel(limit, middle, sat, even_marks, odd_marks, even_in, odd_in, heavy_in, plain_in, heavy, plain, *scratch):
    low, high, caps, limits = scratch
    times, lines, cells, depth = middle.shape
    unpack_marks(times, limit, sat, even_marks, odd_marks, caps, limits)
    unpack_halo(even_in, odd_in, low, high)

    def visit(y, at, center, offsets, far_at):
        rows = pl.ds(at, ROWS)
        sums = [heavy[t, y, rows, :] for t in range(times)], [plain[t, y, rows, :] for t in range(times)]
        new_heavy, new_plain = accumulate(
            center, sums, offsets, far_at, within(limits, at), lambda h: caps[y, pl.ds(at + H + h, ROWS), :]
        )
        for t in range(times):
            heavy[t, y, rows, :] = new_heavy[t]
            plain[t, y, rows, :] = new_plain[t]

    each_outer_tile(middle, low, high, visit)


def combine_kernel(cell_count, sums, src_heavy, src_plain, *refs):
    pieces, (src_out, rcv_out, semblance_out) = refs[:-3], refs[-3:]
    total = jnp.sum(sums[...], axis=0)
    total = jnp.broadcast_to(jnp.sum(total, axis=1, keepdims=True), total.shape)
    energy, weighted = total[0:1], total[1:2]
    semblance = weighted / energy
    inverse_rms = 1.0 / jnp.sqrt(energy / cell_count + EPSILON)
    semblance_out[...] = semblance

    def put(out, start, heavy, plain):
        times, lines, count, _ = heavy.shape
        for t in range(times):
            for y in range(lines):
                value = inverse_rms * (heavy[t, y] - semblance * plain[t, y])
                out[t, y, pl.ds(start, count), :] = value.astype(jnp.bfloat16)

    put(src_out, 0, src_heavy, src_plain)
    start = 0
    for heavy, plain in zip(pieces[::2], pieces[1::2]):
        put(rcv_out, start, heavy, plain)
        start += heavy.shape[2]


def exchanges(size, lines):
    assert size % 2 == 0 and lines % 2 == 0
    even = [(i, i + 1) for i in range(0, size, 2)]
    odd = [(i, i + 1) for i in range(1, size - 1, 2)]
    routes = []
    for pairs in (even, odd):
        partner = dict(pairs + [(j, i) for i, j in pairs])
        routes.append(
            [
                (i * lines + line, partner[i] * lines + line if i in partner else i * lines + (line ^ 1))
                for i in range(size)
                for line in range(lines)
            ]
        )
    return routes


def local(source_field, receiver_field, sat_mask, offset_range):
    times, lines, cells, depth = source_field.shape
    size = lax.axis_size("inline")
    grant = pltpu.CompilerParams(vmem_limit_bytes=GRANT)
    image_cells = lines * cells * depth * (2 * H + 1)
    shape = jax.ShapeDtypeStruct
    total = shape((times, lines, cells, depth), jnp.float32)
    field_out = shape(source_field.shape, jnp.bfloat16)
    extended = pltpu.VMEM((times, lines, cells + 2 * REACH, depth), jnp.float32)
    edge = pltpu.VMEM((times, lines, ROWS + REACH, depth), jnp.float32)
    caps = pltpu.VMEM((lines, cells + 2 * H, depth), jnp.float32)
    limits = pltpu.VMEM((cells + 2 * H, depth), jnp.float32)

    def call(kernel, name, out_shape, operands, scratch=(), share=0.0, aliases={}):
        return pl.pallas_call(
            kernel,
            out_shape=out_shape,
            in_specs=[SMEM if operand is offset_range else VMEM for operand in operands],
            out_specs=jax.tree.map(lambda _: VMEM, out_shape),
            scratch_shapes=scratch,
            input_output_aliases=aliases,
            cost_estimate=pl.CostEstimate(
                flops=int(24 * image_cells * share), bytes_accessed=int(share * (1 << 20)), transcendentals=0
            ),
            compiler_params=grant,
            name=name,
        )(*operands)

    src, rcv, sat = source_field, receiver_field, sat_mask
    even, odd = payloads(rcv, sat, offset_range)
    even_route, odd_route = exchanges(size, lax.axis_size("xline"))
    even = lax.ppermute(even, DEVICES, even_route)
    odd = lax.ppermute(odd, DEVICES, odd_route)
    even_late = lax.ppermute(for_even(*edges(src, 2, REACH)), DEVICES, even_route)

    heavy, plain, inner = call(
        inner_kernel,
        "src_inner",
        (total, total, shape((2 * ROWS, depth), jnp.float32)),
        (offset_range, src, rcv, sat),
        [extended, caps],
        0.85,
    )
    sums = call(
        energy_kernel,
        "energy",
        shape((size * lax.axis_size("xline"), 2, depth), jnp.float32),
        (offset_range, src, sat, even, odd, inner),
        [pltpu.VMEM((2 * ROWS, depth), jnp.float32), edge, edge, caps, limits],
        0.15,
    )
    gathered = lax.all_to_all(sums, DEVICES, 0, 0, tiled=True)

    sums, heavy, plain, ahead = lax.optimization_barrier((sums, heavy, plain, src))
    heavy, plain = call(
        outer_kernel,
        "src_outer",
        (total, total),
        (offset_range, ahead, sat, even, odd, even, odd, heavy, plain),
        [edge, edge, caps, limits],
        0.0,
        {7: 0, 8: 1},
    )
    heavy, plain, ahead = lax.optimization_barrier((heavy, plain, ahead))
    odd_late = lax.ppermute(for_odd(*edges(ahead, 2, REACH)), DEVICES, odd_route)
    pieces = call(
        inner_kernel,
        "rcv_inner",
        (total, total),
        (offset_range, rcv, ahead, sat),
        [extended, caps],
        0.0,
    )
    pieces = call(
        outer_kernel,
        "rcv_outer",
        (total, total),
        (offset_range, rcv, sat, even, odd, even_late, odd_late, *pieces),
        [edge, edge, caps, limits],
        0.0,
        {7: 0, 8: 1},
    )

    cell_count = float(lines * lax.axis_size("xline") * cells * size * depth * (2 * H + 1))
    src_adj, rcv_adj, semblance = call(
        functools.partial(combine_kernel, cell_count),
        "combine",
        (field_out, field_out, shape((1, depth), jnp.float32)),
        (gathered, heavy, plain, *pieces),
    )
    return src_adj, rcv_adj, semblance[0, 0]


def solution(mesh):
    return jax.shard_map(
        local,
        mesh=mesh,
        in_specs=(
            P(None, "xline", "inline", None),
            P(None, "xline", "inline", None),
            P("xline", "inline", None),
            P("inline"),
        ),
        out_specs=(P(None, "xline", "inline", None), P(None, "xline", "inline", None), P()),
        check_vma=False,
    )
```

```python
import functools

import jax
import jax.numpy as jnp
from jax import lax
from jax.experimental import pallas as pl
from jax.experimental.pallas import tpu as pltpu
from jax.sharding import PartitionSpec as P

H = 32
EPSILON = 1e-06
SATURATION = 0.25
REACH = 2 * H
ALWAYS = 8
SHARED = H // 2
ROWS = 8
PAIR = 2 * ROWS
LIMIT_ROWS = 16
DEVICES = ("inline", "xline")
GROUP = 8
GRANT = 12 << 20
VMEM = pl.BlockSpec(memory_space=pltpu.VMEM)
SMEM = pl.BlockSpec(memory_space=pltpu.SMEM)


def square_weight(offset):
    relative = (offset / H) ** 2
    return relative * relative


def cap_of(mask):
    return jnp.where(mask != 0, SATURATION * SATURATION, 2.0)


def payload_layout(times, lines):
    mask_at = times * lines * REACH
    return mask_at, mask_at + lines * H


def by_parity(even, odd, work):
    here, size = lax.axis_index("inline"), lax.axis_size("inline")
    parity = lax.rem(here, 2)
    below, above = (here > 0).astype(jnp.float32), (here < size - 1).astype(jnp.float32)

    @pl.when(parity == 0)
    def _():
        work(even, False, above)
        work(odd, True, below)

    @pl.when(parity != 0)
    def _():
        work(even, True, below)
        work(odd, False, above)


def edges(value, axis, width):
    depth = value.shape[-1]
    length = value.shape[axis]
    low = lax.slice_in_dim(value, 0, width, axis=axis).reshape(-1, depth)
    return low, lax.slice_in_dim(value, length - width, length, axis=axis).reshape(-1, depth)


def for_even(low, high):
    return jnp.where(lax.axis_index("inline") % 2 == 0, high, low)


def for_odd(low, high):
    return for_even(high, low)


def payloads(rcv, sat, limit):
    depth = rcv.shape[-1]
    rows = edges(rcv, 2, REACH)
    rows = for_even(*rows), for_odd(*rows)
    *rows, sat = lax.optimization_barrier((*rows, sat))
    masks = edges((sat != 0).astype(jnp.bfloat16), 1, H)
    limits = jnp.full((LIMIT_ROWS, depth), limit[0]).astype(jnp.bfloat16)
    return [
        jnp.concatenate([part, choose(*masks), limits], axis=0) for part, choose in zip(rows, (for_even, for_odd))
    ]


def unpack_marks(times, limit, sat, even_in, odd_in, caps, limits):
    lines, cells, depth = sat.shape
    mask_at, limit_at = payload_layout(times, lines)

    def halo(arrived, low, there):
        row_at = 0 if low else H + cells
        for y in range(lines):
            caps[y, pl.ds(row_at, H), :] = cap_of(arrived[pl.ds(mask_at + y * H, H), :].astype(jnp.float32))
        value = arrived[pl.ds(limit_at, LIMIT_ROWS), :].astype(jnp.float32)
        for part in range(H // LIMIT_ROWS):
            limits[pl.ds(row_at + part * LIMIT_ROWS, LIMIT_ROWS), :] = value

    by_parity(even_in, odd_in, halo)
    for y in range(lines):
        caps[y, pl.ds(H, cells), :] = cap_of(sat[y])
    limits[pl.ds(H, cells), :] = jnp.full((cells, depth), limit[0], jnp.int32).astype(jnp.float32)


def unpack_halo(even_in, odd_in, low_out, high_out):
    times, lines, _, depth = low_out.shape
    blank = jnp.zeros((ROWS, depth), jnp.float32)

    def halo(arrived, low, there):
        out, field_at, blank_at = (low_out, 0, REACH) if low else (high_out, ROWS, 0)
        for t in range(times):
            for y in range(lines):
                at = (t * lines + y) * REACH
                out[t, y, pl.ds(field_at, REACH), :] = arrived[pl.ds(at, REACH), :].astype(jnp.float32) * there
                out[t, y, pl.ds(blank_at, ROWS), :] = blank

    by_parity(even_in, odd_in, halo)


def image_of(center, far):
    image = center[0] * far[0]
    for c, f in zip(center[1:], far[1:]):
        image = image + c * f
    return image


def accumulate(center, sums, offsets, far_at, masked, cap_at):
    heavy, plain = sums
    times = range(len(center))
    near = {}
    for offset in offsets:
        far = far_at(offset)
        image = masked(image_of(center, far), offset)
        if abs(offset) <= SHARED:
            terms = [image * f for f in far]
            if abs(offset) in near:
                terms = [a + b for a, b in zip(near.pop(abs(offset)), terms)]
            near[abs(offset)] = terms
            if offset == 0 or -offset not in offsets or offset > 0:
                near.pop(abs(offset))
                plain = [plain[t] + terms[t] for t in times]
                if offset:
                    square = square_weight(offset)
                    heavy = [heavy[t] + terms[t] * square for t in times]
        else:
            square = square_weight(offset)
            weighed = image * jnp.minimum(cap_at(offset), square)
            plain = [plain[t] + image * far[t] for t in times]
            heavy = [heavy[t] + weighed * far[t] for t in times]
    return heavy, plain


def paired(largest, smallest=0):
    return [sign * size for size in range(smallest, largest + 1) for sign in ((-1, 1) if size else (1,))]


def tiles_of(field, y, base):
    times = field.shape[0]
    both = [field[t, y, pl.ds(base, PAIR), :].astype(jnp.float32) for t in range(times)]
    return [[rows[half * ROWS : (half + 1) * ROWS] for rows in both] for half in range(2)]


def inner_kernel(limit, middle, field, sat, heavy_out, plain_out, *refs):
    *sums_out, shifted, caps = refs
    times, lines, cells, depth = field.shape
    zero = jnp.zeros((ROWS, depth), jnp.float32)
    blank = jnp.zeros((REACH, depth), jnp.float32)
    for t in range(times):
        for y in range(lines):
            shifted[t, y, pl.ds(0, REACH), :] = blank
            shifted[t, y, pl.ds(REACH, cells), :] = field[t, y].astype(jnp.float32)
            shifted[t, y, pl.ds(REACH + cells, REACH), :] = blank
    for y in range(lines):
        caps[y, pl.ds(0, H), :] = blank[:H]
        caps[y, pl.ds(H, cells), :] = cap_of(sat[y])
        caps[y, pl.ds(H + cells, H), :] = blank[:H]
    inside = [(size <= limit[0]).astype(jnp.float32) for size in range(H + 1)]

    def tile(index, totals):
        base = pl.multiple_of(index * PAIR, PAIR)
        for y in range(lines):
            for half, center in enumerate(tiles_of(middle, y, base)):
                at = base + half * ROWS

                def add(offsets, sums):
                    return accumulate(
                        center,
                        sums,
                        offsets,
                        lambda h: [shifted[t, y, pl.ds(at + REACH + 2 * h, ROWS), :] for t in range(times)],
                        lambda image, h: image * inside[abs(h)] if abs(h) > ALWAYS else image,
                        lambda h: caps[y, pl.ds(at + H + h, ROWS), :],
                    )

                sums = add(paired(SHARED), ([zero] * times, [zero] * times))
                for low in range(SHARED + 1, H + 1, GROUP):
                    below = base + PAIR - 1 - 2 * low >= 0
                    above = base + 2 * low < cells
                    for sign, reach in ((-1, below), (1, above)):
                        offsets = [sign * size for size in range(low, min(low + GROUP, H + 1))]
                        needed = jnp.logical_and(reach, limit[0] >= low)
                        sums = lax.cond(needed, functools.partial(add, offsets), lambda kept: kept, sums)
                heavy, plain = sums
                rows = pl.ds(base + half * ROWS, ROWS)
                for t in range(times):
                    heavy_out[t, y, rows, :] = heavy[t]
                    plain_out[t, y, rows, :] = plain[t]
                if sums_out:
                    totals = totals[0] + image_of(center, plain), totals[1] + image_of(center, heavy)
        return totals

    totals = lax.fori_loop(0, cells // PAIR, tile, (zero, zero) if sums_out else 0)
    if sums_out:
        sums_out[0][...] = jnp.concatenate(totals, axis=0)


def within(limits, at):
    def masked(image, offset):
        if abs(offset) <= ALWAYS:
            return image
        return jnp.where(limits[pl.ds(at + H + offset, ROWS), :] >= float(abs(offset)), image, 0.0)

    return masked


def each_outer_tile(middle, low, high, visit):
    times, lines, cells, depth = middle.shape

    for group in range(REACH // PAIR):

        def tile(index, carry, group=group):
            for side, shifted in ((0, low), (1, high)):

                @pl.when(index == side)
                def _():
                    first = cells - (group + 1) * PAIR if side else group * PAIR
                    base = pl.multiple_of(first + (index - side) * PAIR, PAIR)
                    origin = ROWS - cells if side else REACH
                    for y in range(lines):
                        for half, center in enumerate(tiles_of(middle, y, base)):
                            at = base + half * ROWS
                            rank = 2 * group + (1 - half if side else half)
                            sizes = range(ROWS // 2 * rank + 1, H + 1)
                            visit(
                                y,
                                at,
                                center,
                                [size if side else -size for size in sizes],
                                lambda h: [shifted[t, y, pl.ds(at + origin + 2 * h, ROWS), :] for t in range(times)],
                            )

            return carry

        lax.fori_loop(0, 2, tile, 0)


def energy_kernel(limit, src, sat, even_in, odd_in, inner, sums, total, low, high, caps, limits):
    times, lines, cells, depth = src.shape
    unpack_marks(times, limit, sat, even_in, odd_in, caps, limits)
    unpack_halo(even_in, odd_in, low, high)
    total[...] = inner[...]

    def visit(y, at, center, offsets, far_at):
        energy, weighted = total[:ROWS, :], total[ROWS:, :]
        masked = within(limits, at)
        for offset in offsets:
            image = masked(image_of(center, far_at(offset)), offset)
            power = image * image
            energy = energy + power
            square = square_weight(offset)
            if abs(offset) > SHARED:
                square = jnp.minimum(caps[y, pl.ds(at + H + offset, ROWS), :], square)
            weighted = weighted + power * square
        total[:ROWS, :] = energy
        total[ROWS:, :] = weighted

    each_outer_tile(src, low, high, visit)
    rows = [jnp.sum(total[pl.ds(part * ROWS, ROWS), :], axis=0, keepdims=True) for part in range(2)]
    sums[...] = jnp.broadcast_to(jnp.concatenate(rows, axis=0)[None], sums.shape)


def outer_kernel(limit, middle, sat, even_marks, odd_marks, even_in, odd_in, heavy_in, plain_in, heavy, plain, *scratch):
    low, high, caps, limits = scratch
    times, lines, cells, depth = middle.shape
    unpack_marks(times, limit, sat, even_marks, odd_marks, caps, limits)
    unpack_halo(even_in, odd_in, low, high)

    def visit(y, at, center, offsets, far_at):
        rows = pl.ds(at, ROWS)
        sums = [heavy[t, y, rows, :] for t in range(times)], [plain[t, y, rows, :] for t in range(times)]
        new_heavy, new_plain = accumulate(
            center, sums, offsets, far_at, within(limits, at), lambda h: caps[y, pl.ds(at + H + h, ROWS), :]
        )
        for t in range(times):
            heavy[t, y, rows, :] = new_heavy[t]
            plain[t, y, rows, :] = new_plain[t]

    each_outer_tile(middle, low, high, visit)


def combine_kernel(cell_count, sums, src_heavy, src_plain, *refs):
    pieces, (src_out, rcv_out, semblance_out) = refs[:-3], refs[-3:]
    total = jnp.sum(sums[...], axis=0)
    total = jnp.broadcast_to(jnp.sum(total, axis=1, keepdims=True), total.shape)
    energy, weighted = total[0:1], total[1:2]
    semblance = weighted / energy
    inverse_rms = 1.0 / jnp.sqrt(energy / cell_count + EPSILON)
    semblance_out[...] = semblance

    def put(out, start, heavy, plain):
        times, lines, count, _ = heavy.shape
        for t in range(times):
            for y in range(lines):
                value = inverse_rms * (heavy[t, y] - semblance * plain[t, y])
                out[t, y, pl.ds(start, count), :] = value.astype(jnp.bfloat16)

    put(src_out, 0, src_heavy, src_plain)
    start = 0
    for heavy, plain in zip(pieces[::2], pieces[1::2]):
        put(rcv_out, start, heavy, plain)
        start += heavy.shape[2]


def exchanges(size, lines):
    assert size % 2 == 0 and lines % 2 == 0
    even = [(i, i + 1) for i in range(0, size, 2)]
    odd = [(i, i + 1) for i in range(1, size - 1, 2)]
    routes = []
    for pairs in (even, odd):
        partner = dict(pairs + [(j, i) for i, j in pairs])
        routes.append(
            [
                (i * lines + line, partner[i] * lines + line if i in partner else i * lines + (line ^ 1))
                for i in range(size)
                for line in range(lines)
            ]
        )
    return routes


def local(source_field, receiver_field, sat_mask, offset_range):
    times, lines, cells, depth = source_field.shape
    size = lax.axis_size("inline")
    grant = pltpu.CompilerParams(vmem_limit_bytes=GRANT)
    image_cells = lines * cells * depth * (2 * H + 1)
    shape = jax.ShapeDtypeStruct
    total = shape((times, lines, cells, depth), jnp.float32)
    field_out = shape(source_field.shape, jnp.bfloat16)
    extended = pltpu.VMEM((times, lines, cells + 2 * REACH, depth), jnp.float32)
    edge = pltpu.VMEM((times, lines, ROWS + REACH, depth), jnp.float32)
    caps = pltpu.VMEM((lines, cells + 2 * H, depth), jnp.float32)
    limits = pltpu.VMEM((cells + 2 * H, depth), jnp.float32)

    def call(kernel, name, out_shape, operands, scratch=(), share=0.0, aliases={}):
        return pl.pallas_call(
            kernel,
            out_shape=out_shape,
            in_specs=[SMEM if operand is offset_range else VMEM for operand in operands],
            out_specs=jax.tree.map(lambda _: VMEM, out_shape),
            scratch_shapes=scratch,
            input_output_aliases=aliases,
            cost_estimate=pl.CostEstimate(
                flops=int(24 * image_cells * share), bytes_accessed=int(share * (1 << 20)), transcendentals=0
            ),
            compiler_params=grant,
            name=name,
        )(*operands)

    src, rcv, sat = source_field, receiver_field, sat_mask
    even, odd = payloads(rcv, sat, offset_range)
    even_route, odd_route = exchanges(size, lax.axis_size("xline"))
    even = lax.ppermute(even, DEVICES, even_route)
    odd = lax.ppermute(odd, DEVICES, odd_route)
    even_late = lax.ppermute(for_even(*edges(src, 2, REACH)), DEVICES, even_route)

    heavy, plain, inner = call(
        inner_kernel,
        "src_inner",
        (total, total, shape((2 * ROWS, depth), jnp.float32)),
        (offset_range, src, rcv, sat),
        [extended, caps],
        0.85,
    )
    inner, ahead = lax.optimization_barrier((inner, src))
    odd_late = lax.ppermute(for_odd(*edges(ahead, 2, REACH)), DEVICES, odd_route)
    sums = call(
        energy_kernel,
        "energy",
        shape((size * lax.axis_size("xline"), 2, depth), jnp.float32),
        (offset_range, src, sat, even, odd, inner),
        [pltpu.VMEM((2 * ROWS, depth), jnp.float32), edge, edge, caps, limits],
        0.15,
    )
    gathered = lax.all_to_all(sums, DEVICES, 0, 0, tiled=True)

    sums, heavy, plain, ahead, odd_late = lax.optimization_barrier((sums, heavy, plain, src, odd_late))
    heavy, plain = call(
        outer_kernel,
        "src_outer",
        (total, total),
        (offset_range, ahead, sat, even, odd, even, odd, heavy, plain),
        [edge, edge, caps, limits],
        0.25,
        {7: 0, 8: 1},
    )
    pieces = call(
        inner_kernel,
        "rcv_inner",
        (total, total),
        (offset_range, rcv, ahead, sat),
        [extended, caps],
        0.85,
    )
    pieces = call(
        outer_kernel,
        "rcv_outer",
        (total, total),
        (offset_range, rcv, sat, even, odd, even_late, odd_late, *pieces),
        [edge, edge, caps, limits],
        0.25,
        {7: 0, 8: 1},
    )

    cell_count = float(lines * lax.axis_size("xline") * cells * size * depth * (2 * H + 1))
    src_adj, rcv_adj, semblance = call(
        functools.partial(combine_kernel, cell_count),
        "combine",
        (field_out, field_out, shape((1, depth), jnp.float32)),
        (gathered, heavy, plain, *pieces),
    )
    return src_adj, rcv_adj, semblance[0, 0]


def solution(mesh):
    return jax.shard_map(
        local,
        mesh=mesh,
        in_specs=(
            P(None, "xline", "inline", None),
            P(None, "xline", "inline", None),
            P("xline", "inline", None),
            P("inline"),
        ),
        out_specs=(P(None, "xline", "inline", None), P(None, "xline", "inline", None), P()),
        check_vma=False,
    )
```

```python
import functools

import jax
import jax.numpy as jnp
from jax import lax
from jax.experimental import pallas as pl
from jax.experimental.pallas import tpu as pltpu
from jax.sharding import PartitionSpec as P

H = 32
EPSILON = 1e-06
SATURATION = 0.25
REACH = 2 * H
ALWAYS = 8
SHARED = H // 2
ROWS = 8
PAIR = 2 * ROWS
LIMIT_ROWS = 16
DEVICES = ("inline", "xline")
GROUP = 8
GRANT = 12 << 20
VMEM = pl.BlockSpec(memory_space=pltpu.VMEM)
SMEM = pl.BlockSpec(memory_space=pltpu.SMEM)


def square_weight(offset):
    relative = (offset / H) ** 2
    return relative * relative


def cap_of(mask):
    return jnp.where(mask != 0, SATURATION * SATURATION, 2.0)


def payload_layout(times, lines):
    mask_at = times * lines * REACH
    limit_at = mask_at + lines * H
    return mask_at, limit_at, limit_at + LIMIT_ROWS


def by_parity(even, odd, work):
    here, size = lax.axis_index("inline"), lax.axis_size("inline")
    parity = lax.rem(here, 2)
    below, above = (here > 0).astype(jnp.float32), (here < size - 1).astype(jnp.float32)

    @pl.when(parity == 0)
    def _():
        work(even, False, above)
        work(odd, True, below)

    @pl.when(parity != 0)
    def _():
        work(even, True, below)
        work(odd, False, above)


def edges(value, axis, width):
    depth = value.shape[-1]
    length = value.shape[axis]
    low = lax.slice_in_dim(value, 0, width, axis=axis).reshape(-1, depth)
    return low, lax.slice_in_dim(value, length - width, length, axis=axis).reshape(-1, depth)


def for_even(low, high):
    return jnp.where(lax.axis_index("inline") % 2 == 0, high, low)


def for_odd(low, high):
    return for_even(high, low)


def payloads(src, rcv, sat, limit):
    depth = rcv.shape[-1]
    rows = edges(rcv, 2, REACH)
    rows = for_even(*rows), for_odd(*rows)
    *rows, sat, src = lax.optimization_barrier((*rows, sat, src))
    masks = edges((sat != 0).astype(jnp.bfloat16), 1, H)
    limits = jnp.full((LIMIT_ROWS, depth), limit[0]).astype(jnp.bfloat16)
    odd = jnp.concatenate([rows[1], for_odd(*masks), limits], axis=0)
    return jnp.concatenate([rows[0], for_even(*masks), limits, for_even(*edges(src, 2, REACH))], axis=0), odd


def unpack_marks(times, limit, sat, even_in, odd_in, caps, limits):
    lines, cells, depth = sat.shape
    mask_at, limit_at, _ = payload_layout(times, lines)

    def halo(arrived, low, there):
        row_at = 0 if low else H + cells
        for y in range(lines):
            caps[y, pl.ds(row_at, H), :] = cap_of(arrived[pl.ds(mask_at + y * H, H), :].astype(jnp.float32))
        value = arrived[pl.ds(limit_at, LIMIT_ROWS), :].astype(jnp.float32)
        for part in range(H // LIMIT_ROWS):
            limits[pl.ds(row_at + part * LIMIT_ROWS, LIMIT_ROWS), :] = value

    by_parity(even_in, odd_in, halo)
    for y in range(lines):
        caps[y, pl.ds(H, cells), :] = cap_of(sat[y])
    limits[pl.ds(H, cells), :] = jnp.full((cells, depth), limit[0], jnp.int32).astype(jnp.float32)


def unpack_halo(even_in, odd_in, low_out, high_out, even_at=0):
    times, lines, _, depth = low_out.shape
    blank = jnp.zeros((ROWS, depth), jnp.float32)

    def halo(arrived, low, there):
        out, field_at, blank_at = (low_out, 0, REACH) if low else (high_out, ROWS, 0)
        start = even_at if arrived is even_in else 0
        for t in range(times):
            for y in range(lines):
                at = start + (t * lines + y) * REACH
                out[t, y, pl.ds(field_at, REACH), :] = arrived[pl.ds(at, REACH), :].astype(jnp.float32) * there
                out[t, y, pl.ds(blank_at, ROWS), :] = blank

    by_parity(even_in, odd_in, halo)


def image_of(center, far):
    image = center[0] * far[0]
    for c, f in zip(center[1:], far[1:]):
        image = image + c * f
    return image


def accumulate(center, sums, offsets, far_at, masked, cap_at):
    heavy, plain = sums
    times = range(len(center))
    near = {}
    for offset in offsets:
        far = far_at(offset)
        image = masked(image_of(center, far), offset)
        if abs(offset) <= SHARED:
            terms = [image * f for f in far]
            if abs(offset) in near:
                terms = [a + b for a, b in zip(near.pop(abs(offset)), terms)]
            near[abs(offset)] = terms
            if offset == 0 or -offset not in offsets or offset > 0:
                near.pop(abs(offset))
                plain = [plain[t] + terms[t] for t in times]
                if offset:
                    square = square_weight(offset)
                    heavy = [heavy[t] + terms[t] * square for t in times]
        else:
            square = square_weight(offset)
            weighed = image * jnp.minimum(cap_at(offset), square)
            plain = [plain[t] + image * far[t] for t in times]
            heavy = [heavy[t] + weighed * far[t] for t in times]
    return heavy, plain


def paired(largest, smallest=0):
    return [sign * size for size in range(smallest, largest + 1) for sign in ((-1, 1) if size else (1,))]


def tiles_of(field, y, base):
    times = field.shape[0]
    both = [field[t, y, pl.ds(base, PAIR), :].astype(jnp.float32) for t in range(times)]
    return [[rows[half * ROWS : (half + 1) * ROWS] for rows in both] for half in range(2)]


def inner_kernel(limit, middle, field, sat, heavy_out, plain_out, *refs):
    *sums_out, shifted, caps = refs
    times, lines, cells, depth = field.shape
    zero = jnp.zeros((ROWS, depth), jnp.float32)
    blank = jnp.zeros((REACH, depth), jnp.float32)
    for t in range(times):
        for y in range(lines):
            shifted[t, y, pl.ds(0, REACH), :] = blank
            shifted[t, y, pl.ds(REACH, cells), :] = field[t, y].astype(jnp.float32)
            shifted[t, y, pl.ds(REACH + cells, REACH), :] = blank
    for y in range(lines):
        caps[y, pl.ds(0, H), :] = blank[:H]
        caps[y, pl.ds(H, cells), :] = cap_of(sat[y])
        caps[y, pl.ds(H + cells, H), :] = blank[:H]
    inside = [(size <= limit[0]).astype(jnp.float32) for size in range(H + 1)]

    def tile(index, totals):
        base = pl.multiple_of(index * PAIR, PAIR)
        for y in range(lines):
            for half, center in enumerate(tiles_of(middle, y, base)):
                at = base + half * ROWS

                def add(offsets, sums):
                    return accumulate(
                        center,
                        sums,
                        offsets,
                        lambda h: [shifted[t, y, pl.ds(at + REACH + 2 * h, ROWS), :] for t in range(times)],
                        lambda image, h: image * inside[abs(h)] if abs(h) > ALWAYS else image,
                        lambda h: caps[y, pl.ds(at + H + h, ROWS), :],
                    )

                sums = add(paired(SHARED), ([zero] * times, [zero] * times))
                for low in range(SHARED + 1, H + 1, GROUP):
                    below = base + PAIR - 1 - 2 * low >= 0
                    above = base + 2 * low < cells
                    for sign, reach in ((-1, below), (1, above)):
                        offsets = [sign * size for size in range(low, min(low + GROUP, H + 1))]
                        needed = jnp.logical_and(reach, limit[0] >= low)
                        sums = lax.cond(needed, functools.partial(add, offsets), lambda kept: kept, sums)
                heavy, plain = sums
                rows = pl.ds(base + half * ROWS, ROWS)
                for t in range(times):
                    heavy_out[t, y, rows, :] = heavy[t]
                    plain_out[t, y, rows, :] = plain[t]
                if sums_out:
                    totals = totals[0] + image_of(center, plain), totals[1] + image_of(center, heavy)
        return totals

    totals = lax.fori_loop(0, cells // PAIR, tile, (zero, zero) if sums_out else 0)
    if sums_out:
        sums_out[0][...] = jnp.concatenate(totals, axis=0)


def within(limits, at):
    def masked(image, offset):
        if abs(offset) <= ALWAYS:
            return image
        return jnp.where(limits[pl.ds(at + H + offset, ROWS), :] >= float(abs(offset)), image, 0.0)

    return masked


def each_outer_tile(middle, low, high, visit):
    times, lines, cells, depth = middle.shape

    for group in range(REACH // PAIR):

        def tile(index, carry, group=group):
            for side, shifted in ((0, low), (1, high)):

                @pl.when(index == side)
                def _():
                    first = cells - (group + 1) * PAIR if side else group * PAIR
                    base = pl.multiple_of(first + (index - side) * PAIR, PAIR)
                    origin = ROWS - cells if side else REACH
                    for y in range(lines):
                        for half, center in enumerate(tiles_of(middle, y, base)):
                            at = base + half * ROWS
                            rank = 2 * group + (1 - half if side else half)
                            sizes = range(ROWS // 2 * rank + 1, H + 1)
                            visit(
                                y,
                                at,
                                center,
                                [size if side else -size for size in sizes],
                                lambda h: [shifted[t, y, pl.ds(at + origin + 2 * h, ROWS), :] for t in range(times)],
                            )

            return carry

        lax.fori_loop(0, 2, tile, 0)


def energy_kernel(limit, src, sat, even_in, odd_in, inner, sums, total, low, high, caps, limits):
    times, lines, cells, depth = src.shape
    unpack_marks(times, limit, sat, even_in, odd_in, caps, limits)
    unpack_halo(even_in, odd_in, low, high)
    total[...] = inner[...]

    def visit(y, at, center, offsets, far_at):
        energy, weighted = total[:ROWS, :], total[ROWS:, :]
        masked = within(limits, at)
        for offset in offsets:
            image = masked(image_of(center, far_at(offset)), offset)
            power = image * image
            energy = energy + power
            square = square_weight(offset)
            if abs(offset) > SHARED:
                square = jnp.minimum(caps[y, pl.ds(at + H + offset, ROWS), :], square)
            weighted = weighted + power * square
        total[:ROWS, :] = energy
        total[ROWS:, :] = weighted

    each_outer_tile(src, low, high, visit)
    rows = [jnp.sum(total[pl.ds(part * ROWS, ROWS), :], axis=0, keepdims=True) for part in range(2)]
    sums[...] = jnp.broadcast_to(jnp.concatenate(rows, axis=0)[None], sums.shape)


def outer_kernel(source, limit, middle, sat, even_in, odd_in, *refs):
    heavy, plain, low, high, caps, limits = refs[-6:]
    times, lines, cells, depth = middle.shape
    unpack_marks(times, limit, sat, even_in, odd_in, caps, limits)
    if source:
        unpack_halo(even_in, refs[0], low, high, payload_layout(times, lines)[2])
    else:
        unpack_halo(even_in, odd_in, low, high)

    def visit(y, at, center, offsets, far_at):
        rows = pl.ds(at, ROWS)
        sums = [heavy[t, y, rows, :] for t in range(times)], [plain[t, y, rows, :] for t in range(times)]
        new_heavy, new_plain = accumulate(
            center, sums, offsets, far_at, within(limits, at), lambda h: caps[y, pl.ds(at + H + h, ROWS), :]
        )
        for t in range(times):
            heavy[t, y, rows, :] = new_heavy[t]
            plain[t, y, rows, :] = new_plain[t]

    each_outer_tile(middle, low, high, visit)


def combine_kernel(cell_count, sums, src_heavy, src_plain, *refs):
    pieces, (src_out, rcv_out, semblance_out) = refs[:-3], refs[-3:]
    total = jnp.sum(sums[...], axis=0)
    total = jnp.broadcast_to(jnp.sum(total, axis=1, keepdims=True), total.shape)
    energy, weighted = total[0:1], total[1:2]
    semblance = weighted / energy
    inverse_rms = 1.0 / jnp.sqrt(energy / cell_count + EPSILON)
    semblance_out[...] = semblance

    def put(out, start, heavy, plain):
        times, lines, count, _ = heavy.shape
        for t in range(times):
            for y in range(lines):
                value = inverse_rms * (heavy[t, y] - semblance * plain[t, y])
                out[t, y, pl.ds(start, count), :] = value.astype(jnp.bfloat16)

    put(src_out, 0, src_heavy, src_plain)
    start = 0
    for heavy, plain in zip(pieces[::2], pieces[1::2]):
        put(rcv_out, start, heavy, plain)
        start += heavy.shape[2]


def exchanges(size, lines):
    assert size % 2 == 0 and lines % 2 == 0
    even = [(i, i + 1) for i in range(0, size, 2)]
    odd = [(i, i + 1) for i in range(1, size - 1, 2)]
    routes = []
    for pairs in (even, odd):
        partner = dict(pairs + [(j, i) for i, j in pairs])
        routes.append(
            [
                (i * lines + line, partner[i] * lines + line if i in partner else i * lines + (line ^ 1))
                for i in range(size)
                for line in range(lines)
            ]
        )
    return routes


def local(source_field, receiver_field, sat_mask, offset_range):
    times, lines, cells, depth = source_field.shape
    size = lax.axis_size("inline")
    grant = pltpu.CompilerParams(vmem_limit_bytes=GRANT)
    image_cells = lines * cells * depth * (2 * H + 1)
    shape = jax.ShapeDtypeStruct
    total = shape((times, lines, cells, depth), jnp.float32)
    field_out = shape(source_field.shape, jnp.bfloat16)
    extended = pltpu.VMEM((times, lines, cells + 2 * REACH, depth), jnp.float32)
    edge = pltpu.VMEM((times, lines, ROWS + REACH, depth), jnp.float32)
    caps = pltpu.VMEM((lines, cells + 2 * H, depth), jnp.float32)
    limits = pltpu.VMEM((cells + 2 * H, depth), jnp.float32)

    def call(kernel, name, out_shape, operands, scratch=(), share=0.0, aliases={}):
        return pl.pallas_call(
            kernel,
            out_shape=out_shape,
            in_specs=[SMEM if operand is offset_range else VMEM for operand in operands],
            out_specs=jax.tree.map(lambda _: VMEM, out_shape),
            scratch_shapes=scratch,
            input_output_aliases=aliases,
            cost_estimate=pl.CostEstimate(
                flops=int(24 * image_cells * share), bytes_accessed=int(share * (1 << 20)), transcendentals=0
            ),
            compiler_params=grant,
            name=name,
        )(*operands)

    src, rcv, sat = source_field, receiver_field, sat_mask
    even, odd = payloads(src, rcv, sat, offset_range)
    even_route, odd_route = exchanges(size, lax.axis_size("xline"))
    even = lax.ppermute(even, DEVICES, even_route)
    odd = lax.ppermute(odd, DEVICES, odd_route)

    heavy, plain, inner = call(
        inner_kernel,
        "src_inner",
        (total, total, shape((2 * ROWS, depth), jnp.float32)),
        (offset_range, src, rcv, sat),
        [extended, caps],
        0.85,
    )
    inner, ahead = lax.optimization_barrier((inner, src))
    odd_late = lax.ppermute(for_odd(*edges(ahead, 2, REACH)), DEVICES, odd_route)
    sums = call(
        energy_kernel,
        "energy",
        shape((size * lax.axis_size("xline"), 2, depth), jnp.float32),
        (offset_range, src, sat, even, odd, inner),
        [pltpu.VMEM((2 * ROWS, depth), jnp.float32), edge, edge, caps, limits],
        0.15,
    )
    gathered = lax.all_to_all(sums, DEVICES, 0, 0, tiled=True)

    sums, heavy, plain, ahead, odd_late = lax.optimization_barrier((sums, heavy, plain, src, odd_late))
    heavy, plain = call(
        functools.partial(outer_kernel, False),
        "src_outer",
        (total, total),
        (offset_range, ahead, sat, even, odd, heavy, plain),
        [edge, edge, caps, limits],
        0.25,
        {5: 0, 6: 1},
    )
    pieces = call(
        inner_kernel,
        "rcv_inner",
        (total, total),
        (offset_range, rcv, ahead, sat),
        [extended, caps],
        0.85,
    )
    pieces = call(
        functools.partial(outer_kernel, True),
        "rcv_outer",
        (total, total),
        (offset_range, rcv, sat, even, odd, odd_late, *pieces),
        [edge, edge, caps, limits],
        0.25,
        {6: 0, 7: 1},
    )

    cell_count = float(lines * lax.axis_size("xline") * cells * size * depth * (2 * H + 1))
    src_adj, rcv_adj, semblance = call(
        functools.partial(combine_kernel, cell_count),
        "combine",
        (field_out, field_out, shape((1, depth), jnp.float32)),
        (gathered, heavy, plain, *pieces),
    )
    return src_adj, rcv_adj, semblance[0, 0]


def solution(mesh):
    return jax.shard_map(
        local,
        mesh=mesh,
        in_specs=(
            P(None, "xline", "inline", None),
            P(None, "xline", "inline", None),
            P("xline", "inline", None),
            P("inline"),
        ),
        out_specs=(P(None, "xline", "inline", None), P(None, "xline", "inline", None), P()),
        check_vma=False,
    )
```

```python
import functools

import jax
import jax.numpy as jnp
from jax import lax
from jax.experimental import pallas as pl
from jax.experimental.pallas import tpu as pltpu
from jax.sharding import PartitionSpec as P

H = 32
EPSILON = 1e-06
SATURATION = 0.25
REACH = 2 * H
ALWAYS = 8
SHARED = H // 2
ROWS = 8
PAIR = 2 * ROWS
LIMIT_ROWS = 16
DEVICES = ("inline", "xline")
GROUP = 8
GRANT = 12 << 20
VMEM = pl.BlockSpec(memory_space=pltpu.VMEM)
SMEM = pl.BlockSpec(memory_space=pltpu.SMEM)


def square_weight(offset):
    relative = (offset / H) ** 2
    return relative * relative


def cap_of(mask):
    return jnp.where(mask != 0, SATURATION * SATURATION, 2.0)


def payload_layout(times, lines):
    mask_at = times * lines * REACH
    limit_at = mask_at + lines * H
    return mask_at, limit_at, limit_at + LIMIT_ROWS


def by_parity(even, odd, work):
    here, size = lax.axis_index("inline"), lax.axis_size("inline")
    parity = lax.rem(here, 2)
    below, above = (here > 0).astype(jnp.float32), (here < size - 1).astype(jnp.float32)

    @pl.when(parity == 0)
    def _():
        work(even, False, above)
        work(odd, True, below)

    @pl.when(parity != 0)
    def _():
        work(even, True, below)
        work(odd, False, above)


def edges(value, axis, width):
    depth = value.shape[-1]
    length = value.shape[axis]
    low = lax.slice_in_dim(value, 0, width, axis=axis).reshape(-1, depth)
    return low, lax.slice_in_dim(value, length - width, length, axis=axis).reshape(-1, depth)


def for_even(low, high):
    return jnp.where(lax.axis_index("inline") % 2 == 0, high, low)


def for_odd(low, high):
    return for_even(high, low)


def payloads(src, rcv, sat, limit):
    depth = rcv.shape[-1]
    rows = edges(rcv, 2, REACH)
    rows = for_even(*rows), for_odd(*rows)
    *rows, sat, src = lax.optimization_barrier((*rows, sat, src))
    masks = edges((sat != 0).astype(jnp.bfloat16), 1, H)
    limits = jnp.full((LIMIT_ROWS, depth), limit[0]).astype(jnp.bfloat16)
    odd = jnp.concatenate([rows[1], for_odd(*masks), limits], axis=0)
    return jnp.concatenate([rows[0], for_even(*masks), limits, for_even(*edges(src, 2, REACH))], axis=0), odd


def one_pair(even, arrived, work):
    here, size = lax.axis_index("inline"), lax.axis_size("inline")
    above = lax.rem(here + (1 if even else 0), 2)

    @pl.when(above != 0)
    def _():
        work(arrived, False, (here < size - 1).astype(jnp.float32))

    @pl.when(above == 0)
    def _():
        work(arrived, True, (here > 0).astype(jnp.float32))


def unpack_marks(times, limit, sat, caps, limits, over_halos):
    lines, cells, depth = sat.shape
    mask_at, limit_at, _ = payload_layout(times, lines)

    def halo(arrived, low, there):
        row_at = 0 if low else H + cells
        for y in range(lines):
            caps[y, pl.ds(row_at, H), :] = cap_of(arrived[pl.ds(mask_at + y * H, H), :].astype(jnp.float32))
        value = arrived[pl.ds(limit_at, LIMIT_ROWS), :].astype(jnp.float32)
        for part in range(H // LIMIT_ROWS):
            limits[pl.ds(row_at + part * LIMIT_ROWS, LIMIT_ROWS), :] = value

    over_halos(halo)
    for y in range(lines):
        caps[y, pl.ds(H, cells), :] = cap_of(sat[y])
    limits[pl.ds(H, cells), :] = jnp.full((cells, depth), limit[0], jnp.int32).astype(jnp.float32)


def unpack_halo(low_out, high_out, over_halos, even_in=None, even_at=0):
    times, lines, _, depth = low_out.shape
    blank = jnp.zeros((ROWS, depth), jnp.float32)

    def halo(arrived, low, there):
        out, field_at, blank_at = (low_out, 0, REACH) if low else (high_out, ROWS, 0)
        start = even_at if arrived is even_in else 0
        for t in range(times):
            for y in range(lines):
                at = start + (t * lines + y) * REACH
                out[t, y, pl.ds(field_at, REACH), :] = arrived[pl.ds(at, REACH), :].astype(jnp.float32) * there
                out[t, y, pl.ds(blank_at, ROWS), :] = blank

    over_halos(halo)


def image_of(center, far):
    image = center[0] * far[0]
    for c, f in zip(center[1:], far[1:]):
        image = image + c * f
    return image


def accumulate(center, sums, offsets, far_at, masked, cap_at):
    heavy, plain = sums
    times = range(len(center))
    near = {}
    for offset in offsets:
        far = far_at(offset)
        image = masked(image_of(center, far), offset)
        if abs(offset) <= SHARED:
            terms = [image * f for f in far]
            if abs(offset) in near:
                terms = [a + b for a, b in zip(near.pop(abs(offset)), terms)]
            near[abs(offset)] = terms
            if offset == 0 or -offset not in offsets or offset > 0:
                near.pop(abs(offset))
                plain = [plain[t] + terms[t] for t in times]
                if offset:
                    square = square_weight(offset)
                    heavy = [heavy[t] + terms[t] * square for t in times]
        else:
            square = square_weight(offset)
            weighed = image * jnp.minimum(cap_at(offset), square)
            plain = [plain[t] + image * far[t] for t in times]
            heavy = [heavy[t] + weighed * far[t] for t in times]
    return heavy, plain


def paired(largest, smallest=0):
    return [sign * size for size in range(smallest, largest + 1) for sign in ((-1, 1) if size else (1,))]


def tiles_of(field, y, base):
    times = field.shape[0]
    both = [field[t, y, pl.ds(base, PAIR), :].astype(jnp.float32) for t in range(times)]
    return [[rows[half * ROWS : (half + 1) * ROWS] for rows in both] for half in range(2)]


def inner_kernel(limit, middle, field, sat, heavy_out, plain_out, *refs):
    *sums_out, shifted, caps = refs
    times, lines, cells, depth = field.shape
    zero = jnp.zeros((ROWS, depth), jnp.float32)
    blank = jnp.zeros((REACH, depth), jnp.float32)
    for t in range(times):
        for y in range(lines):
            shifted[t, y, pl.ds(0, REACH), :] = blank
            shifted[t, y, pl.ds(REACH, cells), :] = field[t, y].astype(jnp.float32)
            shifted[t, y, pl.ds(REACH + cells, REACH), :] = blank
    for y in range(lines):
        caps[y, pl.ds(0, H), :] = blank[:H]
        caps[y, pl.ds(H, cells), :] = cap_of(sat[y])
        caps[y, pl.ds(H + cells, H), :] = blank[:H]
    inside = [(size <= limit[0]).astype(jnp.float32) for size in range(H + 1)]

    def tile(index, totals):
        base = pl.multiple_of(index * PAIR, PAIR)
        for y in range(lines):
            for half, center in enumerate(tiles_of(middle, y, base)):
                at = base + half * ROWS

                def add(offsets, sums):
                    return accumulate(
                        center,
                        sums,
                        offsets,
                        lambda h: [shifted[t, y, pl.ds(at + REACH + 2 * h, ROWS), :] for t in range(times)],
                        lambda image, h: image * inside[abs(h)] if abs(h) > ALWAYS else image,
                        lambda h: caps[y, pl.ds(at + H + h, ROWS), :],
                    )

                sums = add(paired(SHARED), ([zero] * times, [zero] * times))
                for low in range(SHARED + 1, H + 1, GROUP):
                    below = base + PAIR - 1 - 2 * low >= 0
                    above = base + 2 * low < cells
                    for sign, reach in ((-1, below), (1, above)):
                        offsets = [sign * size for size in range(low, min(low + GROUP, H + 1))]
                        needed = jnp.logical_and(reach, limit[0] >= low)
                        sums = lax.cond(needed, functools.partial(add, offsets), lambda kept: kept, sums)
                heavy, plain = sums
                rows = pl.ds(base + half * ROWS, ROWS)
                for t in range(times):
                    heavy_out[t, y, rows, :] = heavy[t]
                    plain_out[t, y, rows, :] = plain[t]
                if sums_out:
                    totals = totals[0] + image_of(center, plain), totals[1] + image_of(center, heavy)
        return totals

    totals = lax.fori_loop(0, cells // PAIR, tile, (zero, zero) if sums_out else 0)
    if sums_out:
        sums_out[0][...] = jnp.concatenate(totals, axis=0)


def within(limits, at):
    def masked(image, offset):
        if abs(offset) <= ALWAYS:
            return image
        return jnp.where(limits[pl.ds(at + H + offset, ROWS), :] >= float(abs(offset)), image, 0.0)

    return masked


def each_outer_tile(middle, low, high, visit, sides=(0, 2)):
    times, lines, cells, depth = middle.shape

    for group in range(REACH // PAIR):

        def tile(index, carry, group=group):
            for side, shifted in ((0, low), (1, high)):

                @pl.when(index == side)
                def _():
                    first = cells - (group + 1) * PAIR if side else group * PAIR
                    base = pl.multiple_of(first + (index - side) * PAIR, PAIR)
                    origin = ROWS - cells if side else REACH
                    for y in range(lines):
                        for half, center in enumerate(tiles_of(middle, y, base)):
                            at = base + half * ROWS
                            rank = 2 * group + (1 - half if side else half)
                            sizes = range(ROWS // 2 * rank + 1, H + 1)
                            visit(
                                y,
                                at,
                                center,
                                [size if side else -size for size in sizes],
                                lambda h: [shifted[t, y, pl.ds(at + origin + 2 * h, ROWS), :] for t in range(times)],
                            )

            return carry

        lax.fori_loop(*sides, tile, 0)


def energy_kernel(even, limit, src, sat, arrived, before, sums, total, low, high, caps, limits):
    times, lines, cells, depth = src.shape
    unpack_marks(times, limit, sat, caps, limits, functools.partial(one_pair, even, arrived))
    above = lax.rem(lax.axis_index("inline") + (1 if even else 0), 2)
    unpack_halo(low, high, functools.partial(one_pair, even, arrived))
    total[...] = before[...]

    def visit(y, at, center, offsets, far_at):
        energy, weighted = total[:ROWS, :], total[ROWS:, :]
        masked = within(limits, at)
        for offset in offsets:
            image = masked(image_of(center, far_at(offset)), offset)
            power = image * image
            energy = energy + power
            square = square_weight(offset)
            if abs(offset) > SHARED:
                square = jnp.minimum(caps[y, pl.ds(at + H + offset, ROWS), :], square)
            weighted = weighted + power * square
        total[:ROWS, :] = energy
        total[ROWS:, :] = weighted

    each_outer_tile(src, low, high, visit, (above, above + 1))
    if sums.shape == total.shape:
        sums[...] = total[...]
        return
    rows = [jnp.sum(total[pl.ds(part * ROWS, ROWS), :], axis=0, keepdims=True) for part in range(2)]
    sums[...] = jnp.broadcast_to(jnp.concatenate(rows, axis=0)[None], sums.shape)


def outer_kernel(source, limit, middle, sat, even_in, odd_in, *refs):
    heavy, plain, low, high, caps, limits = refs[-6:]
    times, lines, cells, depth = middle.shape
    unpack_marks(times, limit, sat, caps, limits, functools.partial(by_parity, even_in, odd_in))
    if source:
        late = functools.partial(by_parity, even_in, refs[0])
        unpack_halo(low, high, late, even_in, payload_layout(times, lines)[2])
    else:
        unpack_halo(low, high, functools.partial(by_parity, even_in, odd_in))

    def visit(y, at, center, offsets, far_at):
        rows = pl.ds(at, ROWS)
        sums = [heavy[t, y, rows, :] for t in range(times)], [plain[t, y, rows, :] for t in range(times)]
        new_heavy, new_plain = accumulate(
            center, sums, offsets, far_at, within(limits, at), lambda h: caps[y, pl.ds(at + H + h, ROWS), :]
        )
        for t in range(times):
            heavy[t, y, rows, :] = new_heavy[t]
            plain[t, y, rows, :] = new_plain[t]

    each_outer_tile(middle, low, high, visit)


def combine_kernel(cell_count, sums, src_heavy, src_plain, *refs):
    pieces, (src_out, rcv_out, semblance_out) = refs[:-3], refs[-3:]
    total = jnp.sum(sums[...], axis=0)
    total = jnp.broadcast_to(jnp.sum(total, axis=1, keepdims=True), total.shape)
    energy, weighted = total[0:1], total[1:2]
    semblance = weighted / energy
    inverse_rms = 1.0 / jnp.sqrt(energy / cell_count + EPSILON)
    semblance_out[...] = semblance

    def put(out, start, heavy, plain):
        times, lines, count, _ = heavy.shape
        for t in range(times):
            for y in range(lines):
                value = inverse_rms * (heavy[t, y] - semblance * plain[t, y])
                out[t, y, pl.ds(start, count), :] = value.astype(jnp.bfloat16)

    put(src_out, 0, src_heavy, src_plain)
    start = 0
    for heavy, plain in zip(pieces[::2], pieces[1::2]):
        put(rcv_out, start, heavy, plain)
        start += heavy.shape[2]


def exchanges(size, lines):
    assert size % 2 == 0 and lines % 2 == 0
    even = [(i, i + 1) for i in range(0, size, 2)]
    odd = [(i, i + 1) for i in range(1, size - 1, 2)]
    routes = []
    for pairs in (even, odd):
        partner = dict(pairs + [(j, i) for i, j in pairs])
        routes.append(
            [
                (i * lines + line, partner[i] * lines + line if i in partner else i * lines + (line ^ 1))
                for i in range(size)
                for line in range(lines)
            ]
        )
    return routes


def local(source_field, receiver_field, sat_mask, offset_range):
    times, lines, cells, depth = source_field.shape
    size = lax.axis_size("inline")
    grant = pltpu.CompilerParams(vmem_limit_bytes=GRANT)
    image_cells = lines * cells * depth * (2 * H + 1)
    shape = jax.ShapeDtypeStruct
    total = shape((times, lines, cells, depth), jnp.float32)
    field_out = shape(source_field.shape, jnp.bfloat16)
    extended = pltpu.VMEM((times, lines, cells + 2 * REACH, depth), jnp.float32)
    edge = pltpu.VMEM((times, lines, ROWS + REACH, depth), jnp.float32)
    caps = pltpu.VMEM((lines, cells + 2 * H, depth), jnp.float32)
    limits = pltpu.VMEM((cells + 2 * H, depth), jnp.float32)

    def call(kernel, name, out_shape, operands, scratch=(), share=0.0, aliases={}):
        return pl.pallas_call(
            kernel,
            out_shape=out_shape,
            in_specs=[SMEM if operand is offset_range else VMEM for operand in operands],
            out_specs=jax.tree.map(lambda _: VMEM, out_shape),
            scratch_shapes=scratch,
            input_output_aliases=aliases,
            cost_estimate=pl.CostEstimate(
                flops=int(24 * image_cells * share), bytes_accessed=int(share * (1 << 20)), transcendentals=0
            ),
            compiler_params=grant,
            name=name,
        )(*operands)

    src, rcv, sat = source_field, receiver_field, sat_mask
    even, odd = payloads(src, rcv, sat, offset_range)
    even_route, odd_route = exchanges(size, lax.axis_size("xline"))
    even = lax.ppermute(even, DEVICES, even_route)
    odd = lax.ppermute(odd, DEVICES, odd_route)

    heavy, plain, inner = call(
        inner_kernel,
        "src_inner",
        (total, total, shape((2 * ROWS, depth), jnp.float32)),
        (offset_range, src, rcv, sat),
        [extended, caps],
        0.85,
    )
    inner, ahead = lax.optimization_barrier((inner, src))
    odd_late = lax.ppermute(for_odd(*edges(ahead, 2, REACH)), DEVICES, odd_route)
    by_row = shape((2 * ROWS, depth), jnp.float32)
    by_device = shape((size * lax.axis_size("xline"), 2, depth), jnp.float32)
    sums = inner
    for is_even, arrived, out_shape in ((False, odd, by_row), (True, even, by_device)):
        sums = call(
            functools.partial(energy_kernel, is_even),
            "energy",
            out_shape,
            (offset_range, src, sat, arrived, sums),
            [pltpu.VMEM(by_row.shape, jnp.float32), edge, edge, caps, limits],
            0.07,
        )
    gathered = lax.all_to_all(sums, DEVICES, 0, 0, tiled=True)

    sums, heavy, plain, ahead, odd_late = lax.optimization_barrier((sums, heavy, plain, src, odd_late))
    heavy, plain = call(
        functools.partial(outer_kernel, False),
        "src_outer",
        (total, total),
        (offset_range, ahead, sat, even, odd, heavy, plain),
        [edge, edge, caps, limits],
        0.25,
        {5: 0, 6: 1},
    )
    pieces = call(
        inner_kernel,
        "rcv_inner",
        (total, total),
        (offset_range, rcv, ahead, sat),
        [extended, caps],
        0.85,
    )
    pieces = call(
        functools.partial(outer_kernel, True),
        "rcv_outer",
        (total, total),
        (offset_range, rcv, sat, even, odd, odd_late, *pieces),
        [edge, edge, caps, limits],
        0.25,
        {6: 0, 7: 1},
    )

    cell_count = float(lines * lax.axis_size("xline") * cells * size * depth * (2 * H + 1))
    src_adj, rcv_adj, semblance = call(
        functools.partial(combine_kernel, cell_count),
        "combine",
        (field_out, field_out, shape((1, depth), jnp.float32)),
        (gathered, heavy, plain, *pieces),
    )
    return src_adj, rcv_adj, semblance[0, 0]


def solution(mesh):
    return jax.shard_map(
        local,
        mesh=mesh,
        in_specs=(
            P(None, "xline", "inline", None),
            P(None, "xline", "inline", None),
            P("xline", "inline", None),
            P("inline"),
        ),
        out_specs=(P(None, "xline", "inline", None), P(None, "xline", "inline", None), P()),
        check_vma=False,
    )
```

```python
import functools

import jax
import jax.numpy as jnp
from jax import lax
from jax.experimental import pallas as pl
from jax.experimental.pallas import tpu as pltpu
from jax.sharding import PartitionSpec as P

H = 32
EPSILON = 1e-06
SATURATION = 0.25
REACH = 2 * H
ALWAYS = 8
SHARED = H // 2
ROWS = 8
PAIR = 2 * ROWS
LIMIT_ROWS = 16
DEVICES = ("inline", "xline")
GROUP = 8
GRANT = 12 << 20
VMEM = pl.BlockSpec(memory_space=pltpu.VMEM)
HBM = pl.BlockSpec(memory_space=pltpu.HBM)
SMEM = pl.BlockSpec(memory_space=pltpu.SMEM)


def square_weight(offset):
    relative = (offset / H) ** 2
    return relative * relative


def cap_of(mask):
    return jnp.where(mask != 0, SATURATION * SATURATION, 2.0)


def payload_layout(times, lines):
    mask_at = times * lines * REACH
    limit_at = mask_at + lines * H
    return mask_at, limit_at, limit_at + LIMIT_ROWS


def by_parity(even, odd, work):
    here, size = lax.axis_index("inline"), lax.axis_size("inline")
    parity = lax.rem(here, 2)
    below, above = (here > 0).astype(jnp.float32), (here < size - 1).astype(jnp.float32)

    @pl.when(parity == 0)
    def _():
        work(even, False, above)
        work(odd, True, below)

    @pl.when(parity != 0)
    def _():
        work(even, True, below)
        work(odd, False, above)


def edges(value, axis, width):
    depth = value.shape[-1]
    length = value.shape[axis]
    low = lax.slice_in_dim(value, 0, width, axis=axis).reshape(-1, depth)
    return low, lax.slice_in_dim(value, length - width, length, axis=axis).reshape(-1, depth)


def for_even(low, high):
    return jnp.where(lax.axis_index("inline") % 2 == 0, high, low)


def for_odd(low, high):
    return for_even(high, low)


def payloads(src, rcv, sat, limit):
    depth = rcv.shape[-1]
    rows = edges(rcv, 2, REACH)
    rows = for_even(*rows), for_odd(*rows)
    *rows, sat, src = lax.optimization_barrier((*rows, sat, src))
    masks = edges((sat != 0).astype(jnp.bfloat16), 1, H)
    limits = jnp.full((LIMIT_ROWS, depth), limit[0]).astype(jnp.bfloat16)
    odd = jnp.concatenate([rows[1], for_odd(*masks), limits], axis=0)
    return jnp.concatenate([rows[0], for_even(*masks), limits, for_even(*edges(src, 2, REACH))], axis=0), odd


def one_pair(even, arrived, work):
    here, size = lax.axis_index("inline"), lax.axis_size("inline")
    above = lax.rem(here + (1 if even else 0), 2)

    @pl.when(above != 0)
    def _():
        work(arrived, False, (here < size - 1).astype(jnp.float32))

    @pl.when(above == 0)
    def _():
        work(arrived, True, (here > 0).astype(jnp.float32))


def unpack_marks(times, limit, sat, caps, limits, over_halos):
    lines, cells, depth = sat.shape
    mask_at, limit_at, _ = payload_layout(times, lines)

    def halo(arrived, low, there):
        row_at = 0 if low else H + cells
        for y in range(lines):
            caps[y, pl.ds(row_at, H), :] = cap_of(arrived[pl.ds(mask_at + y * H, H), :].astype(jnp.float32))
        value = arrived[pl.ds(limit_at, LIMIT_ROWS), :].astype(jnp.float32)
        for part in range(H // LIMIT_ROWS):
            limits[pl.ds(row_at + part * LIMIT_ROWS, LIMIT_ROWS), :] = value

    over_halos(halo)
    for y in range(lines):
        caps[y, pl.ds(H, cells), :] = cap_of(sat[y])
    limits[pl.ds(H, cells), :] = jnp.full((cells, depth), limit[0], jnp.int32).astype(jnp.float32)


def unpack_halo(low_out, high_out, over_halos, even_in=None, even_at=0):
    times, lines, _, depth = low_out.shape
    blank = jnp.zeros((ROWS, depth), jnp.float32)

    def halo(arrived, low, there):
        out, field_at, blank_at = (low_out, 0, REACH) if low else (high_out, ROWS, 0)
        start = even_at if arrived is even_in else 0
        for t in range(times):
            for y in range(lines):
                at = start + (t * lines + y) * REACH
                out[t, y, pl.ds(field_at, REACH), :] = arrived[pl.ds(at, REACH), :].astype(jnp.float32) * there
                out[t, y, pl.ds(blank_at, ROWS), :] = blank

    over_halos(halo)


def image_of(center, far):
    image = center[0] * far[0]
    for c, f in zip(center[1:], far[1:]):
        image = image + c * f
    return image


def accumulate(center, sums, offsets, far_at, masked, cap_at):
    heavy, plain = sums
    times = range(len(center))
    near = {}
    for offset in offsets:
        far = far_at(offset)
        image = masked(image_of(center, far), offset)
        if abs(offset) <= SHARED:
            terms = [image * f for f in far]
            if abs(offset) in near:
                terms = [a + b for a, b in zip(near.pop(abs(offset)), terms)]
            near[abs(offset)] = terms
            if offset == 0 or -offset not in offsets or offset > 0:
                near.pop(abs(offset))
                plain = [plain[t] + terms[t] for t in times]
                if offset:
                    square = square_weight(offset)
                    heavy = [heavy[t] + terms[t] * square for t in times]
        else:
            square = square_weight(offset)
            weighed = image * jnp.minimum(cap_at(offset), square)
            plain = [plain[t] + image * far[t] for t in times]
            heavy = [heavy[t] + weighed * far[t] for t in times]
    return heavy, plain


def paired(largest, smallest=0):
    return [sign * size for size in range(smallest, largest + 1) for sign in ((-1, 1) if size else (1,))]


def tiles_of(field, y, base):
    times = field.shape[0]
    both = [field[t, y, pl.ds(base, PAIR), :].astype(jnp.float32) for t in range(times)]
    return [[rows[half * ROWS : (half + 1) * ROWS] for rows in both] for half in range(2)]


def inner_kernel(limit, middle, field, sat, heavy_out, plain_out, *refs):
    *sums_out, shifted, caps = refs
    times, lines, cells, depth = field.shape
    zero = jnp.zeros((ROWS, depth), jnp.float32)
    blank = jnp.zeros((REACH, depth), jnp.float32)
    for t in range(times):
        for y in range(lines):
            shifted[t, y, pl.ds(0, REACH), :] = blank
            shifted[t, y, pl.ds(REACH, cells), :] = field[t, y].astype(jnp.float32)
            shifted[t, y, pl.ds(REACH + cells, REACH), :] = blank
    for y in range(lines):
        caps[y, pl.ds(0, H), :] = blank[:H]
        caps[y, pl.ds(H, cells), :] = cap_of(sat[y])
        caps[y, pl.ds(H + cells, H), :] = blank[:H]
    inside = [(size <= limit[0]).astype(jnp.float32) for size in range(H + 1)]

    def tile(index, totals):
        base = pl.multiple_of(index * PAIR, PAIR)
        for y in range(lines):
            for half, center in enumerate(tiles_of(middle, y, base)):
                at = base + half * ROWS

                def add(offsets, sums):
                    return accumulate(
                        center,
                        sums,
                        offsets,
                        lambda h: [shifted[t, y, pl.ds(at + REACH + 2 * h, ROWS), :] for t in range(times)],
                        lambda image, h: image * inside[abs(h)] if abs(h) > ALWAYS else image,
                        lambda h: caps[y, pl.ds(at + H + h, ROWS), :],
                    )

                sums = add(paired(SHARED), ([zero] * times, [zero] * times))
                for low in range(SHARED + 1, H + 1, GROUP):
                    below = base + PAIR - 1 - 2 * low >= 0
                    above = base + 2 * low < cells
                    for sign, reach in ((-1, below), (1, above)):
                        offsets = [sign * size for size in range(low, min(low + GROUP, H + 1))]
                        needed = jnp.logical_and(reach, limit[0] >= low)
                        sums = lax.cond(needed, functools.partial(add, offsets), lambda kept: kept, sums)
                heavy, plain = sums
                rows = pl.ds(base + half * ROWS, ROWS)
                for t in range(times):
                    heavy_out[t, y, rows, :] = heavy[t]
                    plain_out[t, y, rows, :] = plain[t]
                if sums_out:
                    totals = totals[0] + image_of(center, plain), totals[1] + image_of(center, heavy)
        return totals

    totals = lax.fori_loop(0, cells // PAIR, tile, (zero, zero) if sums_out else 0)
    if sums_out:
        sums_out[0][...] = jnp.concatenate(totals, axis=0)


def within(limits, at):
    def masked(image, offset):
        if abs(offset) <= ALWAYS:
            return image
        return jnp.where(limits[pl.ds(at + H + offset, ROWS), :] >= float(abs(offset)), image, 0.0)

    return masked


def each_outer_tile(middle, low, high, visit, sides=(0, 2)):
    times, lines, cells, depth = middle.shape

    for group in range(REACH // PAIR):

        def tile(index, carry, group=group):
            for side, shifted in ((0, low), (1, high)):

                @pl.when(index == side)
                def _():
                    first = cells - (group + 1) * PAIR if side else group * PAIR
                    base = pl.multiple_of(first + (index - side) * PAIR, PAIR)
                    origin = ROWS - cells if side else REACH
                    for y in range(lines):
                        for half, center in enumerate(tiles_of(middle, y, base)):
                            at = base + half * ROWS
                            rank = 2 * group + (1 - half if side else half)
                            sizes = range(ROWS // 2 * rank + 1, H + 1)
                            visit(
                                y,
                                at,
                                center,
                                [size if side else -size for size in sizes],
                                lambda h: [shifted[t, y, pl.ds(at + origin + 2 * h, ROWS), :] for t in range(times)],
                            )

            return carry

        lax.fori_loop(*sides, tile, 0)


def energy_kernel(even, limit, src, sat, arrived, before, sums, total, low, high, caps, limits):
    times, lines, cells, depth = src.shape
    unpack_marks(times, limit, sat, caps, limits, functools.partial(one_pair, even, arrived))
    above = lax.rem(lax.axis_index("inline") + (1 if even else 0), 2)
    unpack_halo(low, high, functools.partial(one_pair, even, arrived))
    total[...] = before[...]

    def visit(y, at, center, offsets, far_at):
        energy, weighted = total[:ROWS, :], total[ROWS:, :]
        masked = within(limits, at)
        for offset in offsets:
            image = masked(image_of(center, far_at(offset)), offset)
            power = image * image
            energy = energy + power
            square = square_weight(offset)
            if abs(offset) > SHARED:
                square = jnp.minimum(caps[y, pl.ds(at + H + offset, ROWS), :], square)
            weighted = weighted + power * square
        total[:ROWS, :] = energy
        total[ROWS:, :] = weighted

    each_outer_tile(src, low, high, visit, (above, above + 1))
    if sums.shape == total.shape:
        sums[...] = total[...]
        return
    rows = [jnp.sum(total[pl.ds(part * ROWS, ROWS), :], axis=0, keepdims=True) for part in range(2)]
    sums[...] = jnp.broadcast_to(jnp.concatenate(rows, axis=0)[None], sums.shape)


def outer_kernel(source, limit, middle, sat, even_in, odd_in, *refs):
    heavy, plain, low, high, caps, limits = refs[-6:]
    times, lines, cells, depth = middle.shape
    unpack_marks(times, limit, sat, caps, limits, functools.partial(by_parity, even_in, odd_in))
    if source:
        late = functools.partial(by_parity, even_in, refs[0])
        unpack_halo(low, high, late, even_in, payload_layout(times, lines)[2])
    else:
        unpack_halo(low, high, functools.partial(by_parity, even_in, odd_in))

    def visit(y, at, center, offsets, far_at):
        rows = pl.ds(at, ROWS)
        sums = [heavy[t, y, rows, :] for t in range(times)], [plain[t, y, rows, :] for t in range(times)]
        new_heavy, new_plain = accumulate(
            center, sums, offsets, far_at, within(limits, at), lambda h: caps[y, pl.ds(at + H + h, ROWS), :]
        )
        for t in range(times):
            heavy[t, y, rows, :] = new_heavy[t]
            plain[t, y, rows, :] = new_plain[t]

    each_outer_tile(middle, low, high, visit)


def combine_kernel(cell_count, sums, src_heavy, src_plain, rcv_heavy, rcv_plain, src_far, rcv_far, semblance_out, near, sems):
    total = jnp.sum(sums[...], axis=0)
    total = jnp.broadcast_to(jnp.sum(total, axis=1, keepdims=True), total.shape)
    energy, weighted = total[0:1], total[1:2]
    semblance = weighted / energy
    inverse_rms = 1.0 / jnp.sqrt(energy / cell_count + EPSILON)
    semblance_out[...] = semblance
    copies = []
    for position, (heavy, plain, far) in enumerate(((src_heavy, src_plain, src_far), (rcv_heavy, rcv_plain, rcv_far))):
        times, lines, _, _ = heavy.shape
        for t in range(times):
            for y in range(lines):
                value = inverse_rms * (heavy[t, y] - semblance * plain[t, y])
                near[position, t, y] = value.astype(jnp.bfloat16)
            copies.append(pltpu.make_async_copy(near.at[position, t], far.at[t], sems.at[position, t]))
            copies[-1].start()
    for copy in copies:
        copy.wait()


def exchanges(size, lines):
    assert size % 2 == 0 and lines % 2 == 0
    even = [(i, i + 1) for i in range(0, size, 2)]
    odd = [(i, i + 1) for i in range(1, size - 1, 2)]
    routes = []
    for pairs in (even, odd):
        partner = dict(pairs + [(j, i) for i, j in pairs])
        routes.append(
            [
                (i * lines + line, partner[i] * lines + line if i in partner else i * lines + (line ^ 1))
                for i in range(size)
                for line in range(lines)
            ]
        )
    return routes


def local(source_field, receiver_field, sat_mask, offset_range):
    times, lines, cells, depth = source_field.shape
    size = lax.axis_size("inline")
    grant = pltpu.CompilerParams(vmem_limit_bytes=GRANT)
    image_cells = lines * cells * depth * (2 * H + 1)
    shape = jax.ShapeDtypeStruct
    total = shape((times, lines, cells, depth), jnp.float32)
    field_out = shape(source_field.shape, jnp.bfloat16)
    extended = pltpu.VMEM((times, lines, cells + 2 * REACH, depth), jnp.float32)
    edge = pltpu.VMEM((times, lines, ROWS + REACH, depth), jnp.float32)
    caps = pltpu.VMEM((lines, cells + 2 * H, depth), jnp.float32)
    limits = pltpu.VMEM((cells + 2 * H, depth), jnp.float32)

    def call(kernel, name, out_shape, operands, scratch=(), share=0.0, aliases={}):
        return pl.pallas_call(
            kernel,
            out_shape=out_shape,
            in_specs=[SMEM if operand is offset_range else VMEM for operand in operands],
            out_specs=jax.tree.map(lambda _: VMEM, out_shape),
            scratch_shapes=scratch,
            input_output_aliases=aliases,
            cost_estimate=pl.CostEstimate(
                flops=int(24 * image_cells * share), bytes_accessed=int(share * (1 << 20)), transcendentals=0
            ),
            compiler_params=grant,
            name=name,
        )(*operands)

    src, rcv, sat = source_field, receiver_field, sat_mask
    even, odd = payloads(src, rcv, sat, offset_range)
    even_route, odd_route = exchanges(size, lax.axis_size("xline"))
    even = lax.ppermute(even, DEVICES, even_route)
    odd = lax.ppermute(odd, DEVICES, odd_route)

    heavy, plain, inner = call(
        inner_kernel,
        "src_inner",
        (total, total, shape((2 * ROWS, depth), jnp.float32)),
        (offset_range, src, rcv, sat),
        [extended, caps],
        0.85,
    )
    inner, ahead = lax.optimization_barrier((inner, src))
    odd_late = lax.ppermute(for_odd(*edges(ahead, 2, REACH)), DEVICES, odd_route)
    by_row = shape((2 * ROWS, depth), jnp.float32)
    by_device = shape((size * lax.axis_size("xline"), 2, depth), jnp.float32)
    sums = inner
    for is_even, arrived, out_shape in ((False, odd, by_row), (True, even, by_device)):
        sums = call(
            functools.partial(energy_kernel, is_even),
            "energy",
            out_shape,
            (offset_range, src, sat, arrived, sums),
            [pltpu.VMEM(by_row.shape, jnp.float32), edge, edge, caps, limits],
            0.07,
        )
    gathered = lax.all_to_all(sums, DEVICES, 0, 0, tiled=True)

    sums, heavy, plain, ahead, odd_late = lax.optimization_barrier((sums, heavy, plain, src, odd_late))
    heavy, plain = call(
        functools.partial(outer_kernel, False),
        "src_outer",
        (total, total),
        (offset_range, ahead, sat, even, odd, heavy, plain),
        [edge, edge, caps, limits],
        0.25,
        {5: 0, 6: 1},
    )
    pieces = call(
        inner_kernel,
        "rcv_inner",
        (total, total),
        (offset_range, rcv, ahead, sat),
        [extended, caps],
        0.85,
    )
    pieces = call(
        functools.partial(outer_kernel, True),
        "rcv_outer",
        (total, total),
        (offset_range, rcv, sat, even, odd, odd_late, *pieces),
        [edge, edge, caps, limits],
        0.25,
        {6: 0, 7: 1},
    )

    cell_count = float(lines * lax.axis_size("xline") * cells * size * depth * (2 * H + 1))
    src_adj, rcv_adj, semblance = pl.pallas_call(
        functools.partial(combine_kernel, cell_count),
        out_shape=(field_out, field_out, shape((1, depth), jnp.float32)),
        in_specs=[VMEM] * 5,
        out_specs=(HBM, HBM, VMEM),
        scratch_shapes=[
            pltpu.VMEM((2, *source_field.shape), jnp.bfloat16),
            pltpu.SemaphoreType.DMA((2, times)),
        ],
        compiler_params=grant,
        name="combine",
    )(gathered, heavy, plain, *pieces)
    return src_adj, rcv_adj, semblance[0, 0]


def solution(mesh):
    return jax.shard_map(
        local,
        mesh=mesh,
        in_specs=(
            P(None, "xline", "inline", None),
            P(None, "xline", "inline", None),
            P("xline", "inline", None),
            P("inline"),
        ),
        out_specs=(P(None, "xline", "inline", None), P(None, "xline", "inline", None), P()),
        check_vma=False,
    )
```
